32 devices in a mesh: img: 16 (over z, y, core), lat: 2 (over x).
Axes of the slice: x: 2, y: 2, z: 4, core: 2. Of those that a mesh axis runs over, the one named last changes fastest.
Arguments:
- patches: bfloat16 [128, 256, 1024], P('img', 'lat'), may hold values from -6 to 6
- latents: bfloat16 [128, 64, 1024], P('img', 'lat'), may hold values from -6 to 6
- cotangent: bfloat16 [128, 64, 1024], P('img', 'lat'), may hold values from -6 to 6
- doc_images: int32 [64], replicated, may hold values from 0 to 8, as said below
- doc_device: int32 [64], replicated, may hold values from 0 to 15, as said below
- query_weight: bfloat16 [1024, 512], replicated, may hold values from -0.1875 to 0.1875
- key_weight: bfloat16 [1024, 512], replicated, may hold values from -0.1875 to 0.1875
- value_weight: bfloat16 [1024, 512], replicated, may hold values from -0.1875 to 0.1875
- output_weight: bfloat16 [512, 1024], replicated, may hold values from -1 to 1
- up_weight: bfloat16 [1024, 4096], replicated, may hold values from -0.1875 to 0.1875
- down_weight: bfloat16 [4096, 1024], replicated, may hold values from -0.09375 to 0.09375
- media_gain: float32 [1024], replicated, may hold values from 0.25 to 1.75
- media_bias: float32 [1024], replicated, may hold values from -2 to 2
- latent_gain: float32 [1024], replicated, may hold values from 0.25 to 1.75
- latent_bias: float32 [1024], replicated, may hold values from -2 to 2
- ffn_gain: float32 [1024], replicated, may hold values from 0.25 to 1.75
- ffn_bias: float32 [1024], replicated, may hold values from -2 to 2
Outputs:
- new_latents: bfloat16 [128, 64, 1024], P('img', 'lat')
- patches_grad: float32 [128, 256, 1024], P('img', 'lat')
- latents_grad: float32 [128, 64, 1024], P('img', 'lat')
- query_grad: float32 [1024, 512], P(('img', 'lat'))
- key_grad: float32 [1024, 512], P(('img', 'lat'))
- value_grad: float32 [1024, 512], P(('img', 'lat'))
- output_grad: float32 [512, 1024], P(('img', 'lat'))
- up_grad: float32 [1024, 4096], P(('img', 'lat'))
- down_grad: float32 [4096, 1024], P(('img', 'lat'))
- media_gain_grad: float32 [1024], P(('img', 'lat'))
- media_bias_grad: float32 [1024], P(('img', 'lat'))
- latent_gain_grad: float32 [1024], P(('img', 'lat'))
- latent_bias_grad: float32 [1024], P(('img', 'lat'))
- ffn_gain_grad: float32 [1024], P(('img', 'lat'))
- ffn_bias_grad: float32 [1024], P(('img', 'lat'))
The draws below stay inside these ranges and needn't reach their ends.
Inputs may be any that keep to these rules, and one draw needn't show every extreme that they name: `doc_images`: the documents that doc_device assigns to one index of img hold 8 images at most in all; on some index they hold exactly 8, all in one document. `doc_device`: each index of img is named by exactly 4 entries.
All inputs are finite; a program needn't handle non-finite values.
Results may differ from the reference program's by a relative error of at most 0.013.
Values may be sent and summed in bfloat16 or wider, within the bound.
A program may use at most 192 MiB of HBM per device.

```python
import jax
import jax.numpy as jnp
from jax import lax

D = 1024
HEADS = 8
HEAD_DIM = 64
FF = 4096
INNER = 512
PATCHES = 256
LATENTS = 64
CAP = 8
DOC_DEV = 4
SLOTS = 128
DOCS = 64


def shared_plan(key):
    owners = DOCS // DOC_DEV
    load_key, busy_key, cut_key, order_key = jax.random.split(key, 4)
    place = jnp.arange(owners, dtype=jnp.int32)
    loads = jax.random.randint(load_key, (owners,), 1, CAP + 1)
    busy = jax.random.randint(busy_key, (), 0, owners)
    loads = jnp.where(place == busy, CAP, loads)
    cuts = jax.random.randint(cut_key, (owners, DOC_DEV - 1), 0, CAP + 1) % (loads[:, None] + 1)
    cuts = jnp.where((place == busy)[:, None], 0, cuts)
    cuts = jnp.sort(cuts, axis=1)
    edges = jnp.concatenate([jnp.zeros((owners, 1), jnp.int32), cuts, loads[:, None]], axis=1)
    pieces = (edges[:, 1:] - edges[:, :-1]).reshape(-1)
    order = jax.random.permutation(order_key, DOCS)
    holders = jnp.repeat(place, DOC_DEV)
    return (pieces[order].astype(jnp.int32), holders[order].astype(jnp.int32))


def draw_doc_images(key, part):
    plan = shared_plan(key)
    return plan[0]


def draw_doc_device(key, part):
    plan = shared_plan(key)
    return plan[1]


def level_of(key, dims, cuts, least, largest):
    level, own = 1.0, jax.random.fold_in(key, 6)
    for dim, shards_of in cuts:
        heights = jnp.exp(jax.random.uniform(jax.random.fold_in(own, dim), (shards_of,), jnp.float32, least / len(cuts), largest / len(cuts)))
        level = level * jnp.repeat(heights, dims[dim] // shards_of).reshape([-1 if axis == dim else 1 for axis in range(len(dims))])
    return level


def normal_values(own_key, shape, deviation, limit, cuts=(), kind=jnp.bfloat16):
    drawn = deviation * jax.random.normal(own_key, shape, jnp.float32)
    if cuts:
        drawn = drawn * level_of(own_key, shape, cuts, -0.22, 0.18)
    return jnp.clip(drawn, -limit, limit).astype(kind)


def setup_inputs(seed: int = 0) -> dict:
    key_of = jax.random.split(jax.random.key(seed), 18)
    patches = normal_values(key_of[0], (SLOTS, PATCHES, D), 1.0, 6.0, ((0, 16), (1, 2)))
    latents = normal_values(key_of[1], (SLOTS, LATENTS, D), 1.0, 6.0, ((0, 16), (1, 2)))
    cotangent = normal_values(key_of[2], (SLOTS, LATENTS, D), 1.0, 6.0, ((0, 16), (1, 2)))
    doc_images = draw_doc_images(jax.random.fold_in(key_of[17], 71), 0)
    doc_device = draw_doc_device(jax.random.fold_in(key_of[17], 71), 0)
    query_weight = normal_values(key_of[5], (D, INNER), D ** -0.5, 0.1875)
    key_weight = normal_values(key_of[6], (D, INNER), D ** -0.5, 0.1875)
    value_weight = normal_values(key_of[7], (D, INNER), D ** -0.5, 0.1875)
    output_weight = normal_values(key_of[8], (INNER, D), (INNER // 16) ** -0.5, 1.0)
    up_weight = normal_values(key_of[9], (D, FF), D ** -0.5, 0.1875)
    down_weight = normal_values(key_of[10], (FF, D), FF ** -0.5, 0.09375)
    media_gain = jnp.clip(1.0 + 0.15 * jax.random.normal(key_of[11], (D,), jnp.float32), 0.25, 1.75)
    media_bias = normal_values(key_of[12], (D,), 0.3, 2.0, (), jnp.float32)
    latent_gain = jnp.clip(1.0 + 0.15 * jax.random.normal(key_of[13], (D,), jnp.float32), 0.25, 1.75)
    latent_bias = normal_values(key_of[14], (D,), 0.3, 2.0, (), jnp.float32)
    ffn_gain = jnp.clip(1.0 + 0.15 * jax.random.normal(key_of[15], (D,), jnp.float32), 0.25, 1.75)
    ffn_bias = normal_values(key_of[16], (D,), 0.3, 2.0, (), jnp.float32)
    return {"patches": patches, "latents": latents, "cotangent": cotangent, "doc_images": doc_images, "doc_device": doc_device, "query_weight": query_weight, "key_weight": key_weight, "value_weight": value_weight, "output_weight": output_weight, "up_weight": up_weight, "down_weight": down_weight, "media_gain": media_gain, "media_bias": media_bias, "latent_gain": latent_gain, "latent_bias": latent_bias, "ffn_gain": ffn_gain, "ffn_bias": ffn_bias}


@jax.custom_vjp
def low(v):
    return lax.optimization_barrier(v.astype(jnp.bfloat16)).astype(jnp.float32)

@jax.custom_vjp
def low_back(v):
    return v

def low_keep(v):
    return (low(v), None)

def low_pass(kept, grad):
    return (grad,)

def back_keep(v):
    return (v, None)

def back_low(kept, grad):
    return (low(grad),)
low.defvjp(low_keep, low_pass)
low_back.defvjp(back_keep, back_low)
highest = lax.Precision.HIGHEST
epsilon = 1e-05

def layer_norm(values, gain, bias):
    centre = values - lax.optimization_barrier(jnp.mean(values, axis=-1, keepdims=True))
    variance = lax.optimization_barrier(jnp.mean(centre * centre, axis=-1, keepdims=True))
    return centre * lax.rsqrt(variance + epsilon) * gain + bias

def image_group(params, group):
    query_weight, key_weight, value_weight, output_weight, up_weight, down_weight, media_gain, media_bias, latent_gain, latent_bias, ffn_gain, ffn_bias = params
    media, latent, active = group
    media_norm = low(layer_norm(media, media_gain, media_bias))
    latent_norm = low(layer_norm(latent, latent_gain, latent_bias))
    key_rows = jnp.concatenate([media_norm, latent_norm], axis=1)
    queries = low(low_back(HEAD_DIM ** (-0.5) * jnp.einsum('cld,de->cle', latent_norm, query_weight, precision=highest)))
    keys = low(low_back(jnp.einsum('crd,de->cre', key_rows, key_weight, precision=highest)))
    values = low(low_back(jnp.einsum('crd,de->cre', key_rows, value_weight, precision=highest)))
    query_heads = queries.reshape(CAP, LATENTS, HEADS, HEAD_DIM)
    key_heads = keys.reshape(CAP, PATCHES + LATENTS, HEADS, HEAD_DIM)
    value_heads = values.reshape(CAP, PATCHES + LATENTS, HEADS, HEAD_DIM)
    scores = low_back(jnp.einsum('cqhd,ckhd->chqk', query_heads, key_heads, precision=highest))
    top = lax.optimization_barrier(jnp.max(scores, axis=-1, keepdims=True))
    expo = jnp.exp(scores - top)
    probs = low(expo / lax.optimization_barrier(jnp.sum(expo, axis=-1, keepdims=True)))
    attended = jnp.einsum('chqk,ckhd->cqhd', probs, value_heads, precision=highest).reshape(CAP, LATENTS, HEADS * HEAD_DIM)
    attended = low(low_back(attended))
    branch = low_back(jnp.einsum('cle,ed->cld', attended, output_weight, precision=highest))
    residual = latent + branch
    ffn_in = low(layer_norm(residual, ffn_gain, ffn_bias))
    pre_act = low_back(jnp.einsum('cld,df->clf', ffn_in, up_weight, precision=highest))
    act = low(jax.nn.gelu(pre_act, approximate=False))
    ffn_out = low_back(jnp.einsum('clf,fd->cld', act, down_weight, precision=highest))
    return (residual + ffn_out) * active[:, None, None]

def reference(patches, latents, cotangent, doc_images, doc_device, query_weight, key_weight, value_weight, output_weight, up_weight, down_weight, media_gain, media_bias, latent_gain, latent_bias, ffn_gain, ffn_bias):
    groups = SLOTS // CAP
    holding = jnp.zeros((groups,), jnp.int32).at[doc_device].add(doc_images)
    active = (jnp.arange(CAP, dtype=jnp.int32)[None, :] < holding[:, None]).astype(jnp.float32)
    params = (query_weight.astype(jnp.float32), key_weight.astype(jnp.float32), value_weight.astype(jnp.float32), output_weight.astype(jnp.float32), up_weight.astype(jnp.float32), down_weight.astype(jnp.float32), media_gain.astype(jnp.float32), media_bias.astype(jnp.float32), latent_gain.astype(jnp.float32), latent_bias.astype(jnp.float32), ffn_gain.astype(jnp.float32), ffn_bias.astype(jnp.float32))
    media = patches.astype(jnp.float32).reshape(groups, CAP, PATCHES, D)
    latent = latents.astype(jnp.float32).reshape(groups, CAP, LATENTS, D)
    checked = jax.checkpoint(image_group)

    def forward(weights, media_all, latent_all):
        return lax.map(lambda group: checked(weights, group), (media_all, latent_all, active))
    output, pull = jax.vjp(forward, params, media, latent)
    param_grads, media_grad, latent_grad = pull(cotangent.astype(jnp.float32).reshape(groups, CAP, LATENTS, D))
    return (output.reshape(SLOTS, LATENTS, D).astype(jnp.bfloat16), media_grad.reshape(SLOTS, PATCHES, D), latent_grad.reshape(SLOTS, LATENTS, D), param_grads[0], param_grads[1], param_grads[2], param_grads[3], param_grads[4], param_grads[5], param_grads[6], param_grads[7], param_grads[8], param_grads[9], param_grads[10], param_grads[11])
```

```python
from functools import partial

import jax
import jax.numpy as jnp
from jax import lax
from jax.experimental import pallas as pl
from jax.experimental.pallas import tpu as pltpu
from jax.sharding import PartitionSpec as P

HEADS = 8
HEAD_DIM = 64
INNER = HEADS * HEAD_DIM
LANES = 128
PER = LANES // HEADS
EPS = 1e-05
BF = jnp.bfloat16
F32 = jnp.float32
VMEM_LIMIT = 56 * 1024 * 1024


def dot(a, b):
    return lax.dot_general(a, b, (((1,), (0,)), ((), ())), preferred_element_type=F32)


def dot_t(a, b):
    return lax.dot_general(a, b, (((1,), (1,)), ((), ())), preferred_element_type=F32)


def t_dot(a, b):
    return lax.dot_general(a, b, (((0,), (0,)), ((), ())), preferred_element_type=F32)


def call(body, grid, ins, outs, args, flops, scratch=()):
    moved = sum(a.size * a.dtype.itemsize for a in args)
    moved += sum(o[0].size * o[0].dtype.itemsize for o in outs)
    return pl.pallas_call(
        body,
        grid=grid,
        in_specs=ins,
        out_specs=[o[1] for o in outs],
        out_shape=[o[0] for o in outs],
        scratch_shapes=list(scratch),
        compiler_params=pltpu.CompilerParams(
            dimension_semantics=("arbitrary",) * len(grid), vmem_limit_bytes=VMEM_LIMIT
        ),
        cost_estimate=pl.CostEstimate(flops=flops, bytes_accessed=moved, transcendentals=0),
    )(*args)


def whole(shape):
    return pl.BlockSpec(shape, lambda *_: (0,) * len(shape))


def rows(block, width):
    return pl.BlockSpec((block, width), lambda i: (i, 0))


def cols(height, block):
    return pl.BlockSpec((height, block), lambda i: (0, i))


def struct(shape, dtype):
    return jax.ShapeDtypeStruct(shape, dtype)


def centred(v):
    centre = v - jnp.mean(v, axis=-1, keepdims=True)
    scale = lax.rsqrt(jnp.mean(centre * centre, axis=-1, keepdims=True) + EPS)
    return centre * scale, scale


def norm_back(unit, scale, gain, grad):
    push = grad * gain
    mean_push = jnp.mean(push, axis=-1, keepdims=True)
    mean_both = jnp.mean(push * unit, axis=-1, keepdims=True)
    return scale * (push - mean_push - unit * mean_both)


def column_sum(v):
    return jnp.sum(v, axis=0, keepdims=True)


def latent_body(latent, gain, bias, wq, norm, query):
    unit, _ = centred(latent[...].astype(F32))
    low = (unit * gain[...] + bias[...]).astype(BF)
    norm[...] = low
    query[...] = (HEAD_DIM**-0.5 * dot(low, wq[...])).astype(BF)


def media_body(patch, gain, bias, wk, wv, latent_norm, norm, kp, vp, kl, vl):
    @pl.when(pl.program_id(0) == 0)
    def _():
        kl[...] = dot(latent_norm[...], wk[...]).astype(BF)
        vl[...] = dot(latent_norm[...], wv[...]).astype(BF)

    unit, _ = centred(patch[...].astype(F32))
    low = (unit * gain[...] + bias[...]).astype(BF)
    norm[...] = low
    kp[...] = dot(low, wk[...]).astype(BF)
    vp[...] = dot(low, wv[...]).astype(BF)


def head_of(shape):
    return lax.broadcasted_iota(jnp.int32, shape, 1) // HEAD_DIM


def spread_rows(v):
    head = head_of(v.shape)
    zero = jnp.zeros_like(v)
    return jnp.concatenate([jnp.where(head == h, v, zero) for h in range(HEADS)], axis=0)


def gather_rows(v):
    count = v.shape[0] // HEADS
    head = head_of((count, v.shape[1]))
    total = jnp.zeros((count, v.shape[1]), F32)
    for h in range(HEADS):
        total = jnp.where(head == h, v[h * count : (h + 1) * count], total)
    return total


def pack_lanes(columns):
    count = columns[0].shape[0]
    lane = lax.broadcasted_iota(jnp.int32, (count, LANES), 1)
    step = LANES // len(columns)
    total = jnp.zeros((count, LANES), F32)
    for h, column in enumerate(columns):
        total = jnp.where(lane // step == h, column, total)
    return total


def widen(packed):
    head = head_of((packed.shape[0], INNER))
    total = jnp.zeros((packed.shape[0], INNER), F32)
    for h in range(HEADS):
        total = jnp.where(head == h, packed[:, h * PER : h * PER + 1], total)
    return total


def stack_heads(packed, offset):
    return jnp.concatenate(
        [packed[:, h * PER + offset : h * PER + offset + 1] for h in range(HEADS)], axis=0
    )


def attend_body(qo, qp, kp, vp, kl, vl, oo, op, so, sp):
    own = qo.shape[0]
    big = spread_rows(jnp.concatenate([qo[...], qp[...]], axis=0))
    keys = jnp.concatenate([kp[...], kl[...]], axis=0)
    values = jnp.concatenate([vp[...], vl[...]], axis=0)
    scores = dot_t(big, keys)
    top = jnp.max(scores, axis=-1, keepdims=True)
    expo = jnp.exp(scores - top)
    total = jnp.sum(expo, axis=-1, keepdims=True)
    probs = (expo / total).astype(BF)
    out = gather_rows(dot(probs, values))
    log_total = top + jnp.log(total)
    count = log_total.shape[0] // HEADS
    packed = pack_lanes([log_total[h * count : (h + 1) * count] for h in range(HEADS)])
    oo[...] = out[:own]
    op[...] = out[own:].astype(BF)
    so[...] = packed[:own]
    sp[...] = packed[own:]


def forward_body(
    slot_rows,
    holding,
    oo,
    orecv,
    so,
    srecv,
    latent,
    cot,
    wo,
    wup,
    wdown,
    gain,
    bias,
    new_latents,
    act_out,
    pre_out,
    ffn_t,
    og_out,
    residual_grad,
    attended_grad,
    stats,
    output_grad,
    vectors,
    residual,
    ffn_in,
    acc,
    gacc,
    attended,
    packed,
):
    step = pl.program_id(0)
    count = latent.shape[0]
    slot = lax.broadcasted_iota(jnp.int32, (count, 1), 0) // slot_rows
    live = jnp.where(slot < holding[0, 0], 1.0, 0.0).astype(F32)

    @pl.when(step == 0)
    def _():
        a, b = so[...], srecv[...]
        top = jnp.maximum(a, b)
        both = top + jnp.log(jnp.exp(a - top) + jnp.exp(b - top))
        packed[...] = both
        mix = widen(jnp.exp(a - both)) * oo[...]
        mix += widen(jnp.exp(b - both)) * orecv[...].astype(F32)
        attended[...] = mix
        res = latent[...].astype(F32) + dot(mix.astype(BF), wo[...])
        residual[...] = res
        unit, _ = centred(res)
        low = (unit * gain[...] + bias[...]).astype(BF)
        ffn_in[...] = low
        ffn_t[...] = low.T
        og_out[...] = (cot[...].astype(F32) * live).astype(BF)
        acc[...] = jnp.zeros_like(acc)
        gacc[...] = jnp.zeros_like(gacc)

    pre = dot(ffn_in[...], wup[...])
    cdf = 0.5 * (1.0 + lax.erf(pre * (0.5**0.5)))
    act = (pre * cdf).astype(BF)
    act_out[...] = act
    acc[...] += dot(act, wdown[...])
    act_grad = dot_t(og_out[...], wdown[...])
    pdf = jnp.exp(-0.5 * pre * pre) * 0.3989422804014327
    pre_grad = (act_grad * (cdf + pre * pdf)).astype(BF)
    pre_out[...] = pre_grad
    gacc[...] += dot_t(pre_grad, wup[...])

    @pl.when(step == pl.num_programs(0) - 1)
    def _():
        res = residual[...]
        new_latents[...] = ((res + acc[...]) * live).astype(BF)
        unit, scale = centred(res)
        grad = gacc[...]
        vectors[0:1, :] = column_sum(grad * unit)
        vectors[1:2, :] = column_sum(grad)
        res_grad = og_out[...].astype(F32) + norm_back(unit, scale, gain[...], grad)
        residual_grad[...] = res_grad
        branch = res_grad.astype(BF)
        back = dot_t(branch, wo[...]).astype(BF)
        attended_grad[...] = back
        mix = attended[...]
        product = back.astype(F32) * mix
        head = head_of(product.shape)
        sums = [
            jnp.sum(jnp.where(head == h, product, 0.0), axis=-1, keepdims=True)
            for h in range(HEADS)
        ]
        delta = pack_lanes(sums)
        lane = lax.broadcasted_iota(jnp.int32, delta.shape, 1)
        stats[...] = jnp.where(lane % PER < PER // 2, packed[...], delta)
        output_grad[...] = t_dot(mix.astype(BF), branch).astype(BF)


def attend_back_body(qo, qp, kp, vp, kl, vl, do, dp, so, sp, dkvp, dkvl, dqo, dqp):
    own = qo.shape[0]
    patches = kp.shape[0]
    big = spread_rows(jnp.concatenate([qo[...], qp[...]], axis=0))
    back = spread_rows(jnp.concatenate([do[...], dp[...]], axis=0))
    keys = jnp.concatenate([kp[...], kl[...]], axis=0)
    values = jnp.concatenate([vp[...], vl[...]], axis=0)
    stats = jnp.concatenate([so[...], sp[...]], axis=0)
    probs = jnp.exp(dot_t(big, keys) - stack_heads(stats, 0))
    score_grad = (probs * (dot_t(back, values) - stack_heads(stats, PER // 2))).astype(BF)
    values_grad = t_dot(probs.astype(BF), back).astype(BF)
    keys_grad = t_dot(score_grad, big).astype(BF)
    dkvp[:, :INNER] = keys_grad[:patches]
    dkvp[:, INNER:] = values_grad[:patches]
    dkvl[:, :INNER] = keys_grad[patches:]
    dkvl[:, INNER:] = values_grad[patches:]
    dq = gather_rows(dot(score_grad, keys))
    dqo[...] = dq[:own]
    dqp[...] = dq[own:].astype(BF)


def up_grad_body(left, right, out):
    out[...] = dot(left[...], right[...]).astype(BF)


def down_grad_body(left, right, out):
    out[...] = t_dot(left[...], right[...]).astype(BF)


def kv_grad_body(media, latent, dkvp, dkvl, out):
    out[...] = (t_dot(media[...], dkvp[...]) + t_dot(latent[...], dkvl[...])).astype(BF)


def patch_back_body(patch, dkvp, wk, wv, gain, out, vectors):
    @pl.when(pl.program_id(0) == 0)
    def _():
        vectors[...] = jnp.zeros_like(vectors)

    grad = dot_t(dkvp[:, :INNER], wk[...]) + dot_t(dkvp[:, INNER:], wv[...])
    unit, scale = centred(patch[...].astype(F32))
    vectors[0:1, :] += column_sum(grad * unit)
    vectors[1:2, :] += column_sum(grad)
    out[...] = norm_back(unit, scale, gain[...], grad)


def latent_back_body(
    latent, norm, dkvl, dqo, drecv, residual_grad, wq, wk, wv, gain, out, query_grad, vectors
):
    dq = (dqo[...] + drecv[...].astype(F32)).astype(BF)
    query_grad[...] = (HEAD_DIM**-0.5 * t_dot(norm[...], dq)).astype(BF)
    grad = dot_t(dkvl[:, :INNER], wk[...]) + dot_t(dkvl[:, INNER:], wv[...])
    grad += HEAD_DIM**-0.5 * dot_t(dq, wq[...])
    unit, scale = centred(latent[...].astype(F32))
    vectors[0:1, :] = column_sum(grad * unit)
    vectors[1:2, :] = column_sum(grad)
    out[...] = residual_grad[...] + norm_back(unit, scale, gain[...], grad)


def swap_lat(v):
    return lax.ppermute(v, "lat", [(0, 1), (1, 0)])


def halving_sum(v, order, bits, count, keep):
    left = list(range(bits - 1, -1, -1)) + [-1]
    mine = lax.axis_index("img")
    for place, axis in enumerate(order):
        dim = left.index(axis)
        if axis < 0:
            bit = lax.axis_index("lat")
            pairs, name = [(0, 1), (1, 0)], "lat"
        else:
            bit = (mine // 2**axis) % 2
            pairs, name = [(i, i ^ 2**axis) for i in range(count)], "img"
        out = lax.dynamic_index_in_dim(v, 1 - bit, dim, keepdims=False)
        stay = lax.dynamic_index_in_dim(v, bit, dim, keepdims=False)
        got = lax.ppermute(out, name, pairs)
        v = stay.astype(F32) + got.astype(F32)
        if place < len(order) - 1 and keep == BF:
            v = v.astype(BF)
        left.pop(dim)
    return v


def local(
    count,
    patches,
    latents,
    cotangent,
    doc_images,
    doc_device,
    query_weight,
    key_weight,
    value_weight,
    output_weight,
    up_weight,
    down_weight,
    media_gain,
    media_bias,
    latent_gain,
    latent_bias,
    ffn_gain,
    ffn_bias,
):
    slots, own_patches, width = patches.shape
    own_latents = latents.shape[1]
    hidden = up_weight.shape[1]
    np_, nl = slots * own_patches, slots * own_latents
    mine = lax.axis_index("img")
    holding = jnp.sum(jnp.where(doc_device == mine, doc_images, 0)).reshape(1, 1)
    patch = patches.reshape(np_, width)
    latent = latents.reshape(nl, width)
    cot = cotangent.reshape(nl, width)
    mg, mb = media_gain.reshape(1, width), media_bias.reshape(1, width)
    lg, lb = latent_gain.reshape(1, width), latent_bias.reshape(1, width)
    fg, fb = ffn_gain.reshape(1, width), ffn_bias.reshape(1, width)
    wspec = whole((width, INNER))
    vspec = whole((1, width))
    lspec = whole((nl, width))

    norm_l, query = call(
        latent_body,
        (1,),
        [lspec, vspec, vspec, wspec],
        [(struct((nl, width), BF), lspec), (struct((nl, INNER), BF), whole((nl, INNER)))],
        (latent, lg, lb, query_weight),
        2 * nl * width * INNER,
    )
    query_peer = swap_lat(query)
    blk = min(np_, 256)
    norm_m, kp, vp, kl, vl = call(
        media_body,
        (np_ // blk,),
        [rows(blk, width), vspec, vspec, wspec, wspec, lspec],
        [
            (struct((np_, width), BF), rows(blk, width)),
            (struct((np_, INNER), BF), rows(blk, INNER)),
            (struct((np_, INNER), BF), rows(blk, INNER)),
            (struct((nl, INNER), BF), whole((nl, INNER))),
            (struct((nl, INNER), BF), whole((nl, INNER))),
        ],
        (patch, mg, mb, key_weight, value_weight, norm_l),
        4 * (np_ + nl) * width * INNER,
    )
    q_s, p_s, s_s = rows(own_latents, INNER), rows(own_patches, INNER), rows(own_latents, LANES)
    att_flops = 4 * slots * (own_patches + own_latents) * INNER * INNER
    o_own, o_peer, s_own, s_peer = call(
        attend_body,
        (slots,),
        [q_s, q_s, p_s, p_s, q_s, q_s],
        [
            (struct((nl, INNER), F32), q_s),
            (struct((nl, INNER), BF), q_s),
            (struct((nl, LANES), F32), s_s),
            (struct((nl, LANES), F32), s_s),
        ],
        (query, query_peer, kp, vp, kl, vl),
        att_flops,
    )
    o_recv, s_recv = swap_lat(o_peer), swap_lat(s_peer)
    fblk = min(hidden, 512)
    nspec = whole((nl, INNER))
    (
        new_latents,
        act,
        pre_grad,
        ffn_t,
        out_grad,
        residual_grad,
        attended_grad,
        stats,
        output_grad,
        ffn_vec,
    ) = call(
        partial(forward_body, own_latents),
        (hidden // fblk,),
        [
            pl.BlockSpec(memory_space=pltpu.SMEM),
            nspec,
            nspec,
            whole((nl, LANES)),
            whole((nl, LANES)),
            lspec,
            lspec,
            whole((INNER, width)),
            cols(width, fblk),
            rows(fblk, width),
            vspec,
            vspec,
        ],
        [
            (struct((nl, width), BF), lspec),
            (struct((nl, hidden), BF), cols(nl, fblk)),
            (struct((nl, hidden), BF), cols(nl, fblk)),
            (struct((width, nl), BF), whole((width, nl))),
            (struct((nl, width), BF), lspec),
            (struct((nl, width), F32), lspec),
            (struct((nl, INNER), BF), nspec),
            (struct((nl, LANES), F32), whole((nl, LANES))),
            (struct((INNER, width), BF), whole((INNER, width))),
            (struct((2, width), F32), whole((2, width))),
        ],
        (
            holding,
            o_own,
            o_recv,
            s_own,
            s_recv,
            latent,
            cot,
            output_weight,
            up_weight,
            down_weight,
            fg,
            fb,
        ),
        8 * nl * width * hidden,
        scratch=[
            pltpu.VMEM((nl, width), F32),
            pltpu.VMEM((nl, width), BF),
            pltpu.VMEM((nl, width), F32),
            pltpu.VMEM((nl, width), F32),
            pltpu.VMEM((nl, INNER), F32),
            pltpu.VMEM((nl, LANES), F32),
        ],
    )
    grad_peer, stats_peer = swap_lat(attended_grad), swap_lat(stats)
    (down_grad,) = call(
        down_grad_body,
        (hidden // fblk,),
        [cols(nl, fblk), lspec],
        [(struct((hidden, width), BF), rows(fblk, width))],
        (act, out_grad),
        2 * nl * width * hidden,
    )
    (up_grad,) = call(
        up_grad_body,
        (hidden // fblk,),
        [whole((width, nl)), cols(nl, fblk)],
        [(struct((width, hidden), BF), cols(width, fblk))],
        (ffn_t, pre_grad),
        2 * nl * width * hidden,
    )
    dkvp, dkvl, dq_own, dq_peer = call(
        attend_back_body,
        (slots,),
        [q_s, q_s, p_s, p_s, q_s, q_s, q_s, q_s, s_s, s_s],
        [
            (struct((np_, 2 * INNER), BF), rows(own_patches, 2 * INNER)),
            (struct((nl, 2 * INNER), BF), rows(own_latents, 2 * INNER)),
            (struct((nl, INNER), F32), q_s),
            (struct((nl, INNER), BF), q_s),
        ],
        (query, query_peer, kp, vp, kl, vl, attended_grad, grad_peer, stats, stats_peer),
        att_flops * 5 // 2,
    )
    dq_recv = swap_lat(dq_peer)
    kblk = 256
    (kv_grad,) = call(
        kv_grad_body,
        (2 * INNER // kblk,),
        [whole((np_, width)), lspec, cols(np_, kblk), cols(nl, kblk)],
        [(struct((width, 2 * INNER), BF), cols(width, kblk))],
        (norm_m, norm_l, dkvp, dkvl),
        4 * (np_ + nl) * width * INNER,
    )
    patches_grad, media_vec = call(
        patch_back_body,
        (np_ // blk,),
        [rows(blk, width), rows(blk, 2 * INNER), wspec, wspec, vspec],
        [(struct((np_, width), F32), rows(blk, width)), (struct((2, width), F32), whole((2, width)))],
        (patch, dkvp, key_weight, value_weight, mg),
        4 * np_ * width * INNER,
    )
    latents_grad, query_grad, latent_vec = call(
        latent_back_body,
        (1,),
        [
            lspec,
            lspec,
            whole((nl, 2 * INNER)),
            nspec,
            nspec,
            lspec,
            wspec,
            wspec,
            wspec,
            vspec,
        ],
        [
            (struct((nl, width), F32), lspec),
            (struct((width, INNER), BF), wspec),
            (struct((2, width), F32), whole((2, width))),
        ],
        (
            latent,
            norm_l,
            dkvl,
            dq_own,
            dq_recv,
            residual_grad,
            query_weight,
            key_weight,
            value_weight,
            lg,
        ),
        8 * nl * width * INNER,
    )

    bits = count.bit_length() - 1
    first = list(range(1, bits))
    orders = (
        [0, -1] + first,
        [0] + first + [-1],
        [0] + first[1:] + [-1] + first[:1],
    )

    def reduce(v, order, keep=BF):
        shape = (2,) * (bits + 1) + (v.shape[0] // (2 * count),) + v.shape[1:]
        return halving_sum(v.reshape(shape), order, bits, count, keep)

    def reduce_parts(v):
        unit = v.shape[1] // 8
        cuts = (0, 3 * unit, 6 * unit, 8 * unit)
        return jnp.concatenate(
            [reduce(v[:, a:b], order) for a, b, order in zip(cuts, cuts[1:], orders)], axis=1
        )

    down_sum = reduce_parts(down_grad)
    up_sum = reduce_parts(up_grad)
    output_sum = reduce(output_grad, orders[1])
    kv_sum = reduce_parts(kv_grad)
    query_sum = reduce(query_grad, orders[0])
    vec = jnp.concatenate([media_vec, latent_vec, ffn_vec], axis=0)
    vec = vec.reshape(6, 2 * count, width // (2 * count)).transpose(1, 0, 2)
    vec_sum = reduce(vec, orders[2], F32)[0]
    return (
        new_latents.reshape(latents.shape),
        patches_grad.reshape(patches.shape),
        latents_grad.reshape(latents.shape),
        query_sum,
        kv_sum[:, :INNER],
        kv_sum[:, INNER:],
        output_sum,
        up_sum,
        down_sum,
        vec_sum[0],
        vec_sum[1],
        vec_sum[2],
        vec_sum[3],
        vec_sum[4],
        vec_sum[5],
    )


def solution(mesh):
    split = P("img", "lat", None)
    both = P(("img", "lat"), None)
    line = P(("img", "lat"))
    return jax.shard_map(
        partial(local, mesh.shape["img"]),
        mesh=mesh,
        in_specs=(split,) * 3 + (P(),) * 14,
        out_specs=(split,) * 3 + (both,) * 6 + (line,) * 6,
        check_vma=False,
    )
```

```python
from functools import partial

import jax
import jax.numpy as jnp
from jax import lax
from jax.experimental import pallas as pl
from jax.experimental.pallas import tpu as pltpu
from jax.sharding import PartitionSpec as P

HEADS = 8
HEAD_DIM = 64
INNER = HEADS * HEAD_DIM
LANES = 128
PER = LANES // HEADS
EPS = 1e-05
BF = jnp.bfloat16
F32 = jnp.float32
VMEM_LIMIT = 56 * 1024 * 1024


def dot(a, b):
    return lax.dot_general(a, b, (((1,), (0,)), ((), ())), preferred_element_type=F32)


def dot_t(a, b):
    return lax.dot_general(a, b, (((1,), (1,)), ((), ())), preferred_element_type=F32)


def t_dot(a, b):
    return lax.dot_general(a, b, (((0,), (0,)), ((), ())), preferred_element_type=F32)


def call(body, grid, ins, outs, args, flops, scratch=()):
    moved = sum(a.size * a.dtype.itemsize for a in args)
    moved += sum(o[0].size * o[0].dtype.itemsize for o in outs)
    return pl.pallas_call(
        body,
        grid=grid,
        in_specs=ins,
        out_specs=[o[1] for o in outs],
        out_shape=[o[0] for o in outs],
        scratch_shapes=list(scratch),
        compiler_params=pltpu.CompilerParams(
            dimension_semantics=("arbitrary",) * len(grid), vmem_limit_bytes=VMEM_LIMIT
        ),
        cost_estimate=pl.CostEstimate(flops=flops, bytes_accessed=moved, transcendentals=0),
    )(*args)


def whole(shape):
    return pl.BlockSpec(shape, lambda *_: (0,) * len(shape))


def rows(block, width):
    return pl.BlockSpec((block, width), lambda i: (i, 0))


def cols(height, block):
    return pl.BlockSpec((height, block), lambda i: (0, i))


def struct(shape, dtype):
    return jax.ShapeDtypeStruct(shape, dtype)


def centred(v):
    centre = v - jnp.mean(v, axis=-1, keepdims=True)
    scale = lax.rsqrt(jnp.mean(centre * centre, axis=-1, keepdims=True) + EPS)
    return centre * scale, scale


def norm_back(unit, scale, gain, grad):
    push = grad * gain
    mean_push = jnp.mean(push, axis=-1, keepdims=True)
    mean_both = jnp.mean(push * unit, axis=-1, keepdims=True)
    return scale * (push - mean_push - unit * mean_both)


def column_sum(v):
    return jnp.sum(v, axis=0, keepdims=True)


def latent_body(latent, gain, bias, wq, norm, query):
    unit, _ = centred(latent[...].astype(F32))
    low = (unit * gain[...] + bias[...]).astype(BF)
    norm[...] = low
    query[...] = (HEAD_DIM**-0.5 * dot(low, wq[...])).astype(BF)


def media_body(patch, gain, bias, wk, wv, latent_norm, norm, kp, vp, kl, vl):
    @pl.when(pl.program_id(0) == 0)
    def _():
        kl[...] = dot(latent_norm[...], wk[...]).astype(BF)
        vl[...] = dot(latent_norm[...], wv[...]).astype(BF)

    unit, _ = centred(patch[...].astype(F32))
    low = (unit * gain[...] + bias[...]).astype(BF)
    norm[...] = low
    kp[...] = dot(low, wk[...]).astype(BF)
    vp[...] = dot(low, wv[...]).astype(BF)


def head_of(shape):
    return lax.broadcasted_iota(jnp.int32, shape, 1) // HEAD_DIM


def spread_rows(v):
    head = head_of(v.shape)
    zero = jnp.zeros_like(v)
    return jnp.concatenate([jnp.where(head == h, v, zero) for h in range(HEADS)], axis=0)


def gather_rows(v):
    count = v.shape[0] // HEADS
    head = head_of((count, v.shape[1]))
    total = jnp.zeros((count, v.shape[1]), F32)
    for h in range(HEADS):
        total = jnp.where(head == h, v[h * count : (h + 1) * count], total)
    return total


def pack_lanes(columns):
    count = columns[0].shape[0]
    lane = lax.broadcasted_iota(jnp.int32, (count, LANES), 1)
    step = LANES // len(columns)
    total = jnp.zeros((count, LANES), F32)
    for h, column in enumerate(columns):
        total = jnp.where(lane // step == h, column, total)
    return total


def widen(packed):
    head = head_of((packed.shape[0], INNER))
    total = jnp.zeros((packed.shape[0], INNER), F32)
    for h in range(HEADS):
        total = jnp.where(head == h, packed[:, h * PER : h * PER + 1], total)
    return total


def stack_heads(packed, offset):
    return jnp.concatenate(
        [packed[:, h * PER + offset : h * PER + offset + 1] for h in range(HEADS)], axis=0
    )


def attend_body(qo, qp, kp, vp, kl, vl, oo, op, so, sp):
    own = qo.shape[0]
    big = spread_rows(jnp.concatenate([qo[...], qp[...]], axis=0))
    keys = jnp.concatenate([kp[...], kl[...]], axis=0)
    values = jnp.concatenate([vp[...], vl[...]], axis=0)
    scores = dot_t(big, keys)
    top = jnp.max(scores, axis=-1, keepdims=True)
    expo = jnp.exp(scores - top)
    total = jnp.sum(expo, axis=-1, keepdims=True)
    probs = (expo / total).astype(BF)
    out = gather_rows(dot(probs, values))
    log_total = top + jnp.log(total)
    count = log_total.shape[0] // HEADS
    packed = pack_lanes([log_total[h * count : (h + 1) * count] for h in range(HEADS)])
    oo[...] = out[:own]
    op[...] = out[own:].astype(BF)
    so[...] = packed[:own]
    sp[...] = packed[own:]


def forward_body(
    slot_rows,
    holding,
    oo,
    orecv,
    so,
    srecv,
    latent,
    cot,
    wo,
    wup,
    wdown,
    gain,
    bias,
    new_latents,
    act_out,
    pre_out,
    ffn_t,
    og_out,
    residual_grad,
    attended_grad,
    stats,
    output_grad,
    vectors,
    residual,
    ffn_in,
    acc,
    gacc,
    attended,
    packed,
):
    step = pl.program_id(0)
    count = latent.shape[0]
    slot = lax.broadcasted_iota(jnp.int32, (count, 1), 0) // slot_rows
    live = jnp.where(slot < holding[0, 0], 1.0, 0.0).astype(F32)

    @pl.when(step == 0)
    def _():
        a, b = so[...], srecv[...]
        top = jnp.maximum(a, b)
        both = top + jnp.log(jnp.exp(a - top) + jnp.exp(b - top))
        packed[...] = both
        mix = widen(jnp.exp(a - both)) * oo[...]
        mix += widen(jnp.exp(b - both)) * orecv[...].astype(F32)
        attended[...] = mix
        res = latent[...].astype(F32) + dot(mix.astype(BF), wo[...])
        residual[...] = res
        unit, _ = centred(res)
        low = (unit * gain[...] + bias[...]).astype(BF)
        ffn_in[...] = low
        ffn_t[...] = low.T
        og_out[...] = (cot[...].astype(F32) * live).astype(BF)
        acc[...] = jnp.zeros_like(acc)
        gacc[...] = jnp.zeros_like(gacc)

    pre = dot(ffn_in[...], wup[...])
    cdf = 0.5 * (1.0 + lax.erf(pre * (0.5**0.5)))
    act = (pre * cdf).astype(BF)
    act_out[...] = act
    acc[...] += dot(act, wdown[...])
    act_grad = dot_t(og_out[...], wdown[...])
    pdf = jnp.exp(-0.5 * pre * pre) * 0.3989422804014327
    pre_grad = (act_grad * (cdf + pre * pdf)).astype(BF)
    pre_out[...] = pre_grad
    gacc[...] += dot_t(pre_grad, wup[...])

    @pl.when(step == pl.num_programs(0) - 1)
    def _():
        res = residual[...]
        new_latents[...] = ((res + acc[...]) * live).astype(BF)
        unit, scale = centred(res)
        grad = gacc[...]
        vectors[0:1, :] = column_sum(grad * unit)
        vectors[1:2, :] = column_sum(grad)
        res_grad = og_out[...].astype(F32) + norm_back(unit, scale, gain[...], grad)
        residual_grad[...] = res_grad
        branch = res_grad.astype(BF)
        back = dot_t(branch, wo[...]).astype(BF)
        attended_grad[...] = back
        mix = attended[...]
        product = back.astype(F32) * mix
        head = head_of(product.shape)
        sums = [
            jnp.sum(jnp.where(head == h, product, 0.0), axis=-1, keepdims=True)
            for h in range(HEADS)
        ]
        delta = pack_lanes(sums)
        lane = lax.broadcasted_iota(jnp.int32, delta.shape, 1)
        stats[...] = jnp.where(lane % PER < PER // 2, packed[...], delta)
        output_grad[...] = t_dot(mix.astype(BF), branch).astype(BF)


def attend_back_body(qo, qp, kp, vp, kl, vl, do, dp, so, sp, dkvp, dkvl, dqo, dqp):
    own = qo.shape[0]
    patches = kp.shape[0]
    big = spread_rows(jnp.concatenate([qo[...], qp[...]], axis=0))
    back = spread_rows(jnp.concatenate([do[...], dp[...]], axis=0))
    keys = jnp.concatenate([kp[...], kl[...]], axis=0)
    values = jnp.concatenate([vp[...], vl[...]], axis=0)
    stats = jnp.concatenate([so[...], sp[...]], axis=0)
    probs = jnp.exp(dot_t(big, keys) - stack_heads(stats, 0))
    score_grad = (probs * (dot_t(back, values) - stack_heads(stats, PER // 2))).astype(BF)
    values_grad = t_dot(probs.astype(BF), back).astype(BF)
    keys_grad = t_dot(score_grad, big).astype(BF)
    dkvp[:, :INNER] = keys_grad[:patches]
    dkvp[:, INNER:] = values_grad[:patches]
    dkvl[:, :INNER] = keys_grad[patches:]
    dkvl[:, INNER:] = values_grad[patches:]
    dq = gather_rows(dot(score_grad, keys))
    dqo[...] = dq[:own]
    dqp[...] = dq[own:].astype(BF)


def up_grad_body(left, right, out):
    out[...] = dot(left[...], right[...]).astype(BF)


def down_grad_body(left, right, out):
    out[...] = t_dot(left[...], right[...]).astype(BF)


def kv_grad_body(media, latent, dkvp, dkvl, out):
    out[...] = (t_dot(media[...], dkvp[...]) + t_dot(latent[...], dkvl[...])).astype(BF)


def patch_back_body(patch, dkvp, wk, wv, gain, out, vectors):
    @pl.when(pl.program_id(0) == 0)
    def _():
        vectors[...] = jnp.zeros_like(vectors)

    grad = dot_t(dkvp[:, :INNER], wk[...]) + dot_t(dkvp[:, INNER:], wv[...])
    unit, scale = centred(patch[...].astype(F32))
    vectors[0:1, :] += column_sum(grad * unit)
    vectors[1:2, :] += column_sum(grad)
    out[...] = norm_back(unit, scale, gain[...], grad)


def latent_back_body(
    latent, norm, dkvl, dqo, drecv, residual_grad, wq, wk, wv, gain, out, query_grad, vectors
):
    dq = (dqo[...] + drecv[...].astype(F32)).astype(BF)
    product = (HEAD_DIM**-0.5 * t_dot(norm[...], dq)).astype(BF)
    if query_grad.shape == product.shape:
        query_grad[...] = product
    else:
        product = product.reshape(-1, 32, INNER)
        shape = query_grad.shape[:-1] + (INNER,)
        query_grad[..., :INNER] = product[:, :16].reshape(shape)
        query_grad[..., INNER:] = product[:, 16:].reshape(shape)
    grad = dot_t(dkvl[:, :INNER], wk[...]) + dot_t(dkvl[:, INNER:], wv[...])
    grad += HEAD_DIM**-0.5 * dot_t(dq, wq[...])
    unit, scale = centred(latent[...].astype(F32))
    vectors[0:1, :] = column_sum(grad * unit)
    vectors[1:2, :] = column_sum(grad)
    out[...] = residual_grad[...] + norm_back(unit, scale, gain[...], grad)


def first_body(ints, latent, cot, gain, bias, wq, norm, query, og):
    unit, _ = centred(latent[...].astype(F32))
    low = (unit * gain[...] + bias[...]).astype(BF)
    norm[...] = low
    query[...] = (HEAD_DIM**-0.5 * dot(low, wq[...])).astype(BF)
    count = latent.shape[0]
    slot = lax.broadcasted_iota(jnp.int32, (count, 1), 0) // ints[6]
    live = jnp.where(slot < ints[0], 1.0, 0.0).astype(F32)
    og[...] = (cot[...].astype(F32) * live).astype(BF)


def ffn_body(
    ints,
    oo,
    orecv,
    so,
    srecv,
    latent,
    og,
    wo,
    wup,
    wdown,
    gain,
    bias,
    new_latents,
    act_own,
    act_send,
    pre_out,
    ffn_own,
    ffn_send,
    residual,
    gacc,
    attended,
    packed,
    ffn_in,
    acc,
):
    step = pl.program_id(0)
    count = latent.shape[0]
    core = ints[1]

    @pl.when(step == 0)
    def _():
        a, b = so[...], srecv[...]
        top = jnp.maximum(a, b)
        both = top + jnp.log(jnp.exp(a - top) + jnp.exp(b - top))
        packed[...] = both
        mix = widen(jnp.exp(a - both)) * oo[...]
        mix += widen(jnp.exp(b - both)) * orecv[...].astype(F32)
        attended[...] = mix
        res = latent[...].astype(F32) + dot(mix.astype(BF), wo[...])
        residual[...] = res
        unit, _ = centred(res)
        low = (unit * gain[...] + bias[...]).astype(BF)
        ffn_in[...] = low
        turned = low.T.reshape(8, 2, -1, count)
        even, odd = turned[:, 0], turned[:, 1]
        ffn_own[...] = jnp.where(core == 0, even, odd).reshape(ffn_own.shape)
        ffn_send[...] = jnp.where(core == 0, odd, even).reshape(ffn_send.shape)
        acc[...] = jnp.zeros_like(acc)
        gacc[...] = jnp.zeros_like(gacc)

    pre = dot(ffn_in[...], wup[...])
    cdf = 0.5 * (1.0 + lax.erf(pre * (0.5**0.5)))
    act = (pre * cdf).astype(BF)
    turned = act.T
    half = turned.shape[0] // 2
    even, odd = turned[:half], turned[half:]
    act_own[...] = jnp.where(core == 0, even, odd).reshape(act_own.shape)
    act_send[...] = jnp.where(core == 0, odd, even).reshape(act_send.shape)
    acc[...] += dot(act, wdown[...])
    act_grad = dot_t(og[...], wdown[...])
    pdf = jnp.exp(-0.5 * pre * pre) * 0.3989422804014327
    pre_grad = (act_grad * (cdf + pre * pdf)).astype(BF)
    pre_out[...] = pre_grad
    gacc[...] += dot_t(pre_grad, wup[...])

    @pl.when(step == pl.num_programs(0) - 1)
    def _():
        slot = lax.broadcasted_iota(jnp.int32, (count, 1), 0) // ints[6]
        live = jnp.where(slot < ints[0], 1.0, 0.0).astype(F32)
        new_latents[...] = ((residual[...] + acc[...]) * live).astype(BF)


def ffn_back_body(
    residual, gacc, og, mix_ref, packed, wo, gain, residual_grad, attended_grad, stats, out, vectors
):
    unit, scale = centred(residual[...])
    grad = gacc[...]
    vectors[0:1, :] = column_sum(grad * unit)
    vectors[1:2, :] = column_sum(grad)
    res_grad = og[...].astype(F32) + norm_back(unit, scale, gain[...], grad)
    residual_grad[...] = res_grad
    branch = res_grad.astype(BF)
    back = dot_t(branch, wo[...]).astype(BF)
    attended_grad[...] = back
    mix = mix_ref[...]
    product = back.astype(F32) * mix
    head = head_of(product.shape)
    sums = [
        jnp.sum(jnp.where(head == h, product, 0.0), axis=-1, keepdims=True) for h in range(HEADS)
    ]
    delta = pack_lanes(sums)
    lane = lax.broadcasted_iota(jnp.int32, delta.shape, 1)
    stats[...] = jnp.where(lane % PER < PER // 2, packed[...], delta)
    out[...] = t_dot(mix.astype(BF), branch).astype(BF).reshape(out.shape)


def pick(ref, part, bit):
    if part == 0:
        v = ref[:, :, :, bit]
    elif part == 1:
        v = ref[:, :, bit]
    else:
        v = ref[:, bit]
    return v.reshape(-1, v.shape[-1])


def down_part_body(ints, own, sib, og, og_sib, a_out, a_keep, b_out, b_keep, c_out, c_keep):
    step = pl.program_id(0)

    def fill(part, out, keep):
        bit = ints[2 + part]
        for ref, b in ((out, 1 - bit), (keep, bit)):
            v = dot(pick(own, part, b), og[...]) + dot(pick(sib, part, b), og_sib[...])
            v = v.astype(BF).reshape(8, 4, 32, v.shape[-1])
            wide = v.shape[-1]
            for k in range(4):
                ref[:, 0, :, k * wide : (k + 1) * wide] = v[:, k]

    @pl.when(step < 2)
    def _():
        fill(0, a_out, a_keep)

    @pl.when(step == 2)
    def _():
        fill(1, b_out, b_keep)

    @pl.when(step == 3)
    def _():
        fill(2, c_out, c_keep)


def up_part_body(ints, own, sib, pre, pre_sib, a_out, a_keep, b_out, b_keep, c_out, c_keep):
    step = pl.program_id(0)

    def fill(part, out, keep):
        bit = ints[2 + part]
        for ref, b in ((out, 1 - bit), (keep, bit)):
            v = dot(pick(own, part, b), pre[...]) + dot(pick(sib, part, b), pre_sib[...])
            ref[...] = v.astype(BF).reshape(ref.shape)

    @pl.when(step == 0)
    def _():
        fill(0, a_out, a_keep)

    @pl.when((step == 1) | (step == 2))
    def _():
        fill(1, b_out, b_keep)

    @pl.when(step == 3)
    def _():
        fill(2, c_out, c_keep)


def plus(a, b):
    return a.astype(F32) + b.astype(F32)


def reduce_body(
    akd, ard, aku, aru, bkd, brd, bku, bru, ckd, crd, cku, cru,
    kv, og, qg, media_vec, latent_vec, ffn_vec,
    fin, vec,
    wa, wb, wc, ra1, ra2, ra3, a2, a3, rb1, rb2, rb3, b2, b3, rc1, rc2, rc3, c2, c3,
    kk, rk0, wk, rk1, k2, rk2, k3, rk3, k4, rk4,
    kq, rq0, wq, rq1, q2, rq2, q3, rq3, q4, rq4,
    vs, vr, load_sem, send_sem, recv_sem,
):
    mine = lax.axis_index("img")
    xb = lax.axis_index("lat")
    cb, yb, z1, z2 = mine % 2, (mine // 2) % 2, (mine // 4) % 2, (mine // 8) % 2

    def to(bit, weight):
        return (mine + weight - 2 * weight * bit, xb)

    peer = {"c": to(cb, 1), "y": to(yb, 2), "z": to(z1, 4), "w": to(z2, 8), "x": (mine, 1 - xb)}
    barrier = pltpu.get_barrier_semaphore()
    for axis in peer:
        pl.semaphore_signal(
            barrier, inc=1, device_id=peer[axis], device_id_type=pl.DeviceIdType.MESH
        )

    used = []

    def send(src, dst, axis):
        slot = len(used)
        copy = pltpu.make_async_remote_copy(
            src_ref=src,
            dst_ref=dst,
            send_sem=send_sem.at[slot],
            recv_sem=recv_sem.at[slot],
            device_id=peer[axis],
            device_id_type=pl.DeviceIdType.MESH,
        )
        copy.start()
        used.append(copy)
        return copy

    loads = []
    for i, (src, dst) in enumerate(
        (
            (kv.at[:, :, :, cb], kk),
            (og.at[:, :, :, cb], kq.at[:, :, :, :, pl.ds(0, 16)]),
            (qg.at[:, :, :, cb], kq.at[:, :, :, :, pl.ds(16, 16)]),
        )
    ):
        loads.append(pltpu.make_async_copy(src, dst, load_sem.at[i]))
        loads[-1].start()
    vs[0] = jnp.zeros(vs.shape[1:], F32)
    vs[0, 0:2, :] = media_vec[...]
    vs[0, 2:4, :] = latent_vec[...]
    vs[0, 4:6, :] = ffn_vec[...]

    pl.semaphore_wait(barrier, len(peer))
    q0 = send(qg.at[:, :, :, 1 - cb], rq0.at[:, :, :, :, pl.ds(16, 16)], "c")
    o0 = send(og.at[:, :, :, 1 - cb], rq0.at[:, :, :, :, pl.ds(0, 16)], "c")
    k0 = send(kv.at[:, :, :, 1 - cb], rk0, "c")
    vec_order = "cxyzw"
    vc = send(vs.at[0], vr.at[0], vec_order[0])

    def vec_step(i, vc):
        vc.wait_recv()
        if i < 4:
            vs[i + 1] = vs[i] + vr[i]
            return send(vs.at[i + 1], vr.at[i + 1], vec_order[i + 1])
        vec[...] = vs[i] + vr[i]

    wa[:, :, :, 0:2] = plus(akd[...], ard[...]).astype(BF)
    wa[:, :, :, 2:3] = plus(aku[...], aru[...]).astype(BF)
    sa1 = send(wa.at[:, :, 1 - yb], ra1, "y")
    wb[:, :, :, 0:1] = plus(bkd[...], brd[...]).astype(BF)
    wb[:, :, :, 1:3] = plus(bku[...], bru[...]).astype(BF)
    sb1 = send(wb.at[:, :, 1 - xb], rb1, "x")
    loads[0].wait()
    k0.wait_recv()
    wk[...] = plus(kk[...], rk0[...]).astype(BF)
    sk1 = send(wk.at[:, :, :, 1 - xb], rk1, "x")
    wc[:, :, :, 0:1] = plus(ckd[...], crd[...]).astype(BF)
    wc[:, :, :, 1:2] = plus(cku[...], cru[...]).astype(BF)
    sc1 = send(wc.at[:, :, 1 - xb], rc1, "x")
    loads[1].wait()
    loads[2].wait()
    q0.wait_recv()
    o0.wait_recv()
    wq[...] = plus(kq[...], rq0[...]).astype(BF)
    sq1 = send(wq.at[:, 1 - z1], rq1, "z")
    vc = vec_step(0, vc)

    sa1.wait_recv()
    a2[...] = plus(wa[:, :, yb], ra1[...]).astype(BF)
    sa2 = send(a2.at[:, 1 - z1], ra2, "z")
    sb1.wait_recv()
    b2[...] = plus(wb[:, :, xb], rb1[...]).astype(BF)
    sb2 = send(b2.at[:, 1 - z1], rb2, "z")
    vc = vec_step(1, vc)
    sk1.wait_recv()
    k2[...] = plus(wk[:, :, :, xb], rk1[...]).astype(BF)
    sk2 = send(k2.at[:, :, 1 - yb], rk2, "y")
    sc1.wait_recv()
    c2[...] = plus(wc[:, :, xb], rc1[...]).astype(BF)
    sc2 = send(c2.at[:, 1 - yb], rc2, "y")
    sq1.wait_recv()
    q2[...] = plus(wq[:, z1], rq1[...]).astype(BF)
    sq2 = send(q2.at[:, :, 1 - xb], rq2, "x")
    vc = vec_step(2, vc)

    sa2.wait_recv()
    a3[...] = plus(a2[:, z1], ra2[...]).astype(BF)
    sa3 = send(a3.at[1 - z2], ra3, "w")
    sb2.wait_recv()
    b3[...] = plus(b2[:, z1], rb2[...]).astype(BF)
    sb3 = send(b3.at[1 - z2], rb3, "w")
    sk2.wait_recv()
    k3[...] = plus(k2[:, :, yb], rk2[...]).astype(BF)
    sk3 = send(k3.at[:, 1 - z1], rk3, "z")
    sc2.wait_recv()
    c3[...] = plus(c2[:, yb], rc2[...]).astype(BF)
    sc3 = send(c3.at[1 - z2], rc3, "w")
    sq2.wait_recv()
    q3[...] = plus(q2[:, :, xb], rq2[...]).astype(BF)
    sq3 = send(q3.at[:, 1 - yb], rq3, "y")
    vc = vec_step(3, vc)

    sk3.wait_recv()
    k4[...] = plus(k3[:, z1], rk3[...]).astype(BF)
    sk4 = send(k4.at[1 - z2], rk4, "w")
    sq3.wait_recv()
    q4[...] = plus(q3[:, yb], rq3[...]).astype(BF)
    sq4 = send(q4.at[1 - z2], rq4, "w")
    sa3.wait_recv()
    fin[0:3] = plus(a3[z2], ra3[...])
    sb3.wait_recv()
    fin[3:6] = plus(b3[z2], rb3[...])
    sc3.wait_recv()
    fin[6:8] = plus(c3[z2], rc3[...])
    vec_step(4, vc)
    sk4.wait_recv()
    fin[8] = plus(k4[z2], rk4[...])
    sq4.wait_recv()
    fin[9] = plus(q4[z2], rq4[...])
    for copy in used:
        copy.wait_send()


def unpack_body(ints, fin, vec, up, down, key, value, out, query, thin):
    for g, i in enumerate((2, 4, 5, 7)):
        up[:, g * 1024 : (g + 1) * 1024] = fin[i]
    for g, i in enumerate((0, 1, 3, 6)):
        for k in range(4):
            down[k * 32 : (k + 1) * 32, g * 256 : (g + 1) * 256] = fin[
                i, :, k * 256 : (k + 1) * 256
            ]
    key[...] = fin[8, :, :INNER]
    value[...] = fin[8, :, INNER:]
    out[...] = fin[9, 0:16]
    query[0:16] = fin[9, 16:32, :INNER]
    query[16:32] = fin[9, 16:32, INNER:]
    width = vec.shape[1]
    turned = pltpu.roll(vec[...], width - ints[5] * 32, 1)
    thin[...] = turned[:, :LANES]


def swap_lat(v):
    return lax.ppermute(v, "lat", [(0, 1), (1, 0)])


def halving_sum(v, order, bits, count, keep):
    left = list(range(bits - 1, -1, -1)) + [-1]
    mine = lax.axis_index("img")
    for place, axis in enumerate(order):
        dim = left.index(axis)
        if axis < 0:
            bit = lax.axis_index("lat")
            pairs, name = [(0, 1), (1, 0)], "lat"
        else:
            bit = (mine // 2**axis) % 2
            pairs, name = [(i, i ^ 2**axis) for i in range(count)], "img"
        out = lax.dynamic_index_in_dim(v, 1 - bit, dim, keepdims=False)
        stay = lax.dynamic_index_in_dim(v, bit, dim, keepdims=False)
        got = lax.ppermute(out, name, pairs)
        v = stay.astype(F32) + got.astype(F32)
        if place < len(order) - 1 and keep == BF:
            v = v.astype(BF)
        left.pop(dim)
    return v


def local(
    count,
    patches,
    latents,
    cotangent,
    doc_images,
    doc_device,
    query_weight,
    key_weight,
    value_weight,
    output_weight,
    up_weight,
    down_weight,
    media_gain,
    media_bias,
    latent_gain,
    latent_bias,
    ffn_gain,
    ffn_bias,
):
    slots, own_patches, width = patches.shape
    own_latents = latents.shape[1]
    hidden = up_weight.shape[1]
    np_, nl = slots * own_patches, slots * own_latents
    mine = lax.axis_index("img")
    holding = jnp.sum(jnp.where(doc_device == mine, doc_images, 0)).reshape(1, 1)
    patch = patches.reshape(np_, width)
    latent = latents.reshape(nl, width)
    cot = cotangent.reshape(nl, width)
    mg, mb = media_gain.reshape(1, width), media_bias.reshape(1, width)
    lg, lb = latent_gain.reshape(1, width), latent_bias.reshape(1, width)
    fg, fb = ffn_gain.reshape(1, width), ffn_bias.reshape(1, width)
    wspec = whole((width, INNER))
    vspec = whole((1, width))
    lspec = whole((nl, width))

    norm_l, query = call(
        latent_body,
        (1,),
        [lspec, vspec, vspec, wspec],
        [(struct((nl, width), BF), lspec), (struct((nl, INNER), BF), whole((nl, INNER)))],
        (latent, lg, lb, query_weight),
        2 * nl * width * INNER,
    )
    query_peer = swap_lat(query)
    blk = min(np_, 256)
    norm_m, kp, vp, kl, vl = call(
        media_body,
        (np_ // blk,),
        [rows(blk, width), vspec, vspec, wspec, wspec, lspec],
        [
            (struct((np_, width), BF), rows(blk, width)),
            (struct((np_, INNER), BF), rows(blk, INNER)),
            (struct((np_, INNER), BF), rows(blk, INNER)),
            (struct((nl, INNER), BF), whole((nl, INNER))),
            (struct((nl, INNER), BF), whole((nl, INNER))),
        ],
        (patch, mg, mb, key_weight, value_weight, norm_l),
        4 * (np_ + nl) * width * INNER,
    )
    q_s, p_s, s_s = rows(own_latents, INNER), rows(own_patches, INNER), rows(own_latents, LANES)
    att_flops = 4 * slots * (own_patches + own_latents) * INNER * INNER
    o_own, o_peer, s_own, s_peer = call(
        attend_body,
        (slots,),
        [q_s, q_s, p_s, p_s, q_s, q_s],
        [
            (struct((nl, INNER), F32), q_s),
            (struct((nl, INNER), BF), q_s),
            (struct((nl, LANES), F32), s_s),
            (struct((nl, LANES), F32), s_s),
        ],
        (query, query_peer, kp, vp, kl, vl),
        att_flops,
    )
    o_recv, s_recv = swap_lat(o_peer), swap_lat(s_peer)
    fblk = min(hidden, 512)
    nspec = whole((nl, INNER))
    (
        new_latents,
        act,
        pre_grad,
        ffn_t,
        out_grad,
        residual_grad,
        attended_grad,
        stats,
        output_grad,
        ffn_vec,
    ) = call(
        partial(forward_body, own_latents),
        (hidden // fblk,),
        [
            pl.BlockSpec(memory_space=pltpu.SMEM),
            nspec,
            nspec,
            whole((nl, LANES)),
            whole((nl, LANES)),
            lspec,
            lspec,
            whole((INNER, width)),
            cols(width, fblk),
            rows(fblk, width),
            vspec,
            vspec,
        ],
        [
            (struct((nl, width), BF), lspec),
            (struct((nl, hidden), BF), cols(nl, fblk)),
            (struct((nl, hidden), BF), cols(nl, fblk)),
            (struct((width, nl), BF), whole((width, nl))),
            (struct((nl, width), BF), lspec),
            (struct((nl, width), F32), lspec),
            (struct((nl, INNER), BF), nspec),
            (struct((nl, LANES), F32), whole((nl, LANES))),
            (struct((INNER, width), BF), whole((INNER, width))),
            (struct((2, width), F32), whole((2, width))),
        ],
        (
            holding,
            o_own,
            o_recv,
            s_own,
            s_recv,
            latent,
            cot,
            output_weight,
            up_weight,
            down_weight,
            fg,
            fb,
        ),
        8 * nl * width * hidden,
        scratch=[
            pltpu.VMEM((nl, width), F32),
            pltpu.VMEM((nl, width), BF),
            pltpu.VMEM((nl, width), F32),
            pltpu.VMEM((nl, width), F32),
            pltpu.VMEM((nl, INNER), F32),
            pltpu.VMEM((nl, LANES), F32),
        ],
    )
    grad_peer, stats_peer = swap_lat(attended_grad), swap_lat(stats)
    (down_grad,) = call(
        down_grad_body,
        (hidden // fblk,),
        [cols(nl, fblk), lspec],
        [(struct((hidden, width), BF), rows(fblk, width))],
        (act, out_grad),
        2 * nl * width * hidden,
    )
    (up_grad,) = call(
        up_grad_body,
        (hidden // fblk,),
        [whole((width, nl)), cols(nl, fblk)],
        [(struct((width, hidden), BF), cols(width, fblk))],
        (ffn_t, pre_grad),
        2 * nl * width * hidden,
    )
    dkvp, dkvl, dq_own, dq_peer = call(
        attend_back_body,
        (slots,),
        [q_s, q_s, p_s, p_s, q_s, q_s, q_s, q_s, s_s, s_s],
        [
            (struct((np_, 2 * INNER), BF), rows(own_patches, 2 * INNER)),
            (struct((nl, 2 * INNER), BF), rows(own_latents, 2 * INNER)),
            (struct((nl, INNER), F32), q_s),
            (struct((nl, INNER), BF), q_s),
        ],
        (query, query_peer, kp, vp, kl, vl, attended_grad, grad_peer, stats, stats_peer),
        att_flops * 5 // 2,
    )
    dq_recv = swap_lat(dq_peer)
    kblk = 256
    (kv_grad,) = call(
        kv_grad_body,
        (2 * INNER // kblk,),
        [whole((np_, width)), lspec, cols(np_, kblk), cols(nl, kblk)],
        [(struct((width, 2 * INNER), BF), cols(width, kblk))],
        (norm_m, norm_l, dkvp, dkvl),
        4 * (np_ + nl) * width * INNER,
    )
    patches_grad, media_vec = call(
        patch_back_body,
        (np_ // blk,),
        [rows(blk, width), rows(blk, 2 * INNER), wspec, wspec, vspec],
        [(struct((np_, width), F32), rows(blk, width)), (struct((2, width), F32), whole((2, width)))],
        (patch, dkvp, key_weight, value_weight, mg),
        4 * np_ * width * INNER,
    )
    latents_grad, query_grad, latent_vec = call(
        latent_back_body,
        (1,),
        [
            lspec,
            lspec,
            whole((nl, 2 * INNER)),
            nspec,
            nspec,
            lspec,
            wspec,
            wspec,
            wspec,
            vspec,
        ],
        [
            (struct((nl, width), F32), lspec),
            (struct((width, INNER), BF), wspec),
            (struct((2, width), F32), whole((2, width))),
        ],
        (
            latent,
            norm_l,
            dkvl,
            dq_own,
            dq_recv,
            residual_grad,
            query_weight,
            key_weight,
            value_weight,
            lg,
        ),
        8 * nl * width * INNER,
    )

    bits = count.bit_length() - 1
    first = list(range(1, bits))
    orders = (
        [0, -1] + first,
        [0] + first + [-1],
        [0] + first[1:] + [-1] + first[:1],
    )

    def reduce(v, order, keep=BF):
        shape = (2,) * (bits + 1) + (v.shape[0] // (2 * count),) + v.shape[1:]
        return halving_sum(v.reshape(shape), order, bits, count, keep)

    def reduce_parts(v):
        unit = v.shape[1] // 8
        cuts = (0, 3 * unit, 6 * unit, 8 * unit)
        return jnp.concatenate(
            [reduce(v[:, a:b], order) for a, b, order in zip(cuts, cuts[1:], orders)], axis=1
        )

    down_sum = reduce_parts(down_grad)
    up_sum = reduce_parts(up_grad)
    output_sum = reduce(output_grad, orders[1])
    kv_sum = reduce_parts(kv_grad)
    query_sum = reduce(query_grad, orders[0])
    vec = jnp.concatenate([media_vec, latent_vec, ffn_vec], axis=0)
    vec = vec.reshape(6, 2 * count, width // (2 * count)).transpose(1, 0, 2)
    vec_sum = reduce(vec, orders[2], F32)[0]
    return (
        new_latents.reshape(latents.shape),
        patches_grad.reshape(patches.shape),
        latents_grad.reshape(latents.shape),
        query_sum,
        kv_sum[:, :INNER],
        kv_sum[:, INNER:],
        output_sum,
        up_sum,
        down_sum,
        vec_sum[0],
        vec_sum[1],
        vec_sum[2],
        vec_sum[3],
        vec_sum[4],
        vec_sum[5],
    )


def fits(mesh):
    return mesh.shape["img"] == 16 and mesh.shape["lat"] == 2


def quick(
    count,
    patches,
    latents,
    cotangent,
    doc_images,
    doc_device,
    query_weight,
    key_weight,
    value_weight,
    output_weight,
    up_weight,
    down_weight,
    media_gain,
    media_bias,
    latent_gain,
    latent_bias,
    ffn_gain,
    ffn_bias,
):
    slots, own_patches, width = patches.shape
    own_latents = latents.shape[1]
    hidden = up_weight.shape[1]
    np_, nl = slots * own_patches, slots * own_latents
    mine, lat = lax.axis_index("img"), lax.axis_index("lat")
    holding = jnp.sum(jnp.where(doc_device == mine, doc_images, 0))
    ints = jnp.stack(
        [
            holding,
            mine % 2,
            lat,
            (mine // 2) % 2,
            (mine // 4) % 2,
            mine * 2 + lat,
            jnp.int32(own_latents),
            jnp.int32(0),
        ]
    ).astype(jnp.int32)
    sspec = pl.BlockSpec(memory_space=pltpu.SMEM)
    patch = patches.reshape(np_, width)
    latent = latents.reshape(nl, width)
    cot = cotangent.reshape(nl, width)
    mg, mb = media_gain.reshape(1, width), media_bias.reshape(1, width)
    lg, lb = latent_gain.reshape(1, width), latent_bias.reshape(1, width)
    fg, fb = ffn_gain.reshape(1, width), ffn_bias.reshape(1, width)
    wspec = whole((width, INNER))
    vspec = whole((1, width))
    lspec = whole((nl, width))
    nspec = whole((nl, INNER))
    core_pairs = [(i, i ^ 1) for i in range(count)]

    def sibling(v):
        return lax.ppermute(v, "img", core_pairs)

    norm_l, query, out_grad = call(
        first_body,
        (1,),
        [sspec, lspec, lspec, vspec, vspec, wspec],
        [
            (struct((nl, width), BF), lspec),
            (struct((nl, INNER), BF), nspec),
            (struct((nl, width), BF), lspec),
        ],
        (ints, latent, cot, lg, lb, query_weight),
        2 * nl * width * INNER,
    )
    query_peer = swap_lat(query)
    og_sib = sibling(out_grad)
    blk = 256
    norm_m, kp, vp, kl, vl = call(
        media_body,
        (np_ // blk,),
        [rows(blk, width), vspec, vspec, wspec, wspec, lspec],
        [
            (struct((np_, width), BF), rows(blk, width)),
            (struct((np_, INNER), BF), rows(blk, INNER)),
            (struct((np_, INNER), BF), rows(blk, INNER)),
            (struct((nl, INNER), BF), nspec),
            (struct((nl, INNER), BF), nspec),
        ],
        (patch, mg, mb, key_weight, value_weight, norm_l),
        4 * (np_ + nl) * width * INNER,
    )
    q_s, p_s, s_s = rows(own_latents, INNER), rows(own_patches, INNER), rows(own_latents, LANES)
    att_flops = 4 * slots * (own_patches + own_latents) * INNER * INNER
    o_own, o_peer, s_own, s_peer = call(
        attend_body,
        (slots,),
        [q_s, q_s, p_s, p_s, q_s, q_s],
        [
            (struct((nl, INNER), F32), q_s),
            (struct((nl, INNER), BF), q_s),
            (struct((nl, LANES), F32), s_s),
            (struct((nl, LANES), F32), s_s),
        ],
        (query, query_peer, kp, vp, kl, vl),
        att_flops,
    )
    o_recv, s_recv = swap_lat(o_peer), swap_lat(s_peer)
    fblk = hidden // 8
    turned = (2, 2, 2, 2, fblk // 4, nl)
    turned_spec = pl.BlockSpec(
        (1, 1, 1) + turned[3:], lambda i: (i // 4, (i // 2) % 2, i % 2, 0, 0, 0)
    )
    ffn_turned = (2, 2, 2, 2, width // (2 * count), nl)
    stat = whole((nl, LANES))
    (
        new_latents,
        act_own,
        act_send,
        pre_grad,
        ffn_own,
        ffn_send,
        residual,
        gacc,
        attended,
        packed,
    ) = call(
        ffn_body,
        (8,),
        [
            sspec,
            nspec,
            nspec,
            stat,
            stat,
            lspec,
            lspec,
            whole((INNER, width)),
            cols(width, fblk),
            rows(fblk, width),
            vspec,
            vspec,
        ],
        [
            (struct((nl, width), BF), lspec),
            (struct(turned, BF), turned_spec),
            (struct(turned, BF), turned_spec),
            (struct((nl, hidden), BF), cols(nl, fblk)),
            (struct(ffn_turned, BF), whole(ffn_turned)),
            (struct(ffn_turned, BF), whole(ffn_turned)),
            (struct((nl, width), F32), lspec),
            (struct((nl, width), F32), lspec),
            (struct((nl, INNER), F32), nspec),
            (struct((nl, LANES), F32), stat),
        ],
        (
            ints,
            o_own,
            o_recv,
            s_own,
            s_recv,
            latent,
            out_grad,
            output_weight,
            up_weight,
            down_weight,
            fg,
            fb,
        ),
        8 * nl * width * hidden,
        scratch=[pltpu.VMEM((nl, width), BF), pltpu.VMEM((nl, width), F32)],
    )
    act_sib, pre_sib, ffn_sib = sibling(act_send), sibling(pre_grad), sibling(ffn_send)
    o_shape = (2, 2, 2, 2, 2, INNER // (2 * count), width)
    residual_grad, attended_grad, stats, output_grad, ffn_vec = call(
        ffn_back_body,
        (1,),
        [lspec, lspec, lspec, nspec, stat, whole((INNER, width)), vspec],
        [
            (struct((nl, width), F32), lspec),
            (struct((nl, INNER), BF), nspec),
            (struct((nl, LANES), F32), stat),
            (struct(o_shape, BF), whole(o_shape)),
            (struct((2, width), F32), whole((2, width))),
        ],
        (residual, gacc, out_grad, attended, packed, output_weight, fg),
        4 * nl * width * INNER,
    )
    grad_peer, stats_peer = swap_lat(attended_grad), swap_lat(stats)

    def part_outs(counts, first):
        outs = []
        for n, start in zip(counts, first):
            shape = (8, n, 32, 1024)
            spec = pl.BlockSpec(
                (8, 1, 32, 1024),
                lambda i, n=n, start=start: (0, jnp.clip(i - start, 0, n - 1), 0, 0),
            )
            outs += [(struct(shape, BF), spec)] * 2
        return outs

    def hops(parts):
        pairs = [[(i, i ^ 2) for i in range(count)], [(i, i ^ 4) for i in range(count)]]
        return (
            swap_lat(parts[0]),
            parts[1],
            lax.ppermute(parts[2], "img", pairs[0]),
            parts[3],
            lax.ppermute(parts[4], "img", pairs[1]),
            parts[5],
        )

    down_parts = call(
        down_part_body,
        (4,),
        [sspec, whole(turned), whole(turned), cols(nl, width // 4), cols(nl, width // 4)],
        part_outs((2, 1, 1), (0, 2, 3)),
        (ints, act_own, act_sib, out_grad, og_sib),
        2 * nl * width * hidden,
    )
    ard, akd, brd, bkd, crd, ckd = hops(down_parts)
    up_parts = call(
        up_part_body,
        (4,),
        [sspec, whole(ffn_turned), whole(ffn_turned), cols(nl, hidden // 4), cols(nl, hidden // 4)],
        part_outs((1, 2, 1), (0, 1, 3)),
        (ints, ffn_own, ffn_sib, pre_grad, pre_sib),
        2 * nl * width * hidden,
    )
    aru, aku, bru, bku, cru, cku = hops(up_parts)
    dkvp, dkvl, dq_own, dq_peer = call(
        attend_back_body,
        (slots,),
        [q_s, q_s, p_s, p_s, q_s, q_s, q_s, q_s, s_s, s_s],
        [
            (struct((np_, 2 * INNER), BF), rows(own_patches, 2 * INNER)),
            (struct((nl, 2 * INNER), BF), rows(own_latents, 2 * INNER)),
            (struct((nl, INNER), F32), q_s),
            (struct((nl, INNER), BF), q_s),
        ],
        (query, query_peer, kp, vp, kl, vl, attended_grad, grad_peer, stats, stats_peer),
        att_flops * 5 // 2,
    )
    dq_recv = swap_lat(dq_peer)
    kblk = 256
    (kv_grad,) = call(
        kv_grad_body,
        (2 * INNER // kblk,),
        [whole((np_, width)), lspec, cols(np_, kblk), cols(nl, kblk)],
        [(struct((width, 2 * INNER), BF), cols(width, kblk))],
        (norm_m, norm_l, dkvp, dkvl),
        4 * (np_ + nl) * width * INNER,
    )
    patches_grad, media_vec = call(
        patch_back_body,
        (np_ // blk,),
        [rows(blk, width), rows(blk, 2 * INNER), wspec, wspec, vspec],
        [(struct((np_, width), F32), rows(blk, width)), (struct((2, width), F32), whole((2, width)))],
        (patch, dkvp, key_weight, value_weight, mg),
        4 * np_ * width * INNER,
    )
    latents_grad, query_grad, latent_vec = call(
        latent_back_body,
        (1,),
        [
            lspec,
            lspec,
            whole((nl, 2 * INNER)),
            nspec,
            nspec,
            lspec,
            wspec,
            wspec,
            wspec,
            vspec,
        ],
        [
            (struct((nl, width), F32), lspec),
            (struct(o_shape, BF), whole(o_shape)),
            (struct((2, width), F32), whole((2, width))),
        ],
        (
            latent,
            norm_l,
            dkvl,
            dq_own,
            dq_recv,
            residual_grad,
            query_weight,
            key_weight,
            value_weight,
            lg,
        ),
        8 * nl * width * INNER,
    )
    block = (32, 1024)
    eight = [
        v.reshape((2, 2, 2, v.shape[1]) + block)
        for v in (akd, ard, aku, aru, bkd, brd, bku, bru, ckd, crd, cku, cru)
    ]
    kv = kv_grad.reshape((2, 2, 2, 2, 2) + block)
    inputs = eight + [kv, output_grad, query_grad, media_vec, latent_vec, ffn_vec]
    vmem = pl.BlockSpec(memory_space=pltpu.VMEM)
    hbm = pl.BlockSpec(memory_space=pl.ANY)

    def ladder(n):
        mid = (n,) + block
        return [(2, 2) + mid, (2,) + mid, mid], [(2, 2) + mid, (2,) + mid]

    scratch = [(2, 2, 2, n) + block for n in (3, 3, 2)]
    for n in (3, 3, 2):
        got, sums = ladder(n)
        scratch += got + sums
    for _ in range(2):
        full = (2, 2, 2, 2) + block
        scratch += [full, full, full]
        for k in (3, 2, 1):
            scratch += [(2,) * k + block] * 2
        scratch += [block]
    scratch = [pltpu.VMEM(shape, BF) for shape in scratch]
    copies = 24
    fin, vec = pl.pallas_call(
        reduce_body,
        in_specs=[vmem] * 12 + [hbm] * 3 + [vmem] * 3,
        out_specs=[vmem, vmem],
        out_shape=[struct((10,) + block, F32), struct((8, width), F32)],
        scratch_shapes=scratch
        + [
            pltpu.VMEM((5, 8, width), F32),
            pltpu.VMEM((5, 8, width), F32),
            pltpu.SemaphoreType.DMA((3,)),
            pltpu.SemaphoreType.DMA((copies + 1,)),
            pltpu.SemaphoreType.DMA((copies + 1,)),
        ],
        compiler_params=pltpu.CompilerParams(
            collective_id=0, has_side_effects=True, vmem_limit_bytes=VMEM_LIMIT
        ),
    )(*inputs)
    d = 2 * count
    shapes = [
        (width // d, hidden),
        (hidden // d, width),
        (width // d, INNER),
        (width // d, INNER),
        (INNER // d, width),
        (width // d, INNER),
        (8, LANES),
    ]
    up_sum, down_sum, key_sum, value_sum, output_sum, query_sum, thin = pl.pallas_call(
        unpack_body,
        in_specs=[sspec, vmem, vmem],
        out_specs=[vmem] * 7,
        out_shape=[struct(shape, F32) for shape in shapes],
    )(ints, fin, vec)
    thin = thin[:, : width // d]
    return (
        new_latents.reshape(latents.shape),
        patches_grad.reshape(patches.shape),
        latents_grad.reshape(latents.shape),
        query_sum,
        key_sum,
        value_sum,
        output_sum,
        up_sum,
        down_sum,
        thin[0],
        thin[1],
        thin[2],
        thin[3],
        thin[4],
        thin[5],
    )


def solution(mesh):
    split = P("img", "lat", None)
    both = P(("img", "lat"), None)
    line = P(("img", "lat"))
    return jax.shard_map(
        partial(quick if fits(mesh) else local, mesh.shape["img"]),
        mesh=mesh,
        in_specs=(split,) * 3 + (P(),) * 14,
        out_specs=(split,) * 3 + (both,) * 6 + (line,) * 6,
        check_vma=False,
    )
```

```python
from functools import partial
from types import SimpleNamespace

import jax
import jax.numpy as jnp
from jax import lax
from jax.experimental import pallas as pl
from jax.experimental.pallas import tpu as pltpu
from jax.sharding import PartitionSpec as P

HEADS = 8
HEAD_DIM = 64
INNER = HEADS * HEAD_DIM
LANES = 128
PER = LANES // HEADS
EPS = 1e-05
BF = jnp.bfloat16
F32 = jnp.float32
VMEM_LIMIT = 56 * 1024 * 1024


def dot(a, b):
    return lax.dot_general(a, b, (((1,), (0,)), ((), ())), preferred_element_type=F32)


def dot_t(a, b):
    return lax.dot_general(a, b, (((1,), (1,)), ((), ())), preferred_element_type=F32)


def t_dot(a, b):
    return lax.dot_general(a, b, (((0,), (0,)), ((), ())), preferred_element_type=F32)


def call(body, grid, ins, outs, args, flops, scratch=()):
    moved = sum(a.size * a.dtype.itemsize for a in args)
    moved += sum(o[0].size * o[0].dtype.itemsize for o in outs)
    return pl.pallas_call(
        body,
        grid=grid,
        in_specs=ins,
        out_specs=[o[1] for o in outs],
        out_shape=[o[0] for o in outs],
        scratch_shapes=list(scratch),
        compiler_params=pltpu.CompilerParams(
            dimension_semantics=("arbitrary",) * len(grid), vmem_limit_bytes=VMEM_LIMIT
        ),
        cost_estimate=pl.CostEstimate(flops=flops, bytes_accessed=moved, transcendentals=0),
    )(*args)


def whole(shape):
    return pl.BlockSpec(shape, lambda *_: (0,) * len(shape))


def rows(block, width):
    return pl.BlockSpec((block, width), lambda i: (i, 0))


def cols(height, block):
    return pl.BlockSpec((height, block), lambda i: (0, i))


def struct(shape, dtype):
    return jax.ShapeDtypeStruct(shape, dtype)


def centred(v):
    centre = v - jnp.mean(v, axis=-1, keepdims=True)
    scale = lax.rsqrt(jnp.mean(centre * centre, axis=-1, keepdims=True) + EPS)
    return centre * scale, scale


def norm_back(unit, scale, gain, grad):
    push = grad * gain
    mean_push = jnp.mean(push, axis=-1, keepdims=True)
    mean_both = jnp.mean(push * unit, axis=-1, keepdims=True)
    return scale * (push - mean_push - unit * mean_both)


def column_sum(v):
    return jnp.sum(v, axis=0, keepdims=True)


def latent_body(latent, gain, bias, wq, norm, query):
    unit, _ = centred(latent[...].astype(F32))
    low = (unit * gain[...] + bias[...]).astype(BF)
    norm[...] = low
    query[...] = (HEAD_DIM**-0.5 * dot(low, wq[...])).astype(BF)


def media_body(patch, gain, bias, wk, wv, latent_norm, norm, kp, vp, kl, vl):
    @pl.when(pl.program_id(0) == 0)
    def _():
        kl[...] = dot(latent_norm[...], wk[...]).astype(BF)
        vl[...] = dot(latent_norm[...], wv[...]).astype(BF)

    unit, _ = centred(patch[...].astype(F32))
    low = (unit * gain[...] + bias[...]).astype(BF)
    norm[...] = low
    kp[...] = dot(low, wk[...]).astype(BF)
    vp[...] = dot(low, wv[...]).astype(BF)


def head_of(shape):
    return lax.broadcasted_iota(jnp.int32, shape, 1) // HEAD_DIM


def spread_rows(v):
    head = head_of(v.shape)
    zero = jnp.zeros_like(v)
    return jnp.concatenate([jnp.where(head == h, v, zero) for h in range(HEADS)], axis=0)


def gather_rows(v):
    count = v.shape[0] // HEADS
    head = head_of((count, v.shape[1]))
    total = jnp.zeros((count, v.shape[1]), F32)
    for h in range(HEADS):
        total = jnp.where(head == h, v[h * count : (h + 1) * count], total)
    return total


def pack_lanes(columns):
    count = columns[0].shape[0]
    lane = lax.broadcasted_iota(jnp.int32, (count, LANES), 1)
    step = LANES // len(columns)
    total = jnp.zeros((count, LANES), F32)
    for h, column in enumerate(columns):
        total = jnp.where(lane // step == h, column, total)
    return total


def widen(packed):
    head = head_of((packed.shape[0], INNER))
    total = jnp.zeros((packed.shape[0], INNER), F32)
    for h in range(HEADS):
        total = jnp.where(head == h, packed[:, h * PER : h * PER + 1], total)
    return total


def stack_heads(packed, offset):
    return jnp.concatenate(
        [packed[:, h * PER + offset : h * PER + offset + 1] for h in range(HEADS)], axis=0
    )


def attend_body(qo, qp, kp, vp, kl, vl, oo, op, so, sp):
    own = qo.shape[0]
    big = spread_rows(jnp.concatenate([qo[...], qp[...]], axis=0))
    keys = jnp.concatenate([kp[...], kl[...]], axis=0)
    values = jnp.concatenate([vp[...], vl[...]], axis=0)
    scores = dot_t(big, keys)
    top = jnp.max(scores, axis=-1, keepdims=True)
    expo = jnp.exp(scores - top)
    total = jnp.sum(expo, axis=-1, keepdims=True)
    probs = (expo / total).astype(BF)
    out = gather_rows(dot(probs, values))
    log_total = top + jnp.log(total)
    count = log_total.shape[0] // HEADS
    packed = pack_lanes([log_total[h * count : (h + 1) * count] for h in range(HEADS)])
    oo[...] = out[:own]
    op[...] = out[own:].astype(BF)
    so[...] = packed[:own]
    sp[...] = packed[own:]


def forward_body(
    slot_rows,
    holding,
    oo,
    orecv,
    so,
    srecv,
    latent,
    cot,
    wo,
    wup,
    wdown,
    gain,
    bias,
    new_latents,
    act_out,
    pre_out,
    ffn_t,
    og_out,
    residual_grad,
    attended_grad,
    stats,
    output_grad,
    vectors,
    residual,
    ffn_in,
    acc,
    gacc,
    attended,
    packed,
):
    step = pl.program_id(0)
    count = latent.shape[0]
    slot = lax.broadcasted_iota(jnp.int32, (count, 1), 0) // slot_rows
    live = jnp.where(slot < holding[0, 0], 1.0, 0.0).astype(F32)

    @pl.when(step == 0)
    def _():
        a, b = so[...], srecv[...]
        top = jnp.maximum(a, b)
        both = top + jnp.log(jnp.exp(a - top) + jnp.exp(b - top))
        packed[...] = both
        mix = widen(jnp.exp(a - both)) * oo[...]
        mix += widen(jnp.exp(b - both)) * orecv[...].astype(F32)
        attended[...] = mix
        res = latent[...].astype(F32) + dot(mix.astype(BF), wo[...])
        residual[...] = res
        unit, _ = centred(res)
        low = (unit * gain[...] + bias[...]).astype(BF)
        ffn_in[...] = low
        ffn_t[...] = low.T
        og_out[...] = (cot[...].astype(F32) * live).astype(BF)
        acc[...] = jnp.zeros_like(acc)
        gacc[...] = jnp.zeros_like(gacc)

    pre = dot(ffn_in[...], wup[...])
    cdf = 0.5 * (1.0 + lax.erf(pre * (0.5**0.5)))
    act = (pre * cdf).astype(BF)
    act_out[...] = act
    acc[...] += dot(act, wdown[...])
    act_grad = dot_t(og_out[...], wdown[...])
    pdf = jnp.exp(-0.5 * pre * pre) * 0.3989422804014327
    pre_grad = (act_grad * (cdf + pre * pdf)).astype(BF)
    pre_out[...] = pre_grad
    gacc[...] += dot_t(pre_grad, wup[...])

    @pl.when(step == pl.num_programs(0) - 1)
    def _():
        res = residual[...]
        new_latents[...] = ((res + acc[...]) * live).astype(BF)
        unit, scale = centred(res)
        grad = gacc[...]
        vectors[0:1, :] = column_sum(grad * unit)
        vectors[1:2, :] = column_sum(grad)
        res_grad = og_out[...].astype(F32) + norm_back(unit, scale, gain[...], grad)
        residual_grad[...] = res_grad
        branch = res_grad.astype(BF)
        back = dot_t(branch, wo[...]).astype(BF)
        attended_grad[...] = back
        mix = attended[...]
        product = back.astype(F32) * mix
        head = head_of(product.shape)
        sums = [
            jnp.sum(jnp.where(head == h, product, 0.0), axis=-1, keepdims=True)
            for h in range(HEADS)
        ]
        delta = pack_lanes(sums)
        lane = lax.broadcasted_iota(jnp.int32, delta.shape, 1)
        stats[...] = jnp.where(lane % PER < PER // 2, packed[...], delta)
        output_grad[...] = t_dot(mix.astype(BF), branch).astype(BF)


def attend_back_body(qo, qp, kp, vp, kl, vl, do, dp, so, sp, dkvp, dkvl, dqo, dqp):
    own = qo.shape[0]
    patches = kp.shape[0]
    big = spread_rows(jnp.concatenate([qo[...], qp[...]], axis=0))
    back = spread_rows(jnp.concatenate([do[...], dp[...]], axis=0))
    keys = jnp.concatenate([kp[...], kl[...]], axis=0)
    values = jnp.concatenate([vp[...], vl[...]], axis=0)
    stats = jnp.concatenate([so[...], sp[...]], axis=0)
    probs = jnp.exp(dot_t(big, keys) - stack_heads(stats, 0))
    score_grad = (probs * (dot_t(back, values) - stack_heads(stats, PER // 2))).astype(BF)
    values_grad = t_dot(probs.astype(BF), back).astype(BF)
    keys_grad = t_dot(score_grad, big).astype(BF)
    dkvp[:, :INNER] = keys_grad[:patches]
    dkvp[:, INNER:] = values_grad[:patches]
    dkvl[:, :INNER] = keys_grad[patches:]
    dkvl[:, INNER:] = values_grad[patches:]
    dq = gather_rows(dot(score_grad, keys))
    dqo[...] = dq[:own]
    dqp[...] = dq[own:].astype(BF)


def up_grad_body(left, right, out):
    out[...] = dot(left[...], right[...]).astype(BF)


def down_grad_body(left, right, out):
    out[...] = t_dot(left[...], right[...]).astype(BF)


def kv_grad_body(media, latent, dkvp, dkvl, out):
    out[...] = (t_dot(media[...], dkvp[...]) + t_dot(latent[...], dkvl[...])).astype(BF)


def patch_back_body(patch, dkvp, wk, wv, gain, out, vectors):
    @pl.when(pl.program_id(0) == 0)
    def _():
        vectors[...] = jnp.zeros_like(vectors)

    grad = dot_t(dkvp[:, :INNER], wk[...]) + dot_t(dkvp[:, INNER:], wv[...])
    unit, scale = centred(patch[...].astype(F32))
    vectors[0:1, :] += column_sum(grad * unit)
    vectors[1:2, :] += column_sum(grad)
    out[...] = norm_back(unit, scale, gain[...], grad)


def latent_back_body(
    latent, norm, dkvl, dqo, drecv, residual_grad, wq, wk, wv, gain, out, query_grad, vectors
):
    dq = (dqo[...] + drecv[...].astype(F32)).astype(BF)
    product = (HEAD_DIM**-0.5 * t_dot(norm[...], dq)).astype(BF)
    if query_grad.shape == product.shape:
        query_grad[...] = product
    else:
        product = product.reshape(-1, 32, INNER)
        shape = query_grad.shape[:-1] + (INNER,)
        query_grad[..., :INNER] = product[:, :16].reshape(shape)
        query_grad[..., INNER:] = product[:, 16:].reshape(shape)
    grad = dot_t(dkvl[:, :INNER], wk[...]) + dot_t(dkvl[:, INNER:], wv[...])
    grad += HEAD_DIM**-0.5 * dot_t(dq, wq[...])
    unit, scale = centred(latent[...].astype(F32))
    vectors[0:1, :] = column_sum(grad * unit)
    vectors[1:2, :] = column_sum(grad)
    out[...] = residual_grad[...] + norm_back(unit, scale, gain[...], grad)


def ffn_back_body(
    residual, gacc, og, mix_ref, packed, wo, gain, residual_grad, attended_grad, stats, out, vectors
):
    unit, scale = centred(residual[...])
    grad = gacc[...]
    vectors[0:1, :] = column_sum(grad * unit)
    vectors[1:2, :] = column_sum(grad)
    res_grad = og[...].astype(F32) + norm_back(unit, scale, gain[...], grad)
    residual_grad[...] = res_grad
    branch = res_grad.astype(BF)
    back = dot_t(branch, wo[...]).astype(BF)
    attended_grad[...] = back
    mix = mix_ref[...]
    product = back.astype(F32) * mix
    head = head_of(product.shape)
    sums = [
        jnp.sum(jnp.where(head == h, product, 0.0), axis=-1, keepdims=True) for h in range(HEADS)
    ]
    delta = pack_lanes(sums)
    lane = lax.broadcasted_iota(jnp.int32, delta.shape, 1)
    stats[...] = jnp.where(lane % PER < PER // 2, packed[...], delta)
    if out is not None:
        out[...] = t_dot(mix.astype(BF), branch).astype(BF).reshape(out.shape)


def plus(a, b):
    return a.astype(F32) + b.astype(F32)


class Names:
    def __getattr__(self, name):
        return name


n = Names()
STREAMS = ("d0", "d1", "d2", "d3", "u0", "u1", "u2", "u3", "K", "W", "Q")
ORDERS = {
    "d0": "ywxz", "d1": "zwyx", "d2": "yxzw", "d3": "yxzw", "u0": "yzwx", "u1": "yxzw",
    "u2": "xyzw", "u3": "zxyw", "K": "wxyz", "W": "yzxw", "Q": "xywz",
}
PLAN = (
    "fi", "md0", "md1", "md2", "md3", "af0:4", "af4:8", "cb", "j0", "j1", "j2", "j3", "u0", "j4", "j5", "u1", "j6", "j7", "fb", "+u0", "u2", "d0",
    "d1", "d2", "d3", "+u0", "u3", "+u1", "at0:5", "+u0", "at5:7", "+d1", "at7:8", "+d0", "+u2",
    "kv0", "kv1", "kv2", "+u1", "kv3", "+u0", "ow", "+d2", "+K", "+u3", "+W", "+d1", "lat",
    "pt0", "+d2", "pt1", "+Q", "+d3", "pt2", "+d0", "+u3", "pt3", "+u1", "+u2", "+V", "+W",
    "+d2", "+K", "+d1", "+Q", "+u1", "+u3", "+u2", "+d2", "+d3", "+W", "+u3", "+Q", "+d0", "+V",
    "+u2", "+K", "+V", "+d3", "+d1", "+W", "+K", "+Q", "+d0", "+V", "+d3", "+W", "+K", "+V",
    "+Q",
)
DIMS = "wzyx"
DIMS_ALL = "wzycx"
BLOCK = (32, 1024)
LOADED = (n.latent, n.wq, n.og, n.patch, n.wo)
GIVEN = LOADED + (
    n.wk, n.wv, n.wup, n.wdown, n.images, n.device, n.fg, n.fb, n.mg, n.mb, n.lg, n.lb,
)


def is_late(s):
    return s in "KWQ"


def main_scratch(nl, np_, width, hidden):
    def bf(*shape):
        return pltpu.VMEM(shape, BF)

    def f4(*shape):
        return pltpu.VMEM(shape, F32)

    step = hidden // 8
    turned = (2, 2, 2, 2, step // 4, nl)
    turned_in = (2, 2, 2, 2, 32, nl)
    items = [
        (n.latent, bf(nl, width)),
        (n.wq, bf(width, INNER)),
        (n.og, bf(nl, width)),
        (n.patch, bf(np_, width)),
        (n.wo, bf(INNER, width)),
        (n.oo, f4(nl, INNER)),
        (n.op, bf(nl, INNER)),
        (n.so, f4(nl, LANES)),
        (n.sp, f4(nl, LANES)),
        (n.orecv, bf(nl, INNER)),
        (n.srecv, f4(nl, LANES)),
        (n.q, bf(nl, INNER)),
        (n.q_peer, bf(nl, INNER)),
        (n.kp, bf(np_, INNER)),
        (n.vp, bf(np_, INNER)),
        (n.kl, bf(nl, INNER)),
        (n.vl, bf(nl, INNER)),
        (n.norm_l, bf(nl, width)),
        (n.norm_m, bf(np_, width)),
        (n.wu, bf(2, width, step)),
        (n.wd, bf(2, step, width)),
        (n.og_sib, bf(nl, width)),
        (n.act_own, bf(*turned)),
        (n.act_send, bf(*turned)),
        (n.act_sib, bf(*turned)),
        (n.ffn_own, bf(*turned_in)),
        (n.ffn_send, bf(*turned_in)),
        (n.ffn_sib, bf(*turned_in)),
        (n.residual, f4(nl, width)),
        (n.gacc, f4(nl, width)),
        (n.acc, f4(nl, width)),
        (n.ffn_in, bf(nl, width)),
        (n.attended, f4(nl, INNER)),
        (n.packed, f4(nl, LANES)),
        (n.fresh, bf(nl, width)),
        (n.grad, bf(nl, INNER)),
        (n.stats, f4(nl, LANES)),
        (n.grad_peer, bf(nl, INNER)),
        (n.stats_peer, f4(nl, LANES)),
        (n.dkvp, bf(np_, 2 * INNER)),
        (n.dkvl, bf(nl, 2 * INNER)),
        (n.dq_peer, bf(nl, INNER)),
        (n.vs, f4(5, 8, width)),
        (n.vr, f4(5, 8, width)),
        (n.sums, f4(2, width)),
        (n.pre, bf(2, 2, 2, 2, 2, *BLOCK)),
        (n.pre_sib, bf(2, 2, 2, 2, 2, *BLOCK)),
    ]
    items += [(s, bf(2, 2, 2, 2, *BLOCK)) for s in STREAMS if not is_late(s)]
    for s in STREAMS:
        wide = BLOCK[1] // 2 if s in "KW" else BLOCK[1]
        for k in range(4 if is_late(s) else 3, -1, -1):
            items.append((s + "_%d" % k, bf(*((2,) * k), BLOCK[0], wide)))
    dma = pltpu.SemaphoreType.DMA
    items += [
        (n.load_sem, dma((len(LOADED) + 4,))),
        (n.weight_sem, dma((2, 2))),
        (n.store_sem, dma((6,))),
        (n.send_sem, dma((80,))),
        (n.recv_sem, dma((80,))),
    ]
    return [k for k, _ in items], [v for _, v in items]


def main_body(names, *refs):
    src = SimpleNamespace(**dict(zip(GIVEN, refs)))
    outs = len(GIVEN)
    fin, vec, patches_low, latents_grad, new_latents = refs[outs : outs + 5]
    t = SimpleNamespace(**dict(zip(names, refs[outs + 5 :])))
    load_sem, weight_sem, store_sem = t.load_sem, t.weight_sem, t.store_sem
    mine = lax.axis_index("img")
    xb = lax.axis_index("lat")
    bit = {"x": xb, "c": mine % 2, "y": (mine // 2) % 2, "z": (mine // 4) % 2, "w": (mine // 8) % 2}

    def to(axis, weight):
        return (mine + weight - 2 * weight * bit[axis], xb)

    peer = {"c": to("c", 1), "y": to("y", 2), "z": to("z", 4), "w": to("w", 8), "x": (mine, 1 - xb)}
    barrier = pltpu.get_barrier_semaphore()
    for axis in peer:
        pl.semaphore_signal(
            barrier, inc=1, device_id=peer[axis], device_id_type=pl.DeviceIdType.MESH
        )

    step = t.wd.shape[1]
    count = t.og.shape[0]
    weights = {}

    def load_weights(j):
        slot = j % 2
        col = pl.ds(j * step, step)
        pair = (
            pltpu.make_async_copy(src.wup.at[:, col], t.wu.at[slot], weight_sem.at[0, slot]),
            pltpu.make_async_copy(src.wdown.at[col], t.wd.at[slot], weight_sem.at[1, slot]),
        )
        for copy in pair:
            copy.start()
        weights[j] = pair

    loads = {}

    def load(names):
        for name in names:
            i = LOADED.index(name)
            loads[name] = pltpu.make_async_copy(getattr(src, name), getattr(t, name), load_sem.at[i])
            loads[name].start()

    def load_kv(first):
        for i, name in enumerate((n.wk, n.wv)):
            loads[name] = pltpu.make_async_copy(
                getattr(src, name), t.wu.at[i], load_sem.at[len(LOADED) + first + i]
            )
            loads[name].start()

    load(LOADED[:3])
    load_kv(0)
    load(LOADED[3:])

    def need(*names):
        for name in names:
            if name in loads:
                loads.pop(name).wait()

    pl.semaphore_wait(barrier, len(peer))
    used = []

    def send(source, target, axis):
        slot = len(used)
        copy = pltpu.make_async_remote_copy(
            src_ref=source,
            dst_ref=target,
            send_sem=t.send_sem.at[slot],
            recv_sem=t.recv_sem.at[slot],
            device_id=peer[axis],
            device_id_type=pl.DeviceIdType.MESH,
        )
        copy.start()
        used.append(copy)
        return copy

    arriving = {}

    def arrive(*names):
        for name in names:
            if name in arriving:
                arriving.pop(name).wait_recv()

    order = {s: ("c" if is_late(s) else "") + ORDERS[s] for s in STREAMS}
    place = {s: 0 for s in STREAMS}
    half = BLOCK[1] // 2
    buffer = {s: getattr(t, s) for s in STREAMS if not is_late(s)}
    buffer["K"] = buffer["W"] = t.pre
    buffer["Q"] = t.pre_sib
    column = {"K": pl.ds(0, half), "W": pl.ds(half, half)}

    def where(s, axis, value):
        done = order[s][: place[s]]
        index = []
        for d in DIMS_ALL if is_late(s) else DIMS:
            if d == axis:
                index.append(value)
            else:
                index.append(bit[d] if d in done else slice(None))
        if s in column:
            index += [slice(None), column[s]]
        return tuple(index)

    def got(s):
        return getattr(t, s + "_%d" % (len(order[s]) - 1 - place[s]))

    def start(s):
        axis = order[s][place[s]]
        arriving[s] = send(buffer[s].at[where(s, axis, 1 - bit[axis])], got(s), axis)

    def take(s):
        axis = order[s][place[s]]
        arrive(s)
        if s == "Q" and place[s] == 0:
            arrive(n.O)
        at = where(s, axis, bit[axis])
        total = plus(buffer[s][at], got(s)[...])
        place[s] += 1
        if place[s] < len(order[s]):
            buffer[s][at] = total.astype(BF)
            start(s)
        elif s in column:
            fin[8, :, column[s]] = total
        else:
            fin[9 if s == "Q" else STREAMS.index(s)] = total

    vs, vr = t.vs, t.vr
    vec_order = "cxyzw"
    vec_place = [0]

    def take_vector():
        i = vec_place[0]
        arrive(n.V)
        if i < 4:
            vs[i + 1] = vs[i] + vr[i]
            arriving["V"] = send(vs.at[i + 1], vr.at[i + 1], vec_order[i + 1])
        else:
            vec[...] = vs[i] + vr[i]
        vec_place[0] += 1

    stores = []

    def store(source, target):
        stores.append(pltpu.make_async_copy(source, target, store_sem.at[len(stores)]))
        stores[-1].start()

    core = bit["c"]
    size = t.patch.shape[0] // 4

    def live_rows():
        total = jnp.int32(0)
        for i in range(src.images.shape[0]):
            total += jnp.where(src.device[i] == mine, src.images[i], 0)
        slot = lax.broadcasted_iota(jnp.int32, (count, 1), 0) // (count // 8)
        return jnp.where(slot < total, 1.0, 0.0).astype(F32)

    def first():
        need(n.latent, n.wq)
        unit, _ = centred(t.latent[...].astype(F32))
        low = (unit * src.lg[...] + src.lb[...]).astype(BF)
        t.norm_l[...] = low
        t.q[...] = (HEAD_DIM**-0.5 * dot(low, t.wq[...])).astype(BF)
        arriving[n.q_peer] = send(t.q, t.q_peer, "x")
        need(n.og, n.wk, n.wv)
        t.og[...] = (t.og[...].astype(F32) * live_rows()).astype(BF)
        arriving[n.og_sib] = send(t.og, t.og_sib, "c")
        t.kl[...] = dot(low, t.wu[0]).astype(BF)
        t.vl[...] = dot(low, t.wu[1]).astype(BF)

    def media(i):
        need(n.patch)
        at = pl.ds(i * size, size)
        unit, _ = centred(t.patch[at].astype(F32))
        low = (unit * src.mg[...] + src.mb[...]).astype(BF)
        t.norm_m[at] = low
        t.kp[at] = dot(low, t.wu[0]).astype(BF)
        t.vp[at] = dot(low, t.wu[1]).astype(BF)
        if i == 3:
            load_weights(0)
            load_weights(1)

    def slot_rows(i):
        lat, med = count // 8, t.kp.shape[0] // 8
        return (
            pl.ds(pl.multiple_of(i * lat, lat), lat),
            pl.ds(pl.multiple_of(i * med, med), med),
        )

    def attend(first, last):
        arrive(n.q_peer)

        @pl.loop(first, last)
        def _(i):
            a, b = slot_rows(i)
            attend_body(
                t.q.at[a], t.q_peer.at[a], t.kp.at[b], t.vp.at[b], t.kl.at[a], t.vl.at[a],
                t.oo.at[a], t.op.at[a], t.so.at[a], t.sp.at[a],
            )

        at = pl.ds(first * (count // 8), (last - first) * (count // 8))
        arriving["o%d" % first] = send(t.op.at[at], t.orecv.at[at], "x")
        arriving["s%d" % first] = send(t.sp.at[at], t.srecv.at[at], "x")

    def combine():
        need(n.wo)
        for name in list(arriving):
            if name[0] in "os" and name[1:].isdigit():
                arrive(name)
        a, b = t.so[...], t.srecv[...]
        top = jnp.maximum(a, b)
        both = top + jnp.log(jnp.exp(a - top) + jnp.exp(b - top))
        t.packed[...] = both
        mix = widen(jnp.exp(a - both)) * t.oo[...]
        mix += widen(jnp.exp(b - both)) * t.orecv[...].astype(F32)
        t.attended[...] = mix
        res = t.latent[...].astype(F32) + dot(mix.astype(BF), t.wo[...])
        t.residual[...] = res
        unit, _ = centred(res)
        low = (unit * src.fg[...] + src.fb[...]).astype(BF)
        t.ffn_in[...] = low
        turned = low.T.reshape(8, 2, -1, count)
        even, odd = turned[:, 0], turned[:, 1]
        shape = t.ffn_own.shape
        t.ffn_own[...] = jnp.where(core == 0, even, odd).reshape(shape)
        t.ffn_send[...] = jnp.where(core == 0, odd, even).reshape(shape)
        arriving[n.ffn_sib] = send(t.ffn_send, t.ffn_sib, "c")

    def ffn(j):
        for copy in weights.pop(j):
            copy.wait()
        wup, wdown = t.wu[j % 2], t.wd[j % 2]
        pre = dot(t.ffn_in[...], wup)
        cdf = 0.5 * (1.0 + lax.erf(pre * (0.5**0.5)))
        act = (pre * cdf).astype(BF)
        turned = act.T
        even, odd = turned[: step // 2], turned[step // 2 :]
        at = (j // 4, (j // 2) % 2, j % 2)
        shape = t.act_own.shape[3:]
        t.act_own[at] = jnp.where(core == 0, even, odd).reshape(shape)
        t.act_send[at] = jnp.where(core == 0, odd, even).reshape(shape)
        arriving["act%d" % j] = send(t.act_send.at[at], t.act_sib.at[at], "c")
        down = dot(act, wdown)
        act_grad = dot_t(t.og[...], wdown)
        pdf = jnp.exp(-0.5 * pre * pre) * 0.3989422804014327
        pre_grad = (act_grad * (cdf + pre * pdf)).astype(BF)
        group = (j // 4, (j // 2) % 2)
        t.pre[group + (slice(None),) * 4 + (pl.ds((j % 2) * step, step),)] = pre_grad.reshape(
            2, 2, 2, 32, step
        )
        if j % 2 == 1:
            name = "pre%d" % (j // 2)
            arriving[name] = send(t.pre.at[group], t.pre_sib.at[group], "c")
            pre_sent.append(len(used) - 1)
        back = dot_t(pre_grad, wup)
        if j == 0:
            t.acc[...] = down
            t.gacc[...] = back
        else:
            t.acc[...] += down
            t.gacc[...] += back
        if j < 6:
            load_weights(j + 2)
        if j == 7:
            load_kv(2)
            t.fresh[...] = ((t.residual[...] + t.acc[...]) * live_rows()).astype(BF)
            store(t.fresh, new_latents)

    pre_sent = []

    def ffn_back():
        ffn_back_body(
            t.residual, t.gacc, t.og, t.attended, t.packed, t.wo, src.fg,
            t.residual, t.grad, t.stats, None, vs.at[0, pl.ds(4, 2)],
        )
        arriving[n.grad_peer] = send(t.grad, t.grad_peer, "x")
        arriving[n.stats_peer] = send(t.stats, t.stats_peer, "x")

    def send_late(rows, name):
        o, r = buffer["Q"], t.Q_4
        arriving[name] = send(
            o.at[:, :, :, 1 - core, :, rows], r.at[:, :, :, :, rows], "c"
        )

    def output_group():
        product = t_dot(t.attended[...].astype(BF), t.residual[...].astype(BF)).astype(BF)
        buffer["Q"][..., pl.ds(0, 16), :] = product.reshape(2, 2, 2, 2, 2, 16, BLOCK[1])
        send_late(pl.ds(0, 16), "O")

    def rows_of(ref, at):
        v = ref[at]
        return v.reshape(-1, v.shape[-1])

    def down_group(g):
        s = "d%d" % g
        arrive(n.og_sib, *("act%d" % j for j in range(8)))
        axis = order[s][0]
        col = pl.ds(g * 256, 256)
        for value in (1 - bit[axis], bit[axis]):
            at = where(s, axis, value)
            v = dot(rows_of(t.act_own, at), t.og[:, col])
            v += dot(rows_of(t.act_sib, at), t.og_sib[:, col])
            v = v.astype(BF).reshape(2, 2, 2, 4, 32, 256)
            for k in range(4):
                buffer[s][at + (slice(None), pl.ds(k * 256, 256))] = v[:, :, :, k]
            if s not in arriving:
                start(s)

    def up_group(g):
        s = "u%d" % g
        arrive(n.ffn_sib, "pre%d" % g)
        axis = order[s][0]
        group = (g // 2, g % 2)
        for value in (1 - bit[axis], bit[axis]):
            at = where(s, axis, value)
            v = dot(rows_of(t.ffn_own, at), rows_of(t.pre, group))
            v += dot(rows_of(t.ffn_sib, at), rows_of(t.pre_sib, group))
            buffer[s][at] = v.astype(BF).reshape((2, 2, 2) + BLOCK)
            if s not in arriving:
                start(s)

    def attend_back(first, last):
        arrive(n.grad_peer, n.stats_peer)

        @pl.loop(first, last)
        def _(i):
            a, b = slot_rows(i)
            attend_back_body(
                t.q.at[a], t.q_peer.at[a], t.kp.at[b], t.vp.at[b], t.kl.at[a],
                t.vl.at[a], t.grad.at[a], t.grad_peer.at[a], t.stats.at[a],
                t.stats_peer.at[a], t.dkvp.at[b], t.dkvl.at[a], t.oo.at[a],
                t.dq_peer.at[a],
            )

        if last == 8:
            arriving[n.dq_recv] = send(t.dq_peer, t.orecv, "x")

    def kv_group(g):
        while pre_sent:
            slot = pre_sent.pop()
            used[slot].wait_send()
            used[slot] = None
        col = pl.ds(g * 256, 256)
        v = t_dot(t.norm_m[...], t.dkvp[:, col])
        v += t_dot(t.norm_l[...], t.dkvl[:, col])
        buffer["K"][..., col] = v.astype(BF).reshape(2, 2, 2, 2, 2, 32, 256)
        if g == 1:
            start("K")
        if g == 3:
            start("W")

    def latent_back():
        need(n.wk, n.wv)
        arrive(n.dq_recv)
        latent_back_body(
            t.latent, t.norm_l, t.dkvl, t.oo, t.orecv, t.residual,
            t.wq, t.wu.at[0], t.wu.at[1], src.lg, t.residual,
            buffer["Q"].at[..., pl.ds(16, 16), :], vs.at[0, pl.ds(2, 2)],
        )
        send_late(pl.ds(16, 16), "Q")
        t.ffn_in[...] = t.residual[...].astype(BF)
        store(t.ffn_in, latents_grad)

    def patch_back(i):
        need(n.wk, n.wv)
        at = pl.ds(i * size, size)
        dkv = t.dkvp
        grad = dot_t(dkv[at, :INNER], t.wu[0]) + dot_t(dkv[at, INNER:], t.wu[1])
        unit, scale = centred(t.patch[at].astype(F32))
        sums = t.sums
        a, b = column_sum(grad * unit), column_sum(grad)
        if i > 0:
            a, b = a + sums[0:1, :], b + sums[1:2, :]
        sums[0:1, :] = a
        sums[1:2, :] = b
        dkv[at] = norm_back(unit, scale, src.mg[...], grad).astype(BF)
        store(dkv.at[at], patches_low.at[at])
        if i == 3:
            vs[0, 0:2, :] = sums[...]
            vs[0, 6:8, :] = jnp.zeros((2, vs.shape[2]), F32)
            arriving["V"] = send(vs.at[0], vr.at[0], vec_order[0])

    simple = {"fi": first, "cb": combine, "fb": ffn_back, "ow": output_group, "lat": latent_back}
    simple["+V"] = take_vector
    for item in PLAN:
        if item in simple:
            simple[item]()
        elif item[0] == "+":
            take(item[1:])
        elif item[:2] == "at":
            a, b = item[2:].split(":")
            attend_back(int(a), int(b))
        elif item[:2] == "af":
            a, b = item[2:].split(":")
            attend(int(a), int(b))
        elif item[:2] == "md":
            media(int(item[2:]))
        elif item[:2] == "kv":
            kv_group(int(item[2:]))
        elif item[:2] == "pt":
            patch_back(int(item[2:]))
        else:
            {"j": ffn, "d": down_group, "u": up_group}[item[0]](int(item[1:]))
    for copy in stores:
        copy.wait()
    for copy in used:
        if copy is not None:
            copy.wait_send()


def last_body(
    patches_in, fresh, latents_in, fin, vec,
    patches_grad, new_latents, latents_grad, up, down, key, value, out, query, *thin,
):
    patches_grad[...] = patches_in[...].astype(F32)
    new_latents[...] = fresh[...]
    latents_grad[...] = latents_in[...].astype(F32)

    @pl.when(pl.program_id(0) == 0)
    def _():
        for g in range(4):
            up[:, g * 1024 : (g + 1) * 1024] = fin[4 + g]
            for k in range(4):
                down[k * 32 : (k + 1) * 32, g * 256 : (g + 1) * 256] = fin[
                    g, :, k * 256 : (k + 1) * 256
                ]
        key[...] = fin[8, :, :INNER]
        value[...] = fin[8, :, INNER:]
        out[...] = fin[9, 0:16]
        query[0:16] = fin[9, 16:32, :INNER]
        query[16:32] = fin[9, 16:32, INNER:]
        place = lax.axis_index("img") * 2 + lax.axis_index("lat")
        width = vec.shape[1]
        turned = pltpu.roll(vec[...], width - place * 32, 1)
        for i, ref in enumerate(thin):
            ref[...] = turned[i : i + 1, :32]


def swap_lat(v):
    return lax.ppermute(v, "lat", [(0, 1), (1, 0)])


def halving_sum(v, order, bits, count, keep):
    left = list(range(bits - 1, -1, -1)) + [-1]
    mine = lax.axis_index("img")
    for place, axis in enumerate(order):
        dim = left.index(axis)
        if axis < 0:
            bit = lax.axis_index("lat")
            pairs, name = [(0, 1), (1, 0)], "lat"
        else:
            bit = (mine // 2**axis) % 2
            pairs, name = [(i, i ^ 2**axis) for i in range(count)], "img"
        out = lax.dynamic_index_in_dim(v, 1 - bit, dim, keepdims=False)
        stay = lax.dynamic_index_in_dim(v, bit, dim, keepdims=False)
        got = lax.ppermute(out, name, pairs)
        v = stay.astype(F32) + got.astype(F32)
        if place < len(order) - 1 and keep == BF:
            v = v.astype(BF)
        left.pop(dim)
    return v


def local(
    count,
    patches,
    latents,
    cotangent,
    doc_images,
    doc_device,
    query_weight,
    key_weight,
    value_weight,
    output_weight,
    up_weight,
    down_weight,
    media_gain,
    media_bias,
    latent_gain,
    latent_bias,
    ffn_gain,
    ffn_bias,
):
    slots, own_patches, width = patches.shape
    own_latents = latents.shape[1]
    hidden = up_weight.shape[1]
    np_, nl = slots * own_patches, slots * own_latents
    mine = lax.axis_index("img")
    holding = jnp.sum(jnp.where(doc_device == mine, doc_images, 0)).reshape(1, 1)
    patch = patches.reshape(np_, width)
    latent = latents.reshape(nl, width)
    cot = cotangent.reshape(nl, width)
    mg, mb = media_gain.reshape(1, width), media_bias.reshape(1, width)
    lg, lb = latent_gain.reshape(1, width), latent_bias.reshape(1, width)
    fg, fb = ffn_gain.reshape(1, width), ffn_bias.reshape(1, width)
    wspec = whole((width, INNER))
    vspec = whole((1, width))
    lspec = whole((nl, width))

    norm_l, query = call(
        latent_body,
        (1,),
        [lspec, vspec, vspec, wspec],
        [(struct((nl, width), BF), lspec), (struct((nl, INNER), BF), whole((nl, INNER)))],
        (latent, lg, lb, query_weight),
        2 * nl * width * INNER,
    )
    query_peer = swap_lat(query)
    blk = min(np_, 256)
    norm_m, kp, vp, kl, vl = call(
        media_body,
        (np_ // blk,),
        [rows(blk, width), vspec, vspec, wspec, wspec, lspec],
        [
            (struct((np_, width), BF), rows(blk, width)),
            (struct((np_, INNER), BF), rows(blk, INNER)),
            (struct((np_, INNER), BF), rows(blk, INNER)),
            (struct((nl, INNER), BF), whole((nl, INNER))),
            (struct((nl, INNER), BF), whole((nl, INNER))),
        ],
        (patch, mg, mb, key_weight, value_weight, norm_l),
        4 * (np_ + nl) * width * INNER,
    )
    q_s, p_s, s_s = rows(own_latents, INNER), rows(own_patches, INNER), rows(own_latents, LANES)
    att_flops = 4 * slots * (own_patches + own_latents) * INNER * INNER
    o_own, o_peer, s_own, s_peer = call(
        attend_body,
        (slots,),
        [q_s, q_s, p_s, p_s, q_s, q_s],
        [
            (struct((nl, INNER), F32), q_s),
            (struct((nl, INNER), BF), q_s),
            (struct((nl, LANES), F32), s_s),
            (struct((nl, LANES), F32), s_s),
        ],
        (query, query_peer, kp, vp, kl, vl),
        att_flops,
    )
    o_recv, s_recv = swap_lat(o_peer), swap_lat(s_peer)
    fblk = min(hidden, 512)
    nspec = whole((nl, INNER))
    (
        new_latents,
        act,
        pre_grad,
        ffn_t,
        out_grad,
        residual_grad,
        attended_grad,
        stats,
        output_grad,
        ffn_vec,
    ) = call(
        partial(forward_body, own_latents),
        (hidden // fblk,),
        [
            pl.BlockSpec(memory_space=pltpu.SMEM),
            nspec,
            nspec,
            whole((nl, LANES)),
            whole((nl, LANES)),
            lspec,
            lspec,
            whole((INNER, width)),
            cols(width, fblk),
            rows(fblk, width),
            vspec,
            vspec,
        ],
        [
            (struct((nl, width), BF), lspec),
            (struct((nl, hidden), BF), cols(nl, fblk)),
            (struct((nl, hidden), BF), cols(nl, fblk)),
            (struct((width, nl), BF), whole((width, nl))),
            (struct((nl, width), BF), lspec),
            (struct((nl, width), F32), lspec),
            (struct((nl, INNER), BF), nspec),
            (struct((nl, LANES), F32), whole((nl, LANES))),
            (struct((INNER, width), BF), whole((INNER, width))),
            (struct((2, width), F32), whole((2, width))),
        ],
        (
            holding,
            o_own,
            o_recv,
            s_own,
            s_recv,
            latent,
            cot,
            output_weight,
            up_weight,
            down_weight,
            fg,
            fb,
        ),
        8 * nl * width * hidden,
        scratch=[
            pltpu.VMEM((nl, width), F32),
            pltpu.VMEM((nl, width), BF),
            pltpu.VMEM((nl, width), F32),
            pltpu.VMEM((nl, width), F32),
            pltpu.VMEM((nl, INNER), F32),
            pltpu.VMEM((nl, LANES), F32),
        ],
    )
    grad_peer, stats_peer = swap_lat(attended_grad), swap_lat(stats)
    (down_grad,) = call(
        down_grad_body,
        (hidden // fblk,),
        [cols(nl, fblk), lspec],
        [(struct((hidden, width), BF), rows(fblk, width))],
        (act, out_grad),
        2 * nl * width * hidden,
    )
    (up_grad,) = call(
        up_grad_body,
        (hidden // fblk,),
        [whole((width, nl)), cols(nl, fblk)],
        [(struct((width, hidden), BF), cols(width, fblk))],
        (ffn_t, pre_grad),
        2 * nl * width * hidden,
    )
    dkvp, dkvl, dq_own, dq_peer = call(
        attend_back_body,
        (slots,),
        [q_s, q_s, p_s, p_s, q_s, q_s, q_s, q_s, s_s, s_s],
        [
            (struct((np_, 2 * INNER), BF), rows(own_patches, 2 * INNER)),
            (struct((nl, 2 * INNER), BF), rows(own_latents, 2 * INNER)),
            (struct((nl, INNER), F32), q_s),
            (struct((nl, INNER), BF), q_s),
        ],
        (query, query_peer, kp, vp, kl, vl, attended_grad, grad_peer, stats, stats_peer),
        att_flops * 5 // 2,
    )
    dq_recv = swap_lat(dq_peer)
    kblk = 256
    (kv_grad,) = call(
        kv_grad_body,
        (2 * INNER // kblk,),
        [whole((np_, width)), lspec, cols(np_, kblk), cols(nl, kblk)],
        [(struct((width, 2 * INNER), BF), cols(width, kblk))],
        (norm_m, norm_l, dkvp, dkvl),
        4 * (np_ + nl) * width * INNER,
    )
    patches_grad, media_vec = call(
        patch_back_body,
        (np_ // blk,),
        [rows(blk, width), rows(blk, 2 * INNER), wspec, wspec, vspec],
        [(struct((np_, width), F32), rows(blk, width)), (struct((2, width), F32), whole((2, width)))],
        (patch, dkvp, key_weight, value_weight, mg),
        4 * np_ * width * INNER,
    )
    latents_grad, query_grad, latent_vec = call(
        latent_back_body,
        (1,),
        [
            lspec,
            lspec,
            whole((nl, 2 * INNER)),
            nspec,
            nspec,
            lspec,
            wspec,
            wspec,
            wspec,
            vspec,
        ],
        [
            (struct((nl, width), F32), lspec),
            (struct((width, INNER), BF), wspec),
            (struct((2, width), F32), whole((2, width))),
        ],
        (
            latent,
            norm_l,
            dkvl,
            dq_own,
            dq_recv,
            residual_grad,
            query_weight,
            key_weight,
            value_weight,
            lg,
        ),
        8 * nl * width * INNER,
    )

    bits = count.bit_length() - 1
    first = list(range(1, bits))
    orders = (
        [0, -1] + first,
        [0] + first + [-1],
        [0] + first[1:] + [-1] + first[:1],
    )

    def reduce(v, order, keep=BF):
        shape = (2,) * (bits + 1) + (v.shape[0] // (2 * count),) + v.shape[1:]
        return halving_sum(v.reshape(shape), order, bits, count, keep)

    def reduce_parts(v):
        unit = v.shape[1] // 8
        cuts = (0, 3 * unit, 6 * unit, 8 * unit)
        return jnp.concatenate(
            [reduce(v[:, a:b], order) for a, b, order in zip(cuts, cuts[1:], orders)], axis=1
        )

    down_sum = reduce_parts(down_grad)
    up_sum = reduce_parts(up_grad)
    output_sum = reduce(output_grad, orders[1])
    kv_sum = reduce_parts(kv_grad)
    query_sum = reduce(query_grad, orders[0])
    vec = jnp.concatenate([media_vec, latent_vec, ffn_vec], axis=0)
    vec = vec.reshape(6, 2 * count, width // (2 * count)).transpose(1, 0, 2)
    vec_sum = reduce(vec, orders[2], F32)[0]
    return (
        new_latents.reshape(latents.shape),
        patches_grad.reshape(patches.shape),
        latents_grad.reshape(latents.shape),
        query_sum,
        kv_sum[:, :INNER],
        kv_sum[:, INNER:],
        output_sum,
        up_sum,
        down_sum,
        vec_sum[0],
        vec_sum[1],
        vec_sum[2],
        vec_sum[3],
        vec_sum[4],
        vec_sum[5],
    )


def fits(mesh):
    return mesh.shape["img"] == 16 and mesh.shape["lat"] == 2


def quick(
    count,
    patches,
    latents,
    cotangent,
    doc_images,
    doc_device,
    query_weight,
    key_weight,
    value_weight,
    output_weight,
    up_weight,
    down_weight,
    media_gain,
    media_bias,
    latent_gain,
    latent_bias,
    ffn_gain,
    ffn_bias,
):
    slots, own_patches, width = patches.shape
    own_latents = latents.shape[1]
    hidden = up_weight.shape[1]
    np_, nl = slots * own_patches, slots * own_latents
    patch = patches.reshape(np_, width)
    latent = latents.reshape(nl, width)
    cot = cotangent.reshape(nl, width)
    mg, mb = media_gain.reshape(1, width), media_bias.reshape(1, width)
    lg, lb = latent_gain.reshape(1, width), latent_bias.reshape(1, width)
    fg, fb = ffn_gain.reshape(1, width), ffn_bias.reshape(1, width)
    sspec = pl.BlockSpec(memory_space=pltpu.SMEM)
    vmem = pl.BlockSpec(memory_space=pltpu.VMEM)
    hbm = pl.BlockSpec(memory_space=pl.ANY)
    names, scratch = main_scratch(nl, np_, width, hidden)
    given = (
        latent, query_weight, cot, patch, output_weight, key_weight, value_weight, up_weight,
        down_weight, doc_images, doc_device, fg, fb, mg, mb, lg, lb,
    )
    fin, vec, patches_low, latents_low, new_latents = pl.pallas_call(
        partial(main_body, names),
        in_specs=[hbm] * 9 + [sspec] * 2 + [vmem] * 6,
        out_specs=[vmem, vmem, hbm, hbm, hbm],
        out_shape=[
            struct((10,) + BLOCK, F32),
            struct((8, width), F32),
            struct((np_, width), BF),
            struct((nl, width), BF),
            struct((nl, width), BF),
        ],
        scratch_shapes=scratch,
        compiler_params=pltpu.CompilerParams(
            collective_id=0, has_side_effects=True, vmem_limit_bytes=60 * 1024 * 1024
        ),
    )(*given)
    d = 2 * count
    small = [
        (width // d, hidden),
        (hidden // d, width),
        (width // d, INNER),
        (width // d, INNER),
        (INNER // d, width),
        (width // d, INNER),
    ] + [(1, width // d)] * 6
    parts = 8
    piece, long = rows(nl // parts, width), rows(np_ // parts, width)
    patches_grad, fresh, latents_out, up_sum, down_sum, key_sum, value_sum, out_sum, query_sum, *thin = call(
        last_body,
        (parts,),
        [long, piece, piece, whole((10,) + BLOCK), whole((8, width))],
        [
            (struct((np_, width), F32), long),
            (struct((nl, width), BF), piece),
            (struct((nl, width), F32), piece),
        ]
        + [(struct(shape, F32), whole(shape)) for shape in small],
        (patches_low, new_latents, latents_low, fin, vec),
        0,
    )
    return (
        fresh.reshape(latents.shape),
        patches_grad.reshape(patches.shape),
        latents_out.reshape(latents.shape),
        query_sum,
        key_sum,
        value_sum,
        out_sum,
        up_sum,
        down_sum,
    ) + tuple(v.reshape(-1) for v in thin)


def solution(mesh):
    split = P("img", "lat", None)
    both = P(("img", "lat"), None)
    line = P(("img", "lat"))
    return jax.shard_map(
        partial(quick if fits(mesh) else local, mesh.shape["img"]),
        mesh=mesh,
        in_specs=(split,) * 3 + (P(),) * 14,
        out_specs=(split,) * 3 + (both,) * 6 + (line,) * 6,
        check_vma=False,
    )
```

```python
from functools import partial
from types import SimpleNamespace

import jax
import jax.numpy as jnp
from jax import lax
from jax.experimental import pallas as pl
from jax.experimental.pallas import tpu as pltpu
from jax.sharding import PartitionSpec as P

HEADS = 8
HEAD_DIM = 64
INNER = HEADS * HEAD_DIM
LANES = 128
PER = LANES // HEADS
EPS = 1e-05
BF = jnp.bfloat16
F32 = jnp.float32
VMEM_LIMIT = 56 * 1024 * 1024


def dot(a, b):
    return lax.dot_general(a, b, (((1,), (0,)), ((), ())), preferred_element_type=F32)


def dot_t(a, b):
    return lax.dot_general(a, b, (((1,), (1,)), ((), ())), preferred_element_type=F32)


def t_dot(a, b):
    return lax.dot_general(a, b, (((0,), (0,)), ((), ())), preferred_element_type=F32)


def call(body, grid, ins, outs, args, flops, scratch=()):
    moved = sum(a.size * a.dtype.itemsize for a in args)
    moved += sum(o[0].size * o[0].dtype.itemsize for o in outs)
    return pl.pallas_call(
        body,
        grid=grid,
        in_specs=ins,
        out_specs=[o[1] for o in outs],
        out_shape=[o[0] for o in outs],
        scratch_shapes=list(scratch),
        compiler_params=pltpu.CompilerParams(
            dimension_semantics=("arbitrary",) * len(grid), vmem_limit_bytes=VMEM_LIMIT
        ),
        cost_estimate=pl.CostEstimate(flops=flops, bytes_accessed=moved, transcendentals=0),
    )(*args)


def whole(shape):
    return pl.BlockSpec(shape, lambda *_: (0,) * len(shape))


def rows(block, width):
    return pl.BlockSpec((block, width), lambda i: (i, 0))


def cols(height, block):
    return pl.BlockSpec((height, block), lambda i: (0, i))


def struct(shape, dtype):
    return jax.ShapeDtypeStruct(shape, dtype)


def centred(v):
    centre = v - jnp.mean(v, axis=-1, keepdims=True)
    scale = lax.rsqrt(jnp.mean(centre * centre, axis=-1, keepdims=True) + EPS)
    return centre * scale, scale


def norm_back(unit, scale, gain, grad):
    push = grad * gain
    mean_push = jnp.mean(push, axis=-1, keepdims=True)
    mean_both = jnp.mean(push * unit, axis=-1, keepdims=True)
    return scale * (push - mean_push - unit * mean_both)


def column_sum(v):
    return jnp.sum(v, axis=0, keepdims=True)


def latent_body(latent, gain, bias, wq, norm, query):
    unit, _ = centred(latent[...].astype(F32))
    low = (unit * gain[...] + bias[...]).astype(BF)
    norm[...] = low
    query[...] = (HEAD_DIM**-0.5 * dot(low, wq[...])).astype(BF)


def media_body(patch, gain, bias, wk, wv, latent_norm, norm, kp, vp, kl, vl):
    @pl.when(pl.program_id(0) == 0)
    def _():
        kl[...] = dot(latent_norm[...], wk[...]).astype(BF)
        vl[...] = dot(latent_norm[...], wv[...]).astype(BF)

    unit, _ = centred(patch[...].astype(F32))
    low = (unit * gain[...] + bias[...]).astype(BF)
    norm[...] = low
    kp[...] = dot(low, wk[...]).astype(BF)
    vp[...] = dot(low, wv[...]).astype(BF)


def head_of(shape):
    return lax.broadcasted_iota(jnp.int32, shape, 1) // HEAD_DIM


def spread_rows(v):
    head = head_of(v.shape)
    zero = jnp.zeros_like(v)
    count = v.shape[1] // HEAD_DIM
    return jnp.concatenate([jnp.where(head == h, v, zero) for h in range(count)], axis=0)


def gather_rows(v):
    heads = v.shape[1] // HEAD_DIM
    count = v.shape[0] // heads
    head = head_of((count, v.shape[1]))
    total = v[:count]
    for h in range(1, heads):
        total = jnp.where(head == h, v[h * count : (h + 1) * count], total)
    return total


def head_groups():
    half = INNER // 2
    return [(g, slice(g * half, (g + 1) * half)) for g in range(2)]


def pack_lanes(columns):
    count = columns[0].shape[0]
    lane = lax.broadcasted_iota(jnp.int32, (count, LANES), 1)
    step = LANES // len(columns)
    total = jnp.zeros((count, LANES), F32)
    for h, column in enumerate(columns):
        total = jnp.where(lane // step == h, column, total)
    return total


def widen(packed):
    head = head_of((packed.shape[0], INNER))
    total = jnp.zeros((packed.shape[0], INNER), F32)
    for h in range(HEADS):
        total = jnp.where(head == h, packed[:, h * PER : h * PER + 1], total)
    return total


def stack_heads(packed, offset, group):
    first = group * HEADS // 2
    return jnp.concatenate(
        [
            packed[:, h * PER + offset : h * PER + offset + 1]
            for h in range(first, first + HEADS // 2)
        ],
        axis=0,
    )


def attend_slots(slots):
    work = []
    for qo, qp, kp, vp, kl, vl, *_ in slots:
        queries = jnp.concatenate([qo[...], qp[...]], axis=0)
        for _, at in head_groups():
            big = spread_rows(queries[:, at])
            keys = jnp.concatenate([kp[:, at], kl[:, at]], axis=0)
            values = jnp.concatenate([vp[:, at], vl[:, at]], axis=0)
            work.append((big, keys, values))
    scores = [dot_t(big, keys) for big, keys, _ in work]
    tops = [jnp.max(v, axis=-1, keepdims=True) for v in scores]
    expos = [jnp.exp(v - top) for v, top in zip(scores, tops)]
    totals = [jnp.sum(v, axis=-1, keepdims=True) for v in expos]
    probs = [(v * (1.0 / total)).astype(BF) for v, total in zip(expos, totals)]
    outs = [gather_rows(dot(v, w[2])) for v, w in zip(probs, work)]
    logs = [top + jnp.log(total) for top, total in zip(tops, totals)]
    for k, (qo, _, _, _, _, _, oo, op, so, sp) in enumerate(slots):
        own = qo.shape[0]
        count = 2 * own
        columns = []
        for g, at in head_groups():
            out, log_total = outs[2 * k + g], logs[2 * k + g]
            columns += [log_total[h * count : (h + 1) * count] for h in range(HEADS // 2)]
            oo[:, at] = out[:own]
            op[:, at] = out[own:].astype(BF)
        packed = pack_lanes(columns)
        so[...] = packed[:own]
        sp[...] = packed[own:]


def attend_body(*refs):
    attend_slots([refs])


def forward_body(
    slot_rows,
    holding,
    oo,
    orecv,
    so,
    srecv,
    latent,
    cot,
    wo,
    wup,
    wdown,
    gain,
    bias,
    new_latents,
    act_out,
    pre_out,
    ffn_t,
    og_out,
    residual_grad,
    attended_grad,
    stats,
    output_grad,
    vectors,
    residual,
    ffn_in,
    acc,
    gacc,
    attended,
    packed,
):
    step = pl.program_id(0)
    count = latent.shape[0]
    slot = lax.broadcasted_iota(jnp.int32, (count, 1), 0) // slot_rows
    live = jnp.where(slot < holding[0, 0], 1.0, 0.0).astype(F32)

    @pl.when(step == 0)
    def _():
        a, b = so[...], srecv[...]
        top = jnp.maximum(a, b)
        both = top + jnp.log(jnp.exp(a - top) + jnp.exp(b - top))
        packed[...] = both
        mix = widen(jnp.exp(a - both)) * oo[...]
        mix += widen(jnp.exp(b - both)) * orecv[...].astype(F32)
        attended[...] = mix
        res = latent[...].astype(F32) + dot(mix.astype(BF), wo[...])
        residual[...] = res
        unit, _ = centred(res)
        low = (unit * gain[...] + bias[...]).astype(BF)
        ffn_in[...] = low
        ffn_t[...] = low.T
        og_out[...] = (cot[...].astype(F32) * live).astype(BF)
        acc[...] = jnp.zeros_like(acc)
        gacc[...] = jnp.zeros_like(gacc)

    pre = dot(ffn_in[...], wup[...])
    cdf = 0.5 * (1.0 + lax.erf(pre * (0.5**0.5)))
    act = (pre * cdf).astype(BF)
    act_out[...] = act
    acc[...] += dot(act, wdown[...])
    act_grad = dot_t(og_out[...], wdown[...])
    pdf = jnp.exp(-0.5 * pre * pre) * 0.3989422804014327
    pre_grad = (act_grad * (cdf + pre * pdf)).astype(BF)
    pre_out[...] = pre_grad
    gacc[...] += dot_t(pre_grad, wup[...])

    @pl.when(step == pl.num_programs(0) - 1)
    def _():
        res = residual[...]
        new_latents[...] = ((res + acc[...]) * live).astype(BF)
        unit, scale = centred(res)
        grad = gacc[...]
        vectors[0:1, :] = column_sum(grad * unit)
        vectors[1:2, :] = column_sum(grad)
        res_grad = og_out[...].astype(F32) + norm_back(unit, scale, gain[...], grad)
        residual_grad[...] = res_grad
        branch = res_grad.astype(BF)
        back = dot_t(branch, wo[...]).astype(BF)
        attended_grad[...] = back
        mix = attended[...]
        product = back.astype(F32) * mix
        head = head_of(product.shape)
        sums = [
            jnp.sum(jnp.where(head == h, product, 0.0), axis=-1, keepdims=True)
            for h in range(HEADS)
        ]
        delta = pack_lanes(sums)
        lane = lax.broadcasted_iota(jnp.int32, delta.shape, 1)
        stats[...] = jnp.where(lane % PER < PER // 2, packed[...], delta)
        output_grad[...] = t_dot(mix.astype(BF), branch).astype(BF)


def attend_back_slots(slots):
    work = []
    for qo, qp, kp, vp, kl, vl, do, dp, so, sp, *_ in slots:
        queries = jnp.concatenate([qo[...], qp[...]], axis=0)
        grads = jnp.concatenate([do[...], dp[...]], axis=0)
        stats = jnp.concatenate([so[...], sp[...]], axis=0)
        for g, at in head_groups():
            big = spread_rows(queries[:, at])
            back = spread_rows(grads[:, at])
            keys = jnp.concatenate([kp[:, at], kl[:, at]], axis=0)
            values = jnp.concatenate([vp[:, at], vl[:, at]], axis=0)
            work.append(
                (big, back, keys, values, stack_heads(stats, 0, g), stack_heads(stats, PER // 2, g))
            )
    scores = [dot_t(w[0], w[2]) for w in work]
    prob_grads = [dot_t(w[1], w[3]) for w in work]
    probs = [jnp.exp(v - w[4]) for v, w in zip(scores, work)]
    score_grads = [(v * (d - w[5])).astype(BF) for v, d, w in zip(probs, prob_grads, work)]
    values_grads = [t_dot(v.astype(BF), w[1]).astype(BF) for v, w in zip(probs, work)]
    keys_grads = [t_dot(v, w[0]).astype(BF) for v, w in zip(score_grads, work)]
    dqs = [gather_rows(dot(v, w[2])) for v, w in zip(score_grads, work)]
    for k, refs in enumerate(slots):
        own, patches = refs[0].shape[0], refs[2].shape[0]
        dkvp, dkvl, dqo, dqp = refs[10:]
        for g, at in head_groups():
            late = slice(INNER + at.start, INNER + at.stop)
            u = 2 * k + g
            dkvp[:, at] = keys_grads[u][:patches]
            dkvp[:, late] = values_grads[u][:patches]
            dkvl[:, at] = keys_grads[u][patches:]
            dkvl[:, late] = values_grads[u][patches:]
            dqo[:, at] = dqs[u][:own]
            dqp[:, at] = dqs[u][own:].astype(BF)


def attend_back_body(*refs):
    attend_back_slots([refs])


def up_grad_body(left, right, out):
    out[...] = dot(left[...], right[...]).astype(BF)


def down_grad_body(left, right, out):
    out[...] = t_dot(left[...], right[...]).astype(BF)


def kv_grad_body(media, latent, dkvp, dkvl, out):
    out[...] = (t_dot(media[...], dkvp[...]) + t_dot(latent[...], dkvl[...])).astype(BF)


def patch_back_body(patch, dkvp, wk, wv, gain, out, vectors):
    @pl.when(pl.program_id(0) == 0)
    def _():
        vectors[...] = jnp.zeros_like(vectors)

    grad = dot_t(dkvp[:, :INNER], wk[...]) + dot_t(dkvp[:, INNER:], wv[...])
    unit, scale = centred(patch[...].astype(F32))
    vectors[0:1, :] += column_sum(grad * unit)
    vectors[1:2, :] += column_sum(grad)
    out[...] = norm_back(unit, scale, gain[...], grad)


def latent_back_body(
    latent, norm, dkvl, dqo, drecv, residual_grad, wq, wk, wv, gain, out, query_grad, vectors
):
    dq = (dqo[...] + drecv[...].astype(F32)).astype(BF)
    product = (HEAD_DIM**-0.5 * t_dot(norm[...], dq)).astype(BF)
    if query_grad.shape == product.shape:
        query_grad[...] = product
    else:
        product = product.reshape(-1, 32, INNER)
        shape = query_grad.shape[:-1] + (INNER,)
        query_grad[..., :INNER] = product[:, :16].reshape(shape)
        query_grad[..., INNER:] = product[:, 16:].reshape(shape)
    grad = dot_t(dkvl[:, :INNER], wk[...]) + dot_t(dkvl[:, INNER:], wv[...])
    grad += HEAD_DIM**-0.5 * dot_t(dq, wq[...])
    unit, scale = centred(latent[...].astype(F32))
    vectors[0:1, :] = column_sum(grad * unit)
    vectors[1:2, :] = column_sum(grad)
    out[...] = residual_grad[...] + norm_back(unit, scale, gain[...], grad)


def ffn_back_body(
    residual, gacc, og, mix_ref, packed, wo, gain, residual_grad, attended_grad, stats, out, vectors
):
    unit, scale = centred(residual[...])
    grad = gacc[...]
    vectors[0:1, :] = column_sum(grad * unit)
    vectors[1:2, :] = column_sum(grad)
    res_grad = og[...].astype(F32) + norm_back(unit, scale, gain[...], grad)
    residual_grad[...] = res_grad
    branch = res_grad.astype(BF)
    back = dot_t(branch, wo[...]).astype(BF)
    attended_grad[...] = back
    mix = mix_ref[...]
    product = back.astype(F32) * mix
    head = head_of(product.shape)
    sums = [
        jnp.sum(jnp.where(head == h, product, 0.0), axis=-1, keepdims=True) for h in range(HEADS)
    ]
    delta = pack_lanes(sums)
    lane = lax.broadcasted_iota(jnp.int32, delta.shape, 1)
    stats[...] = jnp.where(lane % PER < PER // 2, packed[...], delta)
    if out is not None:
        out[...] = t_dot(mix.astype(BF), branch).astype(BF).reshape(out.shape)


def plus(a, b):
    return a.astype(F32) + b.astype(F32)


class Names:
    def __getattr__(self, name):
        return name


n = Names()
STREAMS = ("d0", "d1", "d2", "d3", "u0", "u1", "u2", "u3", "K", "W", "Q")
ORDERS = {
    "d0": "xywz", "d1": "zyxw", "d2": "ywxz", "d3": "xzyw", "u0": "yxzw", "u1": "zyxw",
    "u2": "yxzw", "u3": "zywx", "K": "yzxw", "W": "yxwz", "Q": "xzyw",
}
PLAN = (
    "fi", "md0", "md1", "md2", "md3", "af0:4", "af4:8", "cb", "j0", "j1", "j2", "j3", "u0",
    "j4", "j5", "u1", "j6", "j7", "u2", "fb", "u3", "d0", "+u0", "+u1", "d1", "d2", "d3",
    "at0:8", "+u2", "+u0", "kv0", "+u3", "kv1", "kv2", "+d0", "+d2", "kv3", "+K", "ow", "lat",
    "+W", "+u1", "+d3", "+u2", "+d0", "pt0", "+u0", "+d2", "+Q", "+d1", "pt1", "pt2", "+u1",
    "pt3", "+u2", "+u0", "+u3", "+d0", "+V", "+u1", "+d2", "+K", "+u2", "+Q", "+W", "+u3", "+K",
    "+d1", "+V", "+d3", "+V", "+W", "+Q", "+d1", "+u3", "+K", "+d3", "+V", "+Q", "+W", "+K",
    "+V", "+W", "+Q",
)
DIMS = "wzyx"
DIMS_ALL = "wzycx"
BLOCK = (32, 1024)
LOADED = (n.latent, n.wq, n.og, n.wo)
GIVEN = LOADED + (
    n.patch,
    n.wk, n.wv, n.wup, n.wdown, n.images, n.device, n.fg, n.fb, n.mg, n.mb, n.lg, n.lb,
)


def is_late(s):
    return s in "KWQ"


def main_scratch(nl, np_, width, hidden):
    def bf(*shape):
        return pltpu.VMEM(shape, BF)

    def f4(*shape):
        return pltpu.VMEM(shape, F32)

    step = hidden // 8
    turned = (2, 2, 2, 2, step // 4, nl)
    turned_in = (2, 2, 2, 2, 32, nl)
    items = [
        (n.latent, bf(nl, width)),
        (n.wq, bf(width, INNER)),
        (n.og, bf(nl, width)),
        (n.patch, bf(2, np_ // 4, width)),
        (n.wo, bf(INNER, width)),
        (n.oo, f4(nl, INNER)),
        (n.op, bf(nl, INNER)),
        (n.so, f4(nl, LANES)),
        (n.sp, f4(nl, LANES)),
        (n.orecv, bf(nl, INNER)),
        (n.srecv, f4(nl, LANES)),
        (n.q, bf(nl, INNER)),
        (n.q_peer, bf(nl, INNER)),
        (n.kp, bf(np_, INNER)),
        (n.vp, bf(np_, INNER)),
        (n.kl, bf(nl, INNER)),
        (n.vl, bf(nl, INNER)),
        (n.norm_l, bf(nl, width)),
        (n.norm_m, bf(np_, width)),
        (n.wu, bf(2, width, step)),
        (n.wd, bf(2, step, width)),
        (n.og_sib, bf(nl, width)),
        (n.act_own, bf(*turned)),
        (n.act_send, bf(*turned)),
        (n.act_sib, bf(*turned)),
        (n.ffn_own, bf(*turned_in)),
        (n.ffn_send, bf(*turned_in)),
        (n.ffn_sib, bf(*turned_in)),
        (n.residual, f4(nl, width)),
        (n.gacc, f4(nl, width)),
        (n.acc, f4(nl, width)),
        (n.ffn_in, bf(nl, width)),
        (n.attended, f4(nl, INNER)),
        (n.grad, bf(nl, INNER)),
        (n.stats, f4(nl, LANES)),
        (n.grad_peer, bf(nl, INNER)),
        (n.stats_peer, f4(nl, LANES)),
        (n.dkvp, bf(np_, 2 * INNER)),
        (n.dkvl, bf(nl, 2 * INNER)),
        (n.dq_peer, bf(nl, INNER)),
        (n.vs, f4(5, 8, width)),
        (n.vr, f4(5, 8, width)),
        (n.sums, f4(2, width)),
        (n.pre, bf(2, 2, 2, 2, 2, *BLOCK)),
        (n.pre_sib, bf(2, 2, 2, 2, 2, *BLOCK)),
    ]
    for s in STREAMS:
        if s[0] == "u":
            items.append((s, bf(2, 2, 2, 2, *BLOCK)))
        if s[0] == "d":
            items.append((s, bf(2, 2, 2, *BLOCK)))
            items += [(s + "_p", bf(2, 2, 2, 32, nl)), (s + "_q", bf(2, 2, 2, 32, nl))]
    for axis in "xyz":
        items += [("og_p" + axis, bf(nl, width)), ("og_q" + axis, bf(nl, width))]
    for s in STREAMS:
        wide = BLOCK[1] // 2 if s in "KW" else BLOCK[1]
        for k in range({"u": 3, "d": 2}.get(s[0], 4), -1, -1):
            items.append((s + "_%d" % k, bf(*((2,) * k), BLOCK[0], wide)))
    dma = pltpu.SemaphoreType.DMA
    items += [
        (n.load_sem, dma((len(LOADED) + 4,))),
        (n.weight_sem, dma((2, 2))),
        (n.store_sem, dma((6,))),
        (n.patch_sem, dma((2,))),
        (n.send_sem, dma((96,))),
        (n.recv_sem, dma((96,))),
    ]
    return [k for k, _ in items], [v for _, v in items]


def main_body(names, *refs):
    src = SimpleNamespace(**dict(zip(GIVEN, refs)))
    outs = len(GIVEN)
    fin, vec, patches_low, latents_grad, new_latents = refs[outs : outs + 5]
    t = SimpleNamespace(**dict(zip(names, refs[outs + 5 :])))
    load_sem, weight_sem, store_sem = t.load_sem, t.weight_sem, t.store_sem
    mine = lax.axis_index("img")
    xb = lax.axis_index("lat")
    bit = {"x": xb, "c": mine % 2, "y": (mine // 2) % 2, "z": (mine // 4) % 2, "w": (mine // 8) % 2}

    def to(axis, weight):
        return (mine + weight - 2 * weight * bit[axis], xb)

    peer = {"c": to("c", 1), "y": to("y", 2), "z": to("z", 4), "w": to("w", 8), "x": (mine, 1 - xb)}
    for axis in "xyz":
        beside = peer[axis][0] + 1 - 2 * bit["c"]
        peer["c" + axis] = (beside, peer[axis][1])
    barrier = pltpu.get_barrier_semaphore()
    for axis in peer:
        pl.semaphore_signal(
            barrier, inc=1, device_id=peer[axis], device_id_type=pl.DeviceIdType.MESH
        )

    step = t.wd.shape[1]
    count = t.og.shape[0]
    weights = {}

    def load_weights(j):
        slot = j % 2
        col = pl.ds(j * step, step)
        pair = (
            pltpu.make_async_copy(src.wup.at[:, col], t.wu.at[slot], weight_sem.at[0, slot]),
            pltpu.make_async_copy(src.wdown.at[col], t.wd.at[slot], weight_sem.at[1, slot]),
        )
        for copy in pair:
            copy.start()
        weights[j] = pair

    loads = {}

    def load(names):
        for name in names:
            i = LOADED.index(name)
            loads[name] = pltpu.make_async_copy(getattr(src, name), getattr(t, name), load_sem.at[i])
            loads[name].start()

    def load_kv(first):
        for i, name in enumerate((n.wk, n.wv)):
            loads[name] = pltpu.make_async_copy(
                getattr(src, name), t.wu.at[i], load_sem.at[len(LOADED) + first + i]
            )
            loads[name].start()

    size = src.patch.shape[0] // 4
    patch_loads = []

    def load_patch():
        i = len(patch_loads)
        copy = pltpu.make_async_copy(
            src.patch.at[pl.ds(i % 4 * size, size)], t.patch.at[i % 2], t.patch_sem.at[i % 2]
        )
        copy.start()
        patch_loads.append(copy)

    load(LOADED[:3])
    load_kv(0)
    load_patch()
    load_patch()
    load(LOADED[3:])

    def need(*names):
        for name in names:
            if name in loads:
                loads.pop(name).wait()

    pl.semaphore_wait(barrier, len(peer))
    used = []

    def send(source, target, axis):
        slot = len(used)
        copy = pltpu.make_async_remote_copy(
            src_ref=source,
            dst_ref=target,
            send_sem=t.send_sem.at[slot],
            recv_sem=t.recv_sem.at[slot],
            device_id=peer[axis],
            device_id_type=pl.DeviceIdType.MESH,
        )
        copy.start()
        used.append(copy)
        return copy

    arriving = {}

    def arrive(*names):
        for name in names:
            if name in arriving:
                arriving.pop(name).wait_recv()

    order = {s: ("c" if is_late(s) else "") + ORDERS[s] for s in STREAMS}
    place = {s: 1 if s[0] == "d" else 0 for s in STREAMS}
    half = BLOCK[1] // 2
    buffer = {s: getattr(t, s) for s in STREAMS if not is_late(s)}
    buffer["K"] = buffer["W"] = t.pre
    buffer["Q"] = t.pre_sib
    column = {"K": pl.ds(0, half), "W": pl.ds(half, half)}

    def where(s, axis, value):
        done = order[s][: place[s]]
        index = []
        for d in DIMS_ALL if is_late(s) else DIMS:
            if s[0] == "d" and d == order[s][0]:
                continue
            if d == axis:
                index.append(value)
            else:
                index.append(bit[d] if d in done else slice(None))
        if s in column:
            index += [slice(None), column[s]]
        return tuple(index)

    def got(s):
        return getattr(t, s + "_%d" % (len(order[s]) - 1 - place[s]))

    def start(s):
        axis = order[s][place[s]]
        arriving[s] = send(buffer[s].at[where(s, axis, 1 - bit[axis])], got(s), axis)

    def take(s):
        axis = order[s][place[s]]
        arrive(s)
        if s == "Q" and place[s] == 0:
            arrive(n.O)
        at = where(s, axis, bit[axis])
        total = plus(buffer[s][at], got(s)[...])
        place[s] += 1
        if place[s] < len(order[s]):
            buffer[s][at] = total.astype(BF)
            start(s)
        elif s in column:
            fin[8, :, column[s]] = total
        else:
            fin[9 if s == "Q" else STREAMS.index(s)] = total

    vs, vr = t.vs, t.vr
    vec_order = "cxyzw"
    vec_place = [0]

    def take_vector():
        i = vec_place[0]
        arrive(n.V)
        if i < 4:
            vs[i + 1] = vs[i] + vr[i]
            arriving["V"] = send(vs.at[i + 1], vr.at[i + 1], vec_order[i + 1])
        else:
            vec[...] = vs[i] + vr[i]
        vec_place[0] += 1

    stores = []

    def store(source, target):
        slot = len(stores)
        stores.append(pltpu.make_async_copy(source, target, store_sem.at[slot]))
        stores[slot].start()

    core = bit["c"]
    def live_rows():
        total = jnp.int32(0)
        for i in range(src.images.shape[0]):
            total += jnp.where(src.device[i] == mine, src.images[i], 0)
        slot = lax.broadcasted_iota(jnp.int32, (count, 1), 0) // (count // 8)
        return jnp.where(slot < total, 1.0, 0.0).astype(F32)

    def first():
        need(n.latent, n.wq)
        unit, _ = centred(t.latent[...].astype(F32))
        low = (unit * src.lg[...] + src.lb[...]).astype(BF)
        t.norm_l[...] = low
        t.q[...] = (HEAD_DIM**-0.5 * dot(low, t.wq[...])).astype(BF)
        arriving[n.q_peer] = send(t.q, t.q_peer, "x")
        need(n.og, n.wk, n.wv)
        t.og[...] = (t.og[...].astype(F32) * live_rows()).astype(BF)
        arriving[n.og_sib] = send(t.og, t.og_sib, "c")
        for axis in "xyz":
            arriving["og_p" + axis] = send(t.og, getattr(t, "og_p" + axis), axis)
        t.kl[...] = dot(low, t.wu[0]).astype(BF)
        t.vl[...] = dot(low, t.wu[1]).astype(BF)

    def media(i):
        patch_loads[i].wait()
        at = pl.ds(i * size, size)
        unit, _ = centred(t.patch[i % 2].astype(F32))
        low = (unit * src.mg[...] + src.mb[...]).astype(BF)
        t.norm_m[at] = low
        t.kp[at] = dot(low, t.wu[0]).astype(BF)
        t.vp[at] = dot(low, t.wu[1]).astype(BF)
        load_patch()
        if i == 3:
            load_weights(0)
            load_weights(1)

    def slot_rows(i):
        lat, med = count // 8, t.kp.shape[0] // 8
        return (
            pl.ds(pl.multiple_of(i * lat, lat), lat),
            pl.ds(pl.multiple_of(i * med, med), med),
        )

    def attend(first, last):
        arrive(n.q_peer)

        def refs(i):
            a, b = slot_rows(i)
            return (
                t.q.at[a], t.q_peer.at[a], t.kp.at[b], t.vp.at[b], t.kl.at[a], t.vl.at[a],
                t.oo.at[a], t.op.at[a], t.so.at[a], t.sp.at[a],
            )

        @pl.loop(first // 2, last // 2)
        def _(i):
            attend_slots([refs(2 * i), refs(2 * i + 1)])

        at = pl.ds(first * (count // 8), (last - first) * (count // 8))
        arriving["o%d" % first] = send(t.op.at[at], t.orecv.at[at], "x")
        arriving["s%d" % first] = send(t.sp.at[at], t.srecv.at[at], "x")

    def combine():
        for axis in "xyz":
            name = "og_p" + axis
            arrive(name)
            arriving["og_q" + axis] = send(getattr(t, name), getattr(t, "og_q" + axis), "c")
        need(n.wo)
        for name in list(arriving):
            if name[0] in "os" and name[1:].isdigit():
                arrive(name)
        a, b = t.so[...], t.srecv[...]
        top = jnp.maximum(a, b)
        both = top + jnp.log(jnp.exp(a - top) + jnp.exp(b - top))
        t.so[...] = both
        mix = widen(jnp.exp(a - both)) * t.oo[...]
        mix += widen(jnp.exp(b - both)) * t.orecv[...].astype(F32)
        t.attended[...] = mix
        res = t.latent[...].astype(F32) + dot(mix.astype(BF), t.wo[...])
        t.residual[...] = res
        unit, _ = centred(res)
        low = (unit * src.fg[...] + src.fb[...]).astype(BF)
        t.ffn_in[...] = low
        turned = low.T.reshape(8, 2, -1, count)
        even, odd = turned[:, 0], turned[:, 1]
        shape = t.ffn_own.shape
        t.ffn_own[...] = jnp.where(core == 0, even, odd).reshape(shape)
        t.ffn_send[...] = jnp.where(core == 0, odd, even).reshape(shape)
        arriving[n.ffn_sib] = send(t.ffn_send, t.ffn_sib, "c")

    def ffn(j):
        for copy in weights.pop(j):
            copy.wait()
        wup, wdown = t.wu[j % 2], t.wd[j % 2]
        pre = dot(t.ffn_in[...], wup)
        cdf = 0.5 * (1.0 + lax.erf(pre * (0.5**0.5)))
        pdf = jnp.exp(-0.5 * pre * pre) * 0.3989422804014327
        act = (pre * cdf).astype(BF)
        turned = act.T
        even, odd = turned[: step // 2], turned[step // 2 :]
        at = (j // 4, (j // 2) % 2, j % 2)
        shape = t.act_own.shape[3:]
        t.act_own[at] = jnp.where(core == 0, even, odd).reshape(shape)
        t.act_send[at] = jnp.where(core == 0, odd, even).reshape(shape)
        arriving["act%d" % j] = send(t.act_send.at[at], t.act_sib.at[at], "c")
        down = dot(act, wdown)
        act_grad = dot_t(t.og[...], wdown)
        pre_grad = (act_grad * (cdf + pre * pdf)).astype(BF)
        group = (j // 4, (j // 2) % 2)
        t.pre[group + (slice(None),) * 4 + (pl.ds((j % 2) * step, step),)] = pre_grad.reshape(
            2, 2, 2, 32, step
        )
        if j % 2 == 1:
            name = "pre%d" % (j // 2)
            arriving[name] = send(t.pre.at[group], t.pre_sib.at[group], "c")
            pre_sent.append(len(used) - 1)
        back = dot_t(pre_grad, wup)
        if j == 0:
            t.acc[...] = down
            t.gacc[...] = back
        else:
            t.acc[...] += down
            t.gacc[...] += back
        if j in (3, 7):
            for g in range(4):
                s = "d%d" % g
                axis = order[s][0]
                at = tuple(1 - bit[d] if d == axis else slice(None) for d in DIMS[1:])
                at = (j // 4,) + at + (pl.ds(g * 32, 32),)
                p, q = getattr(t, s + "_p").at[j // 4], getattr(t, s + "_q").at[j // 4]
                arriving[s + "_p%d" % j] = send(t.act_own.at[at], p, axis)
                arriving[s + "_q%d" % j] = send(t.act_send.at[at], q, "c" + axis)
        if j < 6:
            load_weights(j + 2)
        if j == 7:
            load_kv(2)
            t.ffn_in[...] = ((t.residual[...] + t.acc[...]) * live_rows()).astype(BF)
            store(t.ffn_in, new_latents)

    pre_sent = []

    def ffn_back():
        ffn_back_body(
            t.residual, t.gacc, t.og, t.attended, t.so, t.wo, src.fg,
            t.residual, t.grad, t.stats, None, vs.at[0, pl.ds(4, 2)],
        )
        arriving[n.grad_peer] = send(t.grad, t.grad_peer, "x")
        arriving[n.stats_peer] = send(t.stats, t.stats_peer, "x")

    def send_late(rows, name):
        o, r = buffer["Q"], t.Q_4
        arriving[name] = send(
            o.at[:, :, :, 1 - core, :, rows], r.at[:, :, :, :, rows], "c"
        )

    def output_group():
        product = t_dot(t.attended[...].astype(BF), t.residual[...].astype(BF)).astype(BF)
        buffer["Q"][..., pl.ds(0, 16), :] = product.reshape(2, 2, 2, 2, 2, 16, BLOCK[1])
        send_late(pl.ds(0, 16), "O")

    def rows_of(ref, at):
        v = ref[at]
        return v.reshape(-1, v.shape[-1])

    def down_group(g):
        s = "d%d" % g
        axis = order[s][0]
        arrive(n.og_sib, "og_q" + axis, *("act%d" % j for j in range(8)))
        arrive(*(s + end for end in ("_p3", "_q3", "_p7", "_q7")))
        at = tuple(bit[d] if d == axis else slice(None) for d in DIMS) + (pl.ds(g * 32, 32),)
        v = dot(rows_of(t.act_own, at), t.og[...])
        v += dot(rows_of(t.act_sib, at), t.og_sib[...])
        every = (slice(None),)
        v += dot(rows_of(getattr(t, s + "_p"), every), getattr(t, "og_p" + axis)[...])
        v += dot(rows_of(getattr(t, s + "_q"), every), getattr(t, "og_q" + axis)[...])
        buffer[s][...] = v.astype(BF).reshape((2, 2, 2) + BLOCK)
        start(s)

    def up_group(g):
        s = "u%d" % g
        arrive(n.ffn_sib, "pre%d" % g)
        axis = order[s][0]
        group = (g // 2, g % 2)
        for value in (1 - bit[axis], bit[axis]):
            at = where(s, axis, value)
            v = dot(rows_of(t.ffn_own, at), rows_of(t.pre, group))
            v += dot(rows_of(t.ffn_sib, at), rows_of(t.pre_sib, group))
            buffer[s][at] = v.astype(BF).reshape((2, 2, 2) + BLOCK)
            if s not in arriving:
                start(s)

    def attend_back(first, last):
        arrive(n.grad_peer, n.stats_peer)

        def refs(i):
            a, b = slot_rows(i)
            return (
                t.q.at[a], t.q_peer.at[a], t.kp.at[b], t.vp.at[b], t.kl.at[a], t.vl.at[a],
                t.grad.at[a], t.grad_peer.at[a], t.stats.at[a], t.stats_peer.at[a],
                t.dkvp.at[b], t.dkvl.at[a], t.oo.at[a], t.dq_peer.at[a],
            )

        @pl.loop(first // 2, last // 2)
        def _(i):
            attend_back_slots([refs(2 * i), refs(2 * i + 1)])

        if last == 8:
            arriving[n.dq_recv] = send(t.dq_peer, t.orecv, "x")

    def kv_group(g):
        while pre_sent:
            slot = pre_sent.pop()
            used[slot].wait_send()
            used[slot] = None
        col = pl.ds(g * 256, 256)
        v = t_dot(t.norm_m[...], t.dkvp[:, col])
        v += t_dot(t.norm_l[...], t.dkvl[:, col])
        buffer["K"][..., col] = v.astype(BF).reshape(2, 2, 2, 2, 2, 32, 256)
        if g == 1:
            start("K")
        if g == 3:
            start("W")

    def latent_back():
        need(n.wk, n.wv)
        arrive(n.dq_recv)
        latent_back_body(
            t.latent, t.norm_l, t.dkvl, t.oo, t.orecv, t.residual,
            t.wq, t.wu.at[0], t.wu.at[1], src.lg, t.residual,
            buffer["Q"].at[..., pl.ds(16, 16), :], vs.at[0, pl.ds(2, 2)],
        )
        send_late(pl.ds(16, 16), "Q")
        stores[0].wait()
        stores[0] = None
        t.ffn_in[...] = t.residual[...].astype(BF)
        store(t.ffn_in, latents_grad)

    def patch_back(i):
        need(n.wk, n.wv)
        at = pl.ds(i * size, size)
        dkv = t.dkvp
        grad = dot_t(dkv[at, :INNER], t.wu[0]) + dot_t(dkv[at, INNER:], t.wu[1])
        patch_loads[4 + i].wait()
        unit, scale = centred(t.patch[i % 2].astype(F32))
        sums = t.sums
        a, b = column_sum(grad * unit), column_sum(grad)
        if i > 0:
            a, b = a + sums[0:1, :], b + sums[1:2, :]
        sums[0:1, :] = a
        sums[1:2, :] = b
        dkv[at] = norm_back(unit, scale, src.mg[...], grad).astype(BF)
        store(dkv.at[at], patches_low.at[at])
        if i < 2:
            load_patch()
        if i == 3:
            vs[0, 0:2, :] = sums[...]
            vs[0, 6:8, :] = jnp.zeros((2, vs.shape[2]), F32)
            arriving["V"] = send(vs.at[0], vr.at[0], vec_order[0])

    simple = {"fi": first, "cb": combine, "fb": ffn_back, "ow": output_group, "lat": latent_back}
    simple["+V"] = take_vector
    for item in PLAN:
        if item in simple:
            simple[item]()
        elif item[0] == "+":
            take(item[1:])
        elif item[:2] == "at":
            a, b = item[2:].split(":")
            attend_back(int(a), int(b))
        elif item[:2] == "af":
            a, b = item[2:].split(":")
            attend(int(a), int(b))
        elif item[:2] == "md":
            media(int(item[2:]))
        elif item[:2] == "kv":
            kv_group(int(item[2:]))
        elif item[:2] == "pt":
            patch_back(int(item[2:]))
        else:
            {"j": ffn, "d": down_group, "u": up_group}[item[0]](int(item[1:]))
    for copy in stores:
        if copy is not None:
            copy.wait()
    for copy in used:
        if copy is not None:
            copy.wait_send()


def last_body(
    patches_in, latents_in, fresh, fin, vec,
    patches_grad, new_latents, latents_grad, up, down, key, value, out, query, *rest,
):
    thin, (pin, pout, lin, lout, nin, held, sem) = rest[:6], rest[6:]
    copies = []

    def move(source, target):
        copies.append(pltpu.make_async_copy(source, target, sem.at[len(copies)]))
        copies[-1].start()
        return copies[-1]

    parts = pin.shape[0]
    size = pin.shape[1]
    waits = [move(patches_in.at[pl.ds(i * size, size)], pin.at[i]) for i in range(parts)]
    waits += [move(fin, held), move(latents_in, lin), move(fresh, nin)]
    for i in range(parts):
        waits[i].wait()
        pout[i] = pin[i].astype(F32)
        move(pout.at[i], patches_grad.at[pl.ds(i * size, size)])
    waits[parts].wait()
    for g in range(4):
        move(held.at[4 + g], up.at[:, pl.ds(g * 1024, 1024)])
        move(held.at[g], down.at[pl.ds(g * 32, 32)])
    move(held.at[8, :, pl.ds(0, INNER)], key)
    move(held.at[8, :, pl.ds(INNER, INNER)], value)
    move(held.at[9, pl.ds(0, 16)], out)
    for k in range(2):
        move(held.at[9, pl.ds(16, 16), pl.ds(k * INNER, INNER)], query.at[pl.ds(k * 16, 16)])
    waits[parts + 1].wait()
    lout[...] = lin[...].astype(F32)
    move(lout, latents_grad)
    waits[parts + 2].wait()
    move(nin, new_latents)
    place = lax.axis_index("img") * 2 + lax.axis_index("lat")
    width = vec.shape[1]
    turned = pltpu.roll(vec[...], width - place * 32, 1)
    for i, ref in enumerate(thin):
        ref[...] = turned[i : i + 1, :32]
    for copy in copies[len(waits) :]:
        copy.wait()


def swap_lat(v):
    return lax.ppermute(v, "lat", [(0, 1), (1, 0)])


def halving_sum(v, order, bits, count, keep):
    left = list(range(bits - 1, -1, -1)) + [-1]
    mine = lax.axis_index("img")
    for place, axis in enumerate(order):
        dim = left.index(axis)
        if axis < 0:
            bit = lax.axis_index("lat")
            pairs, name = [(0, 1), (1, 0)], "lat"
        else:
            bit = (mine // 2**axis) % 2
            pairs, name = [(i, i ^ 2**axis) for i in range(count)], "img"
        out = lax.dynamic_index_in_dim(v, 1 - bit, dim, keepdims=False)
        stay = lax.dynamic_index_in_dim(v, bit, dim, keepdims=False)
        got = lax.ppermute(out, name, pairs)
        v = stay.astype(F32) + got.astype(F32)
        if place < len(order) - 1 and keep == BF:
            v = v.astype(BF)
        left.pop(dim)
    return v


def local(
    count,
    patches,
    latents,
    cotangent,
    doc_images,
    doc_device,
    query_weight,
    key_weight,
    value_weight,
    output_weight,
    up_weight,
    down_weight,
    media_gain,
    media_bias,
    latent_gain,
    latent_bias,
    ffn_gain,
    ffn_bias,
):
    slots, own_patches, width = patches.shape
    own_latents = latents.shape[1]
    hidden = up_weight.shape[1]
    np_, nl = slots * own_patches, slots * own_latents
    mine = lax.axis_index("img")
    holding = jnp.sum(jnp.where(doc_device == mine, doc_images, 0)).reshape(1, 1)
    patch = patches.reshape(np_, width)
    latent = latents.reshape(nl, width)
    cot = cotangent.reshape(nl, width)
    mg, mb = media_gain.reshape(1, width), media_bias.reshape(1, width)
    lg, lb = latent_gain.reshape(1, width), latent_bias.reshape(1, width)
    fg, fb = ffn_gain.reshape(1, width), ffn_bias.reshape(1, width)
    wspec = whole((width, INNER))
    vspec = whole((1, width))
    lspec = whole((nl, width))

    norm_l, query = call(
        latent_body,
        (1,),
        [lspec, vspec, vspec, wspec],
        [(struct((nl, width), BF), lspec), (struct((nl, INNER), BF), whole((nl, INNER)))],
        (latent, lg, lb, query_weight),
        2 * nl * width * INNER,
    )
    query_peer = swap_lat(query)
    blk = min(np_, 256)
    norm_m, kp, vp, kl, vl = call(
        media_body,
        (np_ // blk,),
        [rows(blk, width), vspec, vspec, wspec, wspec, lspec],
        [
            (struct((np_, width), BF), rows(blk, width)),
            (struct((np_, INNER), BF), rows(blk, INNER)),
            (struct((np_, INNER), BF), rows(blk, INNER)),
            (struct((nl, INNER), BF), whole((nl, INNER))),
            (struct((nl, INNER), BF), whole((nl, INNER))),
        ],
        (patch, mg, mb, key_weight, value_weight, norm_l),
        4 * (np_ + nl) * width * INNER,
    )
    q_s, p_s, s_s = rows(own_latents, INNER), rows(own_patches, INNER), rows(own_latents, LANES)
    att_flops = 4 * slots * (own_patches + own_latents) * INNER * INNER
    o_own, o_peer, s_own, s_peer = call(
        attend_body,
        (slots,),
        [q_s, q_s, p_s, p_s, q_s, q_s],
        [
            (struct((nl, INNER), F32), q_s),
            (struct((nl, INNER), BF), q_s),
            (struct((nl, LANES), F32), s_s),
            (struct((nl, LANES), F32), s_s),
        ],
        (query, query_peer, kp, vp, kl, vl),
        att_flops,
    )
    o_recv, s_recv = swap_lat(o_peer), swap_lat(s_peer)
    fblk = min(hidden, 512)
    nspec = whole((nl, INNER))
    (
        new_latents,
        act,
        pre_grad,
        ffn_t,
        out_grad,
        residual_grad,
        attended_grad,
        stats,
        output_grad,
        ffn_vec,
    ) = call(
        partial(forward_body, own_latents),
        (hidden // fblk,),
        [
            pl.BlockSpec(memory_space=pltpu.SMEM),
            nspec,
            nspec,
            whole((nl, LANES)),
            whole((nl, LANES)),
            lspec,
            lspec,
            whole((INNER, width)),
            cols(width, fblk),
            rows(fblk, width),
            vspec,
            vspec,
        ],
        [
            (struct((nl, width), BF), lspec),
            (struct((nl, hidden), BF), cols(nl, fblk)),
            (struct((nl, hidden), BF), cols(nl, fblk)),
            (struct((width, nl), BF), whole((width, nl))),
            (struct((nl, width), BF), lspec),
            (struct((nl, width), F32), lspec),
            (struct((nl, INNER), BF), nspec),
            (struct((nl, LANES), F32), whole((nl, LANES))),
            (struct((INNER, width), BF), whole((INNER, width))),
            (struct((2, width), F32), whole((2, width))),
        ],
        (
            holding,
            o_own,
            o_recv,
            s_own,
            s_recv,
            latent,
            cot,
            output_weight,
            up_weight,
            down_weight,
            fg,
            fb,
        ),
        8 * nl * width * hidden,
        scratch=[
            pltpu.VMEM((nl, width), F32),
            pltpu.VMEM((nl, width), BF),
            pltpu.VMEM((nl, width), F32),
            pltpu.VMEM((nl, width), F32),
            pltpu.VMEM((nl, INNER), F32),
            pltpu.VMEM((nl, LANES), F32),
        ],
    )
    grad_peer, stats_peer = swap_lat(attended_grad), swap_lat(stats)
    (down_grad,) = call(
        down_grad_body,
        (hidden // fblk,),
        [cols(nl, fblk), lspec],
        [(struct((hidden, width), BF), rows(fblk, width))],
        (act, out_grad),
        2 * nl * width * hidden,
    )
    (up_grad,) = call(
        up_grad_body,
        (hidden // fblk,),
        [whole((width, nl)), cols(nl, fblk)],
        [(struct((width, hidden), BF), cols(width, fblk))],
        (ffn_t, pre_grad),
        2 * nl * width * hidden,
    )
    dkvp, dkvl, dq_own, dq_peer = call(
        attend_back_body,
        (slots,),
        [q_s, q_s, p_s, p_s, q_s, q_s, q_s, q_s, s_s, s_s],
        [
            (struct((np_, 2 * INNER), BF), rows(own_patches, 2 * INNER)),
            (struct((nl, 2 * INNER), BF), rows(own_latents, 2 * INNER)),
            (struct((nl, INNER), F32), q_s),
            (struct((nl, INNER), BF), q_s),
        ],
        (query, query_peer, kp, vp, kl, vl, attended_grad, grad_peer, stats, stats_peer),
        att_flops * 5 // 2,
    )
    dq_recv = swap_lat(dq_peer)
    kblk = 256
    (kv_grad,) = call(
        kv_grad_body,
        (2 * INNER // kblk,),
        [whole((np_, width)), lspec, cols(np_, kblk), cols(nl, kblk)],
        [(struct((width, 2 * INNER), BF), cols(width, kblk))],
        (norm_m, norm_l, dkvp, dkvl),
        4 * (np_ + nl) * width * INNER,
    )
    patches_grad, media_vec = call(
        patch_back_body,
        (np_ // blk,),
        [rows(blk, width), rows(blk, 2 * INNER), wspec, wspec, vspec],
        [(struct((np_, width), F32), rows(blk, width)), (struct((2, width), F32), whole((2, width)))],
        (patch, dkvp, key_weight, value_weight, mg),
        4 * np_ * width * INNER,
    )
    latents_grad, query_grad, latent_vec = call(
        latent_back_body,
        (1,),
        [
            lspec,
            lspec,
            whole((nl, 2 * INNER)),
            nspec,
            nspec,
            lspec,
            wspec,
            wspec,
            wspec,
            vspec,
        ],
        [
            (struct((nl, width), F32), lspec),
            (struct((width, INNER), BF), wspec),
            (struct((2, width), F32), whole((2, width))),
        ],
        (
            latent,
            norm_l,
            dkvl,
            dq_own,
            dq_recv,
            residual_grad,
            query_weight,
            key_weight,
            value_weight,
            lg,
        ),
        8 * nl * width * INNER,
    )

    bits = count.bit_length() - 1
    first = list(range(1, bits))
    orders = (
        [0, -1] + first,
        [0] + first + [-1],
        [0] + first[1:] + [-1] + first[:1],
    )

    def reduce(v, order, keep=BF):
        shape = (2,) * (bits + 1) + (v.shape[0] // (2 * count),) + v.shape[1:]
        return halving_sum(v.reshape(shape), order, bits, count, keep)

    def reduce_parts(v):
        unit = v.shape[1] // 8
        cuts = (0, 3 * unit, 6 * unit, 8 * unit)
        return jnp.concatenate(
            [reduce(v[:, a:b], order) for a, b, order in zip(cuts, cuts[1:], orders)], axis=1
        )

    down_sum = reduce_parts(down_grad)
    up_sum = reduce_parts(up_grad)
    output_sum = reduce(output_grad, orders[1])
    kv_sum = reduce_parts(kv_grad)
    query_sum = reduce(query_grad, orders[0])
    vec = jnp.concatenate([media_vec, latent_vec, ffn_vec], axis=0)
    vec = vec.reshape(6, 2 * count, width // (2 * count)).transpose(1, 0, 2)
    vec_sum = reduce(vec, orders[2], F32)[0]
    return (
        new_latents.reshape(latents.shape),
        patches_grad.reshape(patches.shape),
        latents_grad.reshape(latents.shape),
        query_sum,
        kv_sum[:, :INNER],
        kv_sum[:, INNER:],
        output_sum,
        up_sum,
        down_sum,
        vec_sum[0],
        vec_sum[1],
        vec_sum[2],
        vec_sum[3],
        vec_sum[4],
        vec_sum[5],
    )


def fits(mesh):
    return mesh.shape["img"] == 16 and mesh.shape["lat"] == 2


def quick(
    count,
    patches,
    latents,
    cotangent,
    doc_images,
    doc_device,
    query_weight,
    key_weight,
    value_weight,
    output_weight,
    up_weight,
    down_weight,
    media_gain,
    media_bias,
    latent_gain,
    latent_bias,
    ffn_gain,
    ffn_bias,
):
    slots, own_patches, width = patches.shape
    own_latents = latents.shape[1]
    hidden = up_weight.shape[1]
    np_, nl = slots * own_patches, slots * own_latents
    patch = patches.reshape(np_, width)
    latent = latents.reshape(nl, width)
    cot = cotangent.reshape(nl, width)
    mg, mb = media_gain.reshape(1, width), media_bias.reshape(1, width)
    lg, lb = latent_gain.reshape(1, width), latent_bias.reshape(1, width)
    fg, fb = ffn_gain.reshape(1, width), ffn_bias.reshape(1, width)
    sspec = pl.BlockSpec(memory_space=pltpu.SMEM)
    vmem = pl.BlockSpec(memory_space=pltpu.VMEM)
    hbm = pl.BlockSpec(memory_space=pl.ANY)
    names, scratch = main_scratch(nl, np_, width, hidden)
    given = (
        latent, query_weight, cot, output_weight, patch, key_weight, value_weight, up_weight,
        down_weight, doc_images, doc_device, fg, fb, mg, mb, lg, lb,
    )
    fin, vec, patches_low, latents_low, new_latents = pl.pallas_call(
        partial(main_body, names),
        in_specs=[hbm] * 9 + [sspec] * 2 + [vmem] * 6,
        out_specs=[vmem, vmem, hbm, hbm, hbm],
        out_shape=[
            struct((10,) + BLOCK, F32),
            struct((8, width), F32),
            struct((np_, width), BF),
            struct((nl, width), BF),
            struct((nl, width), BF),
        ],
        scratch_shapes=scratch,
        compiler_params=pltpu.CompilerParams(
            collective_id=0, has_side_effects=True, vmem_limit_bytes=60 * 1024 * 1024
        ),
    )(*given)
    d = 2 * count
    small = [
        (width // d, hidden),
        (hidden // d, width),
        (width // d, INNER),
        (width // d, INNER),
        (INNER // d, width),
        (width // d, INNER),
    ] + [(1, width // d)] * 6
    parts = 8
    patches_grad, fresh, latents_out, up_sum, down_sum, key_sum, value_sum, out_sum, query_sum, *thin = pl.pallas_call(
        last_body,
        in_specs=[hbm] * 4 + [vmem],
        out_specs=[hbm] * 9 + [vmem] * 6,
        out_shape=[struct((np_, width), F32), struct((nl, width), BF), struct((nl, width), F32)]
        + [struct(shape, F32) for shape in small],
        scratch_shapes=[
            pltpu.VMEM((parts, np_ // parts, width), BF),
            pltpu.VMEM((parts, np_ // parts, width), F32),
            pltpu.VMEM((nl, width), BF),
            pltpu.VMEM((nl, width), F32),
            pltpu.VMEM((nl, width), BF),
            pltpu.VMEM((10,) + BLOCK, F32),
            pltpu.SemaphoreType.DMA((2 * parts + 18,)),
        ],
        compiler_params=pltpu.CompilerParams(vmem_limit_bytes=VMEM_LIMIT),
    )(patches_low, latents_low, new_latents, fin, vec)
    return (
        fresh.reshape(latents.shape),
        patches_grad.reshape(patches.shape),
        latents_out.reshape(latents.shape),
        query_sum,
        key_sum,
        value_sum,
        out_sum,
        up_sum,
        down_sum,
    ) + tuple(v.reshape(-1) for v in thin)


def solution(mesh):
    split = P("img", "lat", None)
    both = P(("img", "lat"), None)
    line = P(("img", "lat"))
    return jax.shard_map(
        partial(quick if fits(mesh) else local, mesh.shape["img"]),
        mesh=mesh,
        in_specs=(split,) * 3 + (P(),) * 14,
        out_specs=(split,) * 3 + (both,) * 6 + (line,) * 6,
        check_vma=False,
    )
```

```python
from functools import partial
from types import SimpleNamespace

import jax
import jax.numpy as jnp
from jax import lax
from jax.experimental import pallas as pl
from jax.experimental.pallas import tpu as pltpu
from jax.sharding import PartitionSpec as P

HEADS = 8
HEAD_DIM = 64
INNER = HEADS * HEAD_DIM
LANES = 128
EPS = 1e-05
BF = jnp.bfloat16
F32 = jnp.float32
VMEM_LIMIT = 56 * 1024 * 1024


def dot(a, b):
    return lax.dot_general(a, b, (((1,), (0,)), ((), ())), preferred_element_type=F32)


def dot_t(a, b):
    return lax.dot_general(a, b, (((1,), (1,)), ((), ())), preferred_element_type=F32)


def t_dot(a, b):
    return lax.dot_general(a, b, (((0,), (0,)), ((), ())), preferred_element_type=F32)


def call(body, grid, ins, outs, args, flops, scratch=()):
    moved = sum(a.size * a.dtype.itemsize for a in args)
    moved += sum(o[0].size * o[0].dtype.itemsize for o in outs)
    return pl.pallas_call(
        body,
        grid=grid,
        in_specs=ins,
        out_specs=[o[1] for o in outs],
        out_shape=[o[0] for o in outs],
        scratch_shapes=list(scratch),
        compiler_params=pltpu.CompilerParams(
            dimension_semantics=("arbitrary",) * len(grid), vmem_limit_bytes=VMEM_LIMIT
        ),
        cost_estimate=pl.CostEstimate(flops=flops, bytes_accessed=moved, transcendentals=0),
    )(*args)


def whole(shape):
    return pl.BlockSpec(shape, lambda *_: (0,) * len(shape))


def rows(block, width):
    return pl.BlockSpec((block, width), lambda i: (i, 0))


def cols(height, block):
    return pl.BlockSpec((height, block), lambda i: (0, i))


def struct(shape, dtype):
    return jax.ShapeDtypeStruct(shape, dtype)


def centred(v):
    centre = v - jnp.mean(v, axis=-1, keepdims=True)
    scale = lax.rsqrt(jnp.mean(centre * centre, axis=-1, keepdims=True) + EPS)
    return centre * scale, scale


def norm_back(unit, scale, gain, grad):
    push = grad * gain
    mean_push = jnp.mean(push, axis=-1, keepdims=True)
    mean_both = jnp.mean(push * unit, axis=-1, keepdims=True)
    return scale * (push - mean_push - unit * mean_both)


def column_sum(v):
    return jnp.sum(v, axis=0, keepdims=True)


def latent_body(latent, gain, bias, wq, norm, query):
    unit, _ = centred(latent[...].astype(F32))
    low = (unit * gain[...] + bias[...]).astype(BF)
    norm[...] = low
    query[...] = (HEAD_DIM**-0.5 * dot(low, wq[...])).astype(BF)


def media_body(patch, gain, bias, wk, wv, latent_norm, norm, kp, vp, kl, vl):
    @pl.when(pl.program_id(0) == 0)
    def _():
        kl[...] = dot(latent_norm[...], wk[...]).astype(BF)
        vl[...] = dot(latent_norm[...], wv[...]).astype(BF)

    unit, _ = centred(patch[...].astype(F32))
    low = (unit * gain[...] + bias[...]).astype(BF)
    norm[...] = low
    kp[...] = dot(low, wk[...]).astype(BF)
    vp[...] = dot(low, wv[...]).astype(BF)


def head_of(shape):
    return lax.broadcasted_iota(jnp.int32, shape, 1) // HEAD_DIM


def spread_rows(v):
    head = head_of(v.shape)
    zero = jnp.zeros_like(v)
    count = v.shape[1] // HEAD_DIM
    return jnp.concatenate([jnp.where(head == h, v, zero) for h in range(count)], axis=0)


def gather_rows(v):
    heads = v.shape[1] // HEAD_DIM
    count = v.shape[0] // heads
    head = head_of((count, v.shape[1]))
    total = v[:count]
    for h in range(1, heads):
        total = jnp.where(head == h, v[h * count : (h + 1) * count], total)
    return total


def head_groups():
    half = INNER // 2
    return [(g, slice(g * half, (g + 1) * half)) for g in range(2)]


def pack_lanes(columns, first=0):
    count = columns[0].shape[0]
    lane = lax.broadcasted_iota(jnp.int32, (count, LANES), 1)
    total = jnp.zeros((count, LANES), F32)
    for h, column in enumerate(columns):
        total = jnp.where(lane == first + h, column, total)
    return total


def widen(packed):
    head = head_of((packed.shape[0], INNER))
    total = jnp.zeros((packed.shape[0], INNER), F32)
    for h in range(HEADS):
        total = jnp.where(head == h, packed[:, h : h + 1], total)
    return total


def stack_heads(packed, offset, group):
    first = offset + group * HEADS // 2
    return jnp.concatenate([packed[:, c : c + 1] for c in range(first, first + HEADS // 2)], axis=0)


def attend_slots(slots):
    work = []
    for qo, qp, kp, vp, kl, vl, *_ in slots:
        queries = jnp.concatenate([qo[...], qp[...]], axis=0)
        for _, at in head_groups():
            big = spread_rows(queries[:, at])
            keys = jnp.concatenate([kp[:, at], kl[:, at]], axis=0)
            values = jnp.concatenate([vp[:, at], vl[:, at]], axis=0)
            work.append((big, keys, values))
    scores = [dot_t(big, keys) for big, keys, _ in work]
    tops = [jnp.max(v, axis=-1, keepdims=True) for v in scores]
    expos = [jnp.exp(v - top) for v, top in zip(scores, tops)]
    totals = [jnp.sum(v, axis=-1, keepdims=True) for v in expos]
    probs = [(v * (1.0 / total)).astype(BF) for v, total in zip(expos, totals)]
    outs = [gather_rows(dot(v, w[2])) for v, w in zip(probs, work)]
    logs = [top + jnp.log(total) for top, total in zip(tops, totals)]
    for k, (qo, _, _, _, _, _, oo, op, so, sp) in enumerate(slots):
        own = qo.shape[0]
        count = 2 * own
        columns = []
        for g, at in head_groups():
            out, log_total = outs[2 * k + g], logs[2 * k + g]
            columns += [log_total[h * count : (h + 1) * count] for h in range(HEADS // 2)]
            oo[:, at] = out[:own]
            op[:, at] = out[own:].astype(BF)
        packed = pack_lanes(columns)
        so[...] = packed[:own]
        sp[...] = packed[own:]


def attend_body(*refs):
    attend_slots([refs])


def forward_body(
    slot_rows,
    holding,
    oo,
    orecv,
    so,
    srecv,
    latent,
    cot,
    wo,
    wup,
    wdown,
    gain,
    bias,
    new_latents,
    act_out,
    pre_out,
    ffn_t,
    og_out,
    residual_grad,
    attended_grad,
    stats,
    output_grad,
    vectors,
    residual,
    ffn_in,
    acc,
    gacc,
    attended,
    packed,
):
    step = pl.program_id(0)
    count = latent.shape[0]
    slot = lax.broadcasted_iota(jnp.int32, (count, 1), 0) // slot_rows
    live = jnp.where(slot < holding[0, 0], 1.0, 0.0).astype(F32)

    @pl.when(step == 0)
    def _():
        a, b = so[...], srecv[...]
        top = jnp.maximum(a, b)
        both = top + jnp.log(jnp.exp(a - top) + jnp.exp(b - top))
        packed[...] = both
        mix = widen(jnp.exp(a - both)) * oo[...]
        mix += widen(jnp.exp(b - both)) * orecv[...].astype(F32)
        attended[...] = mix
        res = latent[...].astype(F32) + dot(mix.astype(BF), wo[...])
        residual[...] = res
        unit, _ = centred(res)
        low = (unit * gain[...] + bias[...]).astype(BF)
        ffn_in[...] = low
        ffn_t[...] = low.T
        og_out[...] = (cot[...].astype(F32) * live).astype(BF)
        acc[...] = jnp.zeros_like(acc)
        gacc[...] = jnp.zeros_like(gacc)

    pre = dot(ffn_in[...], wup[...])
    cdf = 0.5 * (1.0 + lax.erf(pre * (0.5**0.5)))
    act = (pre * cdf).astype(BF)
    act_out[...] = act
    acc[...] += dot(act, wdown[...])
    act_grad = dot_t(og_out[...], wdown[...])
    pdf = jnp.exp(-0.5 * pre * pre) * 0.3989422804014327
    pre_grad = (act_grad * (cdf + pre * pdf)).astype(BF)
    pre_out[...] = pre_grad
    gacc[...] += dot_t(pre_grad, wup[...])

    @pl.when(step == pl.num_programs(0) - 1)
    def _():
        res = residual[...]
        new_latents[...] = ((res + acc[...]) * live).astype(BF)
        unit, scale = centred(res)
        grad = gacc[...]
        vectors[0:1, :] = column_sum(grad * unit)
        vectors[1:2, :] = column_sum(grad)
        res_grad = og_out[...].astype(F32) + norm_back(unit, scale, gain[...], grad)
        residual_grad[...] = res_grad
        branch = res_grad.astype(BF)
        back = dot_t(branch, wo[...]).astype(BF)
        attended_grad[...] = back
        mix = attended[...]
        product = back.astype(F32) * mix
        head = head_of(product.shape)
        sums = [
            jnp.sum(jnp.where(head == h, product, 0.0), axis=-1, keepdims=True)
            for h in range(HEADS)
        ]
        delta = pack_lanes(sums, HEADS)
        lane = lax.broadcasted_iota(jnp.int32, delta.shape, 1)
        stats[...] = jnp.where(lane < HEADS, packed[...], delta)
        output_grad[...] = t_dot(mix.astype(BF), branch).astype(BF)


def attend_back_slots(slots):
    work = []
    for qo, qp, kp, vp, kl, vl, do, dp, so, sp, *_ in slots:
        queries = jnp.concatenate([qo[...], qp[...]], axis=0)
        grads = jnp.concatenate([do[...], dp[...]], axis=0)
        stats = jnp.concatenate([so[...], sp[...]], axis=0)
        for g, at in head_groups():
            big = spread_rows(queries[:, at])
            back = spread_rows(grads[:, at])
            keys = jnp.concatenate([kp[:, at], kl[:, at]], axis=0)
            values = jnp.concatenate([vp[:, at], vl[:, at]], axis=0)
            work.append(
                (big, back, keys, values, stack_heads(stats, 0, g), stack_heads(stats, HEADS, g))
            )
    scores = [dot_t(w[0], w[2]) for w in work]
    prob_grads = [dot_t(w[1], w[3]) for w in work]
    probs = [jnp.exp(v - w[4]) for v, w in zip(scores, work)]
    score_grads = [(v * (d - w[5])).astype(BF) for v, d, w in zip(probs, prob_grads, work)]
    values_grads = [t_dot(v.astype(BF), w[1]).astype(BF) for v, w in zip(probs, work)]
    keys_grads = [t_dot(v, w[0]).astype(BF) for v, w in zip(score_grads, work)]
    dqs = [gather_rows(dot(v, w[2])) for v, w in zip(score_grads, work)]
    for k, refs in enumerate(slots):
        own, patches = refs[0].shape[0], refs[2].shape[0]
        dkvp, dkvl, dqo, dqp = refs[10:]
        for g, at in head_groups():
            late = slice(INNER + at.start, INNER + at.stop)
            u = 2 * k + g
            dkvp[:, at] = keys_grads[u][:patches]
            dkvp[:, late] = values_grads[u][:patches]
            dkvl[:, at] = keys_grads[u][patches:]
            dkvl[:, late] = values_grads[u][patches:]
            dqo[:, at] = dqs[u][:own]
            dqp[:, at] = dqs[u][own:].astype(BF)


def attend_back_body(*refs):
    attend_back_slots([refs])


def up_grad_body(left, right, out):
    out[...] = dot(left[...], right[...]).astype(BF)


def down_grad_body(left, right, out):
    out[...] = t_dot(left[...], right[...]).astype(BF)


def kv_grad_body(media, latent, dkvp, dkvl, out):
    out[...] = (t_dot(media[...], dkvp[...]) + t_dot(latent[...], dkvl[...])).astype(BF)


def patch_back_body(patch, dkvp, wk, wv, gain, out, vectors):
    @pl.when(pl.program_id(0) == 0)
    def _():
        vectors[...] = jnp.zeros_like(vectors)

    grad = dot_t(dkvp[:, :INNER], wk[...]) + dot_t(dkvp[:, INNER:], wv[...])
    unit, scale = centred(patch[...].astype(F32))
    vectors[0:1, :] += column_sum(grad * unit)
    vectors[1:2, :] += column_sum(grad)
    out[...] = norm_back(unit, scale, gain[...], grad)


def latent_back_body(
    latent, norm, dkvl, dqo, drecv, residual_grad, wq, wk, wv, gain, out, query_grad, vectors
):
    dq = (dqo[...] + drecv[...].astype(F32)).astype(BF)
    product = (HEAD_DIM**-0.5 * t_dot(norm[...], dq)).astype(BF)
    if query_grad.shape == product.shape:
        query_grad[...] = product
    else:
        product = product.reshape(-1, 32, INNER)
        shape = query_grad.shape[:-1] + (INNER,)
        query_grad[..., :INNER] = product[:, :16].reshape(shape)
        query_grad[..., INNER:] = product[:, 16:].reshape(shape)
    grad = dot_t(dkvl[:, :INNER], wk[...]) + dot_t(dkvl[:, INNER:], wv[...])
    grad += HEAD_DIM**-0.5 * dot_t(dq, wq[...])
    unit, scale = centred(latent[...].astype(F32))
    vectors[0:1, :] = column_sum(grad * unit)
    vectors[1:2, :] = column_sum(grad)
    out[...] = residual_grad[...] + norm_back(unit, scale, gain[...], grad)


def ffn_back_body(
    residual, gacc, og, mix_ref, packed, wo, gain, residual_grad, attended_grad, stats, out, vectors
):
    unit, scale = centred(residual[...])
    grad = gacc[...]
    vectors[0:1, :] = column_sum(grad * unit)
    vectors[1:2, :] = column_sum(grad)
    res_grad = og[...].astype(F32) + norm_back(unit, scale, gain[...], grad)
    residual_grad[...] = res_grad
    branch = res_grad.astype(BF)
    back = dot_t(branch, wo[...]).astype(BF)
    attended_grad[...] = back
    mix = mix_ref[...]
    product = back.astype(F32) * mix
    head = head_of(product.shape)
    sums = [
        jnp.sum(jnp.where(head == h, product, 0.0), axis=-1, keepdims=True) for h in range(HEADS)
    ]
    delta = pack_lanes(sums, HEADS)
    lane = lax.broadcasted_iota(jnp.int32, delta.shape, 1)
    stats[...] = jnp.where(lane < HEADS, packed[...], delta)
    if out is not None:
        out[...] = t_dot(mix.astype(BF), branch).astype(BF).reshape(out.shape)


def plus(a, b):
    return a.astype(F32) + b.astype(F32)


class Names:
    def __getattr__(self, name):
        return name


n = Names()
STREAMS = ("d0", "d1", "d2", "d3", "u0", "u1", "u2", "u3", "K", "W", "Q")
ORDERS = {
    "d0": "zyxw", "d1": "zyxw", "d2": "zxyw", "d3": "ywzx", "u0": "xywz", "u1": "yzxw",
    "u2": "zwyx", "u3": "yxwz", "K": "zxyw", "W": "yzxw", "Q": "xywz",
}
PLAN = (
    "fi", "md0", "md1", "md2", "md3", "af0:4", "af4:6", "af6:8", "cb", "j0", "j1", "j2", "j3",
    "u0", "j4", "j5", "u1", "j6", "j7", "u2", "fb", "u3", "d0", "+u0", "d1", "+u1", "d2", "d3",
    "at0:8", "kv0", "+d2", "kv1", "+u2", "kv2", "+u3", "kv3", "+K", "+d3", "ow", "+u1", "lat",
    "+W", "+d0", "+u3", "pt0", "pt1", "+u0", "+Q", "+u1", "pt2", "pt3", "+u2", "+d0", "+d1",
    "+V", "+d2", "+u3", "+K", "+d3", "+W", "+u0", "+Q", "+u2", "+u1", "+d1", "+V", "+d0", "+K",
    "+d3", "+d2", "+Q", "+u3", "+V", "+u2", "+K", "+d1", "+W", "+u0", "+W", "+Q", "+V", "+K",
    "+W", "+Q", "+V",
)
DIMS = "wzyx"
DOWN_AXES = {ORDERS[s][0] for s in STREAMS if s[0] == "d"}
DIMS_ALL = "wzycx"
BLOCK = (32, 1024)
LOADED = (n.latent, n.wq, n.og, n.wo)
GIVEN = LOADED + (
    n.patch,
    n.wk, n.wv, n.wup, n.wdown, n.images, n.device, n.fg, n.fb, n.mg, n.mb, n.lg, n.lb,
)


def is_late(s):
    return s in "KWQ"


def main_scratch(nl, np_, width, hidden):
    def bf(*shape):
        return pltpu.VMEM(shape, BF)

    def f4(*shape):
        return pltpu.VMEM(shape, F32)

    step = hidden // 8
    turned = (2, 2, 2, 2, step // 4, nl)
    turned_in = (2, 2, 2, 2, 32, nl)
    items = [
        (n.latent, bf(nl, width)),
        (n.wq, bf(width, INNER)),
        (n.og, bf(nl, width)),
        (n.patch, bf(2, np_ // 4, width)),
        (n.wo, bf(INNER, width)),
        (n.oo, f4(nl, INNER)),
        (n.op, bf(nl, INNER)),
        (n.so, f4(nl, LANES)),
        (n.sp, f4(nl, LANES)),
        (n.sp_t, f4(HEADS, nl)),
        (n.orecv, bf(nl, INNER)),
        (n.srecv_t, f4(HEADS, nl)),
        (n.stats_t, f4(2 * HEADS, nl)),
        (n.stats_peer_t, f4(2 * HEADS, nl)),
        (n.q, bf(nl, INNER)),
        (n.q_peer, bf(nl, INNER)),
        (n.kp, bf(np_, INNER)),
        (n.vp, bf(np_, INNER)),
        (n.kl, bf(nl, INNER)),
        (n.vl, bf(nl, INNER)),
        (n.norm_l, bf(nl, width)),
        (n.norm_m, bf(np_, width)),
        (n.wu, bf(2, width, step)),
        (n.wd, bf(2, step, width)),
        (n.og_sib, bf(nl, width)),
        (n.act_own, bf(*turned)),
        (n.act_send, bf(*turned)),
        (n.act_sib, bf(*turned)),
        (n.ffn_own, bf(*turned_in)),
        (n.ffn_send, bf(*turned_in)),
        (n.ffn_sib, bf(*turned_in)),
        (n.residual, f4(nl, width)),
        (n.gacc, f4(nl, width)),
        (n.acc, f4(nl, width)),
        (n.ffn_in, bf(nl, width)),
        (n.attended, f4(nl, INNER)),
        (n.grad, bf(nl, INNER)),
        (n.stats, f4(nl, LANES)),
        (n.grad_peer, bf(nl, INNER)),
        (n.stats_peer, f4(nl, LANES)),
        (n.dkvp, bf(np_, 2 * INNER)),
        (n.dkvl, bf(nl, 2 * INNER)),
        (n.dq_peer, bf(nl, INNER)),
        (n.vs, f4(5, 8, width)),
        (n.vr, f4(5, 8, width)),
        (n.sums, f4(2, width)),
        (n.pre, bf(2, 2, 2, 2, 2, *BLOCK)),
        (n.pre_sib, bf(2, 2, 2, 2, 2, *BLOCK)),
    ]
    for s in STREAMS:
        if s[0] == "u":
            items.append((s, bf(2, 2, 2, 2, *BLOCK)))
        if s[0] == "d":
            items.append((s, bf(2, 2, 2, *BLOCK)))
            items += [(s + "_p", bf(2, 2, 2, 32, nl)), (s + "_q", bf(2, 2, 2, 32, nl))]
    for axis in sorted(DOWN_AXES):
        items += [("og_p" + axis, bf(nl, width)), ("og_q" + axis, bf(nl, width))]
    for s in STREAMS:
        wide = BLOCK[1] // 2 if s in "KW" else BLOCK[1]
        for k in range({"u": 3, "d": 2}.get(s[0], 4), -1, -1):
            items.append((s + "_%d" % k, bf(*((2,) * k), BLOCK[0], wide)))
    dma = pltpu.SemaphoreType.DMA
    items += [
        (n.load_sem, dma((len(LOADED) + 4,))),
        (n.weight_sem, dma((2, 2))),
        (n.store_sem, dma((6,))),
        (n.patch_sem, dma((2,))),
        (n.send_sem, dma((96,))),
        (n.recv_sem, dma((96,))),
    ]
    return [k for k, _ in items], [v for _, v in items]


def main_body(names, *refs):
    src = SimpleNamespace(**dict(zip(GIVEN, refs)))
    outs = len(GIVEN)
    fin, vec, patches_low, latents_grad, new_latents = refs[outs : outs + 5]
    t = SimpleNamespace(**dict(zip(names, refs[outs + 5 :])))
    load_sem, weight_sem, store_sem = t.load_sem, t.weight_sem, t.store_sem
    mine = lax.axis_index("img")
    xb = lax.axis_index("lat")
    bit = {"x": xb, "c": mine % 2, "y": (mine // 2) % 2, "z": (mine // 4) % 2, "w": (mine // 8) % 2}

    def to(axis, weight):
        return (mine + weight - 2 * weight * bit[axis], xb)

    peer = {"c": to("c", 1), "y": to("y", 2), "z": to("z", 4), "w": to("w", 8), "x": (mine, 1 - xb)}
    for axis in sorted(DOWN_AXES):
        beside = peer[axis][0] + 1 - 2 * bit["c"]
        peer["c" + axis] = (beside, peer[axis][1])
    barrier = pltpu.get_barrier_semaphore()
    for axis in peer:
        pl.semaphore_signal(
            barrier, inc=1, device_id=peer[axis], device_id_type=pl.DeviceIdType.MESH
        )

    step = t.wd.shape[1]
    count = t.og.shape[0]
    weights = {}

    def load_weights(j):
        slot = j % 2
        col = pl.ds(j * step, step)
        pair = (
            pltpu.make_async_copy(src.wup.at[:, col], t.wu.at[slot], weight_sem.at[0, slot]),
            pltpu.make_async_copy(src.wdown.at[col], t.wd.at[slot], weight_sem.at[1, slot]),
        )
        for copy in pair:
            copy.start()
        weights[j] = pair

    loads = {}

    def load(names):
        for name in names:
            i = LOADED.index(name)
            loads[name] = pltpu.make_async_copy(getattr(src, name), getattr(t, name), load_sem.at[i])
            loads[name].start()

    def load_kv(first):
        for i, name in enumerate((n.wk, n.wv)):
            loads[name] = pltpu.make_async_copy(
                getattr(src, name), t.wu.at[i], load_sem.at[len(LOADED) + first + i]
            )
            loads[name].start()

    size = src.patch.shape[0] // 4
    patch_loads = []

    def load_patch():
        i = len(patch_loads)
        copy = pltpu.make_async_copy(
            src.patch.at[pl.ds(i % 4 * size, size)], t.patch.at[i % 2], t.patch_sem.at[i % 2]
        )
        copy.start()
        patch_loads.append(copy)

    load(LOADED[:3])
    load_kv(0)
    load_patch()
    load_patch()
    load(LOADED[3:])

    def need(*names):
        for name in names:
            if name in loads:
                loads.pop(name).wait()

    used = []

    def send(source, target, axis):
        slot = len(used)
        copy = pltpu.make_async_remote_copy(
            src_ref=source,
            dst_ref=target,
            send_sem=t.send_sem.at[slot],
            recv_sem=t.recv_sem.at[slot],
            device_id=peer[axis],
            device_id_type=pl.DeviceIdType.MESH,
        )
        copy.start()
        used.append(copy)
        return copy

    arriving = {}

    def arrive(*names):
        for name in names:
            if name in arriving:
                arriving.pop(name).wait_recv()

    order = {s: ("c" if is_late(s) else "") + ORDERS[s] for s in STREAMS}
    place = {s: 1 if s[0] == "d" else 0 for s in STREAMS}
    half = BLOCK[1] // 2
    buffer = {s: getattr(t, s) for s in STREAMS if not is_late(s)}
    buffer["K"] = buffer["W"] = t.pre
    buffer["Q"] = t.pre_sib
    column = {"K": pl.ds(0, half), "W": pl.ds(half, half)}

    def where(s, axis, value):
        done = order[s][: place[s]]
        index = []
        for d in DIMS_ALL if is_late(s) else DIMS:
            if s[0] == "d" and d == order[s][0]:
                continue
            if d == axis:
                index.append(value)
            else:
                index.append(bit[d] if d in done else slice(None))
        if s in column:
            index += [slice(None), column[s]]
        return tuple(index)

    def got(s):
        return getattr(t, s + "_%d" % (len(order[s]) - 1 - place[s]))

    def start(s):
        axis = order[s][place[s]]
        arriving[s] = send(buffer[s].at[where(s, axis, 1 - bit[axis])], got(s), axis)

    def take(s):
        axis = order[s][place[s]]
        arrive(s)
        if s == "Q" and place[s] == 0:
            arrive(n.O)
        at = where(s, axis, bit[axis])
        total = plus(buffer[s][at], got(s)[...])
        place[s] += 1
        if place[s] < len(order[s]):
            buffer[s][at] = total.astype(BF)
            start(s)
        elif s in column:
            fin[8, :, column[s]] = total
        else:
            fin[9 if s == "Q" else STREAMS.index(s)] = total

    vs, vr = t.vs, t.vr
    vec_order = "cxyzw"
    vec_place = [0]

    def take_vector():
        i = vec_place[0]
        arrive(n.V)
        if i < 4:
            vs[i + 1] = vs[i] + vr[i]
            arriving["V"] = send(vs.at[i + 1], vr.at[i + 1], vec_order[i + 1])
        else:
            vec[...] = vs[i] + vr[i]
        vec_place[0] += 1

    stores = []

    def store(source, target):
        slot = len(stores)
        stores.append(pltpu.make_async_copy(source, target, store_sem.at[slot]))
        stores[slot].start()

    core = bit["c"]
    def live_rows():
        total = jnp.int32(0)
        for i in range(src.images.shape[0]):
            total += jnp.where(src.device[i] == mine, src.images[i], 0)
        slot = lax.broadcasted_iota(jnp.int32, (count, 1), 0) // (count // 8)
        return jnp.where(slot < total, 1.0, 0.0).astype(F32)

    def share_og(axes):
        for axis in sorted(DOWN_AXES.intersection(axes)):
            arriving["og_p" + axis] = send(t.og, getattr(t, "og_p" + axis), axis)

    def pass_og(axes):
        for axis in sorted(DOWN_AXES.intersection(axes)):
            name = "og_p" + axis
            arrive(name)
            arriving["og_q" + axis] = send(getattr(t, name), getattr(t, "og_q" + axis), "c")

    def first():
        need(n.latent, n.wq)
        part = count // 2
        for i in range(2):
            at = pl.ds(i * part, part)
            unit, _ = centred(t.latent[at].astype(F32))
            low = (unit * src.lg[...] + src.lb[...]).astype(BF)
            t.norm_l[at] = low
            t.q[at] = (HEAD_DIM**-0.5 * dot(low, t.wq[...])).astype(BF)
            if i == 0:
                pl.semaphore_wait(barrier, len(peer))
            arriving["q%d" % i] = send(t.q.at[at], t.q_peer.at[at], "x")
        low = t.norm_l[...]
        need(n.og, n.wk, n.wv)
        t.og[...] = (t.og[...].astype(F32) * live_rows()).astype(BF)
        arriving[n.og_sib] = send(t.og, t.og_sib, "c")
        share_og("yz")
        t.kl[...] = dot(low, t.wu[0]).astype(BF)
        t.vl[...] = dot(low, t.wu[1]).astype(BF)

    def media(i):
        patch_loads[i].wait()
        at = pl.ds(i * size, size)
        unit, _ = centred(t.patch[i % 2].astype(F32))
        low = (unit * src.mg[...] + src.mb[...]).astype(BF)
        t.norm_m[at] = low
        t.kp[at] = dot(low, t.wu[0]).astype(BF)
        t.vp[at] = dot(low, t.wu[1]).astype(BF)
        load_patch()
        if i == 3:
            load_weights(0)
            load_weights(1)

    def slot_rows(i):
        lat, med = count // 8, t.kp.shape[0] // 8
        return (
            pl.ds(pl.multiple_of(i * lat, lat), lat),
            pl.ds(pl.multiple_of(i * med, med), med),
        )

    def attend(first, last):
        arrive("q0")
        if last > 4:
            arrive("q1")

        def refs(i):
            a, b = slot_rows(i)
            return (
                t.q.at[a], t.q_peer.at[a], t.kp.at[b], t.vp.at[b], t.kl.at[a], t.vl.at[a],
                t.oo.at[a], t.op.at[a], t.so.at[a], t.sp.at[a],
            )

        @pl.loop(first // 2, last // 2)
        def _(i):
            attend_slots([refs(2 * i), refs(2 * i + 1)])

        at = pl.ds(first * (count // 8), (last - first) * (count // 8))
        arriving["o%d" % first] = send(t.op.at[at], t.orecv.at[at], "x")
        if last % 4 == 0:
            at = pl.ds((last - 4) * (count // 8), count // 2)
            t.sp_t[:, at] = t.sp[at].T[:HEADS]
            arriving["s%d" % first] = send(t.sp_t.at[:, at], t.srecv_t.at[:, at], "x")
        if last == 8:
            share_og("x")

    def combine():
        pass_og("yz")
        need(n.wo)
        for name in list(arriving):
            if name[0] in "os" and name[1:].isdigit():
                arrive(name)
        a, b = t.so[:, :HEADS], t.srecv_t[...].T
        top = jnp.maximum(a, b)
        both = top + jnp.log(jnp.exp(a - top) + jnp.exp(b - top))
        t.so[:, :HEADS] = both
        mix = widen(jnp.exp(a - both)) * t.oo[...]
        mix += widen(jnp.exp(b - both)) * t.orecv[...].astype(F32)
        t.attended[...] = mix
        res = t.latent[...].astype(F32) + dot(mix.astype(BF), t.wo[...])
        t.residual[...] = res
        unit, _ = centred(res)
        low = (unit * src.fg[...] + src.fb[...]).astype(BF)
        t.ffn_in[...] = low
        turned = low.T.reshape(8, 2, -1, count)
        even, odd = turned[:, 0], turned[:, 1]
        shape = t.ffn_own.shape
        t.ffn_own[...] = jnp.where(core == 0, even, odd).reshape(shape)
        t.ffn_send[...] = jnp.where(core == 0, odd, even).reshape(shape)
        arriving[n.ffn_sib] = send(t.ffn_send, t.ffn_sib, "c")

    def ffn(j):
        for copy in weights.pop(j):
            copy.wait()
        wup, wdown = t.wu[j % 2], t.wd[j % 2]
        pre = dot(t.ffn_in[...], wup)
        cdf = 0.5 * (1.0 + lax.erf(pre * (0.5**0.5)))
        pdf = jnp.exp(-0.5 * pre * pre) * 0.3989422804014327
        act = (pre * cdf).astype(BF)
        turned = act.T
        even, odd = turned[: step // 2], turned[step // 2 :]
        at = (j // 4, (j // 2) % 2, j % 2)
        shape = t.act_own.shape[3:]
        t.act_own[at] = jnp.where(core == 0, even, odd).reshape(shape)
        t.act_send[at] = jnp.where(core == 0, odd, even).reshape(shape)
        arriving["act%d" % j] = send(t.act_send.at[at], t.act_sib.at[at], "c")
        down = dot(act, wdown)
        act_grad = dot_t(t.og[...], wdown)
        pre_grad = (act_grad * (cdf + pre * pdf)).astype(BF)
        group = (j // 4, (j // 2) % 2)
        t.pre[group + (slice(None),) * 4 + (pl.ds((j % 2) * step, step),)] = pre_grad.reshape(
            2, 2, 2, 32, step
        )
        if j % 2 == 1:
            name = "pre%d" % (j // 2)
            arriving[name] = send(t.pre.at[group], t.pre_sib.at[group], "c")
            pre_sent.append(len(used) - 1)
        back = dot_t(pre_grad, wup)
        if j == 0:
            t.acc[...] = down
            t.gacc[...] = back
        else:
            t.acc[...] += down
            t.gacc[...] += back
        if j in (3, 7):
            for g in range(4):
                s = "d%d" % g
                axis = order[s][0]
                at = tuple(1 - bit[d] if d == axis else slice(None) for d in DIMS[1:])
                at = (j // 4,) + at + (pl.ds(g * 32, 32),)
                p, q = getattr(t, s + "_p").at[j // 4], getattr(t, s + "_q").at[j // 4]
                arriving[s + "_p%d" % j] = send(t.act_own.at[at], p, axis)
                arriving[s + "_q%d" % j] = send(t.act_send.at[at], q, "c" + axis)
        if j < 6:
            load_weights(j + 2)
        if j == 7:
            pass_og("x")
            load_kv(2)
            t.ffn_in[...] = ((t.residual[...] + t.acc[...]) * live_rows()).astype(BF)
            store(t.ffn_in, new_latents)

    pre_sent = []

    def ffn_back():
        ffn_back_body(
            t.residual, t.gacc, t.og, t.attended, t.so, t.wo, src.fg,
            t.residual, t.grad, t.stats, None, vs.at[0, pl.ds(4, 2)],
        )
        arriving[n.grad_peer] = send(t.grad, t.grad_peer, "x")
        t.stats_t[...] = t.stats[...].T[: 2 * HEADS]
        arriving[n.stats_peer] = send(t.stats_t, t.stats_peer_t, "x")

    def send_late(rows, name):
        o, r = buffer["Q"], t.Q_4
        arriving[name] = send(
            o.at[:, :, :, 1 - core, :, rows], r.at[:, :, :, :, rows], "c"
        )

    def output_group():
        product = t_dot(t.attended[...].astype(BF), t.residual[...].astype(BF)).astype(BF)
        buffer["Q"][..., pl.ds(0, 16), :] = product.reshape(2, 2, 2, 2, 2, 16, BLOCK[1])
        send_late(pl.ds(0, 16), "O")

    def rows_of(ref, at):
        v = ref[at]
        return v.reshape(-1, v.shape[-1])

    def down_group(g):
        s = "d%d" % g
        axis = order[s][0]
        arrive(n.og_sib, "og_q" + axis, *("act%d" % j for j in range(8)))
        arrive(*(s + end for end in ("_p3", "_q3", "_p7", "_q7")))
        at = tuple(bit[d] if d == axis else slice(None) for d in DIMS) + (pl.ds(g * 32, 32),)
        v = dot(rows_of(t.act_own, at), t.og[...])
        v += dot(rows_of(t.act_sib, at), t.og_sib[...])
        every = (slice(None),)
        v += dot(rows_of(getattr(t, s + "_p"), every), getattr(t, "og_p" + axis)[...])
        v += dot(rows_of(getattr(t, s + "_q"), every), getattr(t, "og_q" + axis)[...])
        buffer[s][...] = v.astype(BF).reshape((2, 2, 2) + BLOCK)
        start(s)

    def up_group(g):
        s = "u%d" % g
        arrive(n.ffn_sib, "pre%d" % g)
        axis = order[s][0]
        group = (g // 2, g % 2)
        for value in (1 - bit[axis], bit[axis]):
            at = where(s, axis, value)
            v = dot(rows_of(t.ffn_own, at), rows_of(t.pre, group))
            v += dot(rows_of(t.ffn_sib, at), rows_of(t.pre_sib, group))
            buffer[s][at] = v.astype(BF).reshape((2, 2, 2) + BLOCK)
            if s not in arriving:
                start(s)

    def attend_back(first, last):
        if n.stats_peer in arriving:
            arrive(n.grad_peer, n.stats_peer)
            t.stats_peer[:, : 2 * HEADS] = t.stats_peer_t[...].T

        def refs(i):
            a, b = slot_rows(i)
            return (
                t.q.at[a], t.q_peer.at[a], t.kp.at[b], t.vp.at[b], t.kl.at[a], t.vl.at[a],
                t.grad.at[a], t.grad_peer.at[a], t.stats.at[a], t.stats_peer.at[a],
                t.dkvp.at[b], t.dkvl.at[a], t.oo.at[a], t.dq_peer.at[a],
            )

        @pl.loop(first // 2, last // 2)
        def _(i):
            attend_back_slots([refs(2 * i), refs(2 * i + 1)])

        if last == 8:
            arriving[n.dq_recv] = send(t.dq_peer, t.orecv, "x")

    def kv_group(g):
        while pre_sent:
            slot = pre_sent.pop()
            used[slot].wait_send()
            used[slot] = None
        col = pl.ds(g * 256, 256)
        v = t_dot(t.norm_m[...], t.dkvp[:, col])
        v += t_dot(t.norm_l[...], t.dkvl[:, col])
        buffer["K"][..., col] = v.astype(BF).reshape(2, 2, 2, 2, 2, 32, 256)
        if g == 1:
            start("K")
        if g == 3:
            start("W")

    def latent_back():
        need(n.wk, n.wv)
        arrive(n.dq_recv)
        latent_back_body(
            t.latent, t.norm_l, t.dkvl, t.oo, t.orecv, t.residual,
            t.wq, t.wu.at[0], t.wu.at[1], src.lg, t.residual,
            buffer["Q"].at[..., pl.ds(16, 16), :], vs.at[0, pl.ds(2, 2)],
        )
        send_late(pl.ds(16, 16), "Q")
        stores[0].wait()
        stores[0] = None
        t.ffn_in[...] = t.residual[...].astype(BF)
        store(t.ffn_in, latents_grad)

    def patch_back(i):
        need(n.wk, n.wv)
        at = pl.ds(i * size, size)
        dkv = t.dkvp
        grad = dot_t(dkv[at, :INNER], t.wu[0]) + dot_t(dkv[at, INNER:], t.wu[1])
        patch_loads[4 + i].wait()
        unit, scale = centred(t.patch[i % 2].astype(F32))
        sums = t.sums
        a, b = column_sum(grad * unit), column_sum(grad)
        if i > 0:
            a, b = a + sums[0:1, :], b + sums[1:2, :]
        sums[0:1, :] = a
        sums[1:2, :] = b
        dkv[at] = norm_back(unit, scale, src.mg[...], grad).astype(BF)
        store(dkv.at[at], patches_low.at[at])
        if i < 2:
            load_patch()
        if i == 3:
            vs[0, 0:2, :] = sums[...]
            vs[0, 6:8, :] = jnp.zeros((2, vs.shape[2]), F32)
            arriving["V"] = send(vs.at[0], vr.at[0], vec_order[0])

    simple = {"fi": first, "cb": combine, "fb": ffn_back, "ow": output_group, "lat": latent_back}
    simple["+V"] = take_vector
    for item in PLAN:
        if item in simple:
            simple[item]()
        elif item[0] == "+":
            take(item[1:])
        elif item[:2] == "at":
            a, b = item[2:].split(":")
            attend_back(int(a), int(b))
        elif item[:2] == "af":
            a, b = item[2:].split(":")
            attend(int(a), int(b))
        elif item[:2] == "md":
            media(int(item[2:]))
        elif item[:2] == "kv":
            kv_group(int(item[2:]))
        elif item[:2] == "pt":
            patch_back(int(item[2:]))
        else:
            {"j": ffn, "d": down_group, "u": up_group}[item[0]](int(item[1:]))
    for copy in stores:
        if copy is not None:
            copy.wait()
    for copy in used:
        if copy is not None:
            copy.wait_send()


def last_body(
    patches_in, latents_in, fresh, fin, vec,
    patches_grad, new_latents, latents_grad, up, down, key, value, out, query, *rest,
):
    thin, (pin, pout, lin, lout, nin, held, sem) = rest[:6], rest[6:]
    copies = []

    def move(source, target):
        copies.append(pltpu.make_async_copy(source, target, sem.at[len(copies)]))
        copies[-1].start()
        return copies[-1]

    parts = pin.shape[0]
    size = pin.shape[1]
    waits = [move(patches_in.at[pl.ds(i * size, size)], pin.at[i]) for i in range(parts)]
    waits += [move(fin, held), move(latents_in, lin), move(fresh, nin)]
    for i in range(parts):
        waits[i].wait()
        pout[i] = pin[i].astype(F32)
        move(pout.at[i], patches_grad.at[pl.ds(i * size, size)])
    waits[parts].wait()
    for g in range(4):
        move(held.at[4 + g], up.at[:, pl.ds(g * 1024, 1024)])
        move(held.at[g], down.at[pl.ds(g * 32, 32)])
    move(held.at[8, :, pl.ds(0, INNER)], key)
    move(held.at[8, :, pl.ds(INNER, INNER)], value)
    move(held.at[9, pl.ds(0, 16)], out)
    for k in range(2):
        move(held.at[9, pl.ds(16, 16), pl.ds(k * INNER, INNER)], query.at[pl.ds(k * 16, 16)])
    waits[parts + 1].wait()
    lout[...] = lin[...].astype(F32)
    move(lout, latents_grad)
    waits[parts + 2].wait()
    move(nin, new_latents)
    place = lax.axis_index("img") * 2 + lax.axis_index("lat")
    width = vec.shape[1]
    turned = pltpu.roll(vec[...], width - place * 32, 1)
    for i, ref in enumerate(thin):
        ref[...] = turned[i : i + 1, :32]
    for copy in copies[len(waits) :]:
        copy.wait()


def swap_lat(v):
    return lax.ppermute(v, "lat", [(0, 1), (1, 0)])


def halving_sum(v, order, bits, count, keep):
    left = list(range(bits - 1, -1, -1)) + [-1]
    mine = lax.axis_index("img")
    for place, axis in enumerate(order):
        dim = left.index(axis)
        if axis < 0:
            bit = lax.axis_index("lat")
            pairs, name = [(0, 1), (1, 0)], "lat"
        else:
            bit = (mine // 2**axis) % 2
            pairs, name = [(i, i ^ 2**axis) for i in range(count)], "img"
        out = lax.dynamic_index_in_dim(v, 1 - bit, dim, keepdims=False)
        stay = lax.dynamic_index_in_dim(v, bit, dim, keepdims=False)
        got = lax.ppermute(out, name, pairs)
        v = stay.astype(F32) + got.astype(F32)
        if place < len(order) - 1 and keep == BF:
            v = v.astype(BF)
        left.pop(dim)
    return v


def local(
    count,
    patches,
    latents,
    cotangent,
    doc_images,
    doc_device,
    query_weight,
    key_weight,
    value_weight,
    output_weight,
    up_weight,
    down_weight,
    media_gain,
    media_bias,
    latent_gain,
    latent_bias,
    ffn_gain,
    ffn_bias,
):
    slots, own_patches, width = patches.shape
    own_latents = latents.shape[1]
    hidden = up_weight.shape[1]
    np_, nl = slots * own_patches, slots * own_latents
    mine = lax.axis_index("img")
    holding = jnp.sum(jnp.where(doc_device == mine, doc_images, 0)).reshape(1, 1)
    patch = patches.reshape(np_, width)
    latent = latents.reshape(nl, width)
    cot = cotangent.reshape(nl, width)
    mg, mb = media_gain.reshape(1, width), media_bias.reshape(1, width)
    lg, lb = latent_gain.reshape(1, width), latent_bias.reshape(1, width)
    fg, fb = ffn_gain.reshape(1, width), ffn_bias.reshape(1, width)
    wspec = whole((width, INNER))
    vspec = whole((1, width))
    lspec = whole((nl, width))

    norm_l, query = call(
        latent_body,
        (1,),
        [lspec, vspec, vspec, wspec],
        [(struct((nl, width), BF), lspec), (struct((nl, INNER), BF), whole((nl, INNER)))],
        (latent, lg, lb, query_weight),
        2 * nl * width * INNER,
    )
    query_peer = swap_lat(query)
    blk = min(np_, 256)
    norm_m, kp, vp, kl, vl = call(
        media_body,
        (np_ // blk,),
        [rows(blk, width), vspec, vspec, wspec, wspec, lspec],
        [
            (struct((np_, width), BF), rows(blk, width)),
            (struct((np_, INNER), BF), rows(blk, INNER)),
            (struct((np_, INNER), BF), rows(blk, INNER)),
            (struct((nl, INNER), BF), whole((nl, INNER))),
            (struct((nl, INNER), BF), whole((nl, INNER))),
        ],
        (patch, mg, mb, key_weight, value_weight, norm_l),
        4 * (np_ + nl) * width * INNER,
    )
    q_s, p_s, s_s = rows(own_latents, INNER), rows(own_patches, INNER), rows(own_latents, LANES)
    att_flops = 4 * slots * (own_patches + own_latents) * INNER * INNER
    o_own, o_peer, s_own, s_peer = call(
        attend_body,
        (slots,),
        [q_s, q_s, p_s, p_s, q_s, q_s],
        [
            (struct((nl, INNER), F32), q_s),
            (struct((nl, INNER), BF), q_s),
            (struct((nl, LANES), F32), s_s),
            (struct((nl, LANES), F32), s_s),
        ],
        (query, query_peer, kp, vp, kl, vl),
        att_flops,
    )
    o_recv, s_recv = swap_lat(o_peer), swap_lat(s_peer)
    fblk = min(hidden, 512)
    nspec = whole((nl, INNER))
    (
        new_latents,
        act,
        pre_grad,
        ffn_t,
        out_grad,
        residual_grad,
        attended_grad,
        stats,
        output_grad,
        ffn_vec,
    ) = call(
        partial(forward_body, own_latents),
        (hidden // fblk,),
        [
            pl.BlockSpec(memory_space=pltpu.SMEM),
            nspec,
            nspec,
            whole((nl, LANES)),
            whole((nl, LANES)),
            lspec,
            lspec,
            whole((INNER, width)),
            cols(width, fblk),
            rows(fblk, width),
            vspec,
            vspec,
        ],
        [
            (struct((nl, width), BF), lspec),
            (struct((nl, hidden), BF), cols(nl, fblk)),
            (struct((nl, hidden), BF), cols(nl, fblk)),
            (struct((width, nl), BF), whole((width, nl))),
            (struct((nl, width), BF), lspec),
            (struct((nl, width), F32), lspec),
            (struct((nl, INNER), BF), nspec),
            (struct((nl, LANES), F32), whole((nl, LANES))),
            (struct((INNER, width), BF), whole((INNER, width))),
            (struct((2, width), F32), whole((2, width))),
        ],
        (
            holding,
            o_own,
            o_recv,
            s_own,
            s_recv,
            latent,
            cot,
            output_weight,
            up_weight,
            down_weight,
            fg,
            fb,
        ),
        8 * nl * width * hidden,
        scratch=[
            pltpu.VMEM((nl, width), F32),
            pltpu.VMEM((nl, width), BF),
            pltpu.VMEM((nl, width), F32),
            pltpu.VMEM((nl, width), F32),
            pltpu.VMEM((nl, INNER), F32),
            pltpu.VMEM((nl, LANES), F32),
        ],
    )
    grad_peer, stats_peer = swap_lat(attended_grad), swap_lat(stats)
    (down_grad,) = call(
        down_grad_body,
        (hidden // fblk,),
        [cols(nl, fblk), lspec],
        [(struct((hidden, width), BF), rows(fblk, width))],
        (act, out_grad),
        2 * nl * width * hidden,
    )
    (up_grad,) = call(
        up_grad_body,
        (hidden // fblk,),
        [whole((width, nl)), cols(nl, fblk)],
        [(struct((width, hidden), BF), cols(width, fblk))],
        (ffn_t, pre_grad),
        2 * nl * width * hidden,
    )
    dkvp, dkvl, dq_own, dq_peer = call(
        attend_back_body,
        (slots,),
        [q_s, q_s, p_s, p_s, q_s, q_s, q_s, q_s, s_s, s_s],
        [
            (struct((np_, 2 * INNER), BF), rows(own_patches, 2 * INNER)),
            (struct((nl, 2 * INNER), BF), rows(own_latents, 2 * INNER)),
            (struct((nl, INNER), F32), q_s),
            (struct((nl, INNER), BF), q_s),
        ],
        (query, query_peer, kp, vp, kl, vl, attended_grad, grad_peer, stats, stats_peer),
        att_flops * 5 // 2,
    )
    dq_recv = swap_lat(dq_peer)
    kblk = 256
    (kv_grad,) = call(
        kv_grad_body,
        (2 * INNER // kblk,),
        [whole((np_, width)), lspec, cols(np_, kblk), cols(nl, kblk)],
        [(struct((width, 2 * INNER), BF), cols(width, kblk))],
        (norm_m, norm_l, dkvp, dkvl),
        4 * (np_ + nl) * width * INNER,
    )
    patches_grad, media_vec = call(
        patch_back_body,
        (np_ // blk,),
        [rows(blk, width), rows(blk, 2 * INNER), wspec, wspec, vspec],
        [(struct((np_, width), F32), rows(blk, width)), (struct((2, width), F32), whole((2, width)))],
        (patch, dkvp, key_weight, value_weight, mg),
        4 * np_ * width * INNER,
    )
    latents_grad, query_grad, latent_vec = call(
        latent_back_body,
        (1,),
        [
            lspec,
            lspec,
            whole((nl, 2 * INNER)),
            nspec,
            nspec,
            lspec,
            wspec,
            wspec,
            wspec,
            vspec,
        ],
        [
            (struct((nl, width), F32), lspec),
            (struct((width, INNER), BF), wspec),
            (struct((2, width), F32), whole((2, width))),
        ],
        (
            latent,
            norm_l,
            dkvl,
            dq_own,
            dq_recv,
            residual_grad,
            query_weight,
            key_weight,
            value_weight,
            lg,
        ),
        8 * nl * width * INNER,
    )

    bits = count.bit_length() - 1
    first = list(range(1, bits))
    orders = (
        [0, -1] + first,
        [0] + first + [-1],
        [0] + first[1:] + [-1] + first[:1],
    )

    def reduce(v, order, keep=BF):
        shape = (2,) * (bits + 1) + (v.shape[0] // (2 * count),) + v.shape[1:]
        return halving_sum(v.reshape(shape), order, bits, count, keep)

    def reduce_parts(v):
        unit = v.shape[1] // 8
        cuts = (0, 3 * unit, 6 * unit, 8 * unit)
        return jnp.concatenate(
            [reduce(v[:, a:b], order) for a, b, order in zip(cuts, cuts[1:], orders)], axis=1
        )

    down_sum = reduce_parts(down_grad)
    up_sum = reduce_parts(up_grad)
    output_sum = reduce(output_grad, orders[1])
    kv_sum = reduce_parts(kv_grad)
    query_sum = reduce(query_grad, orders[0])
    vec = jnp.concatenate([media_vec, latent_vec, ffn_vec], axis=0)
    vec = vec.reshape(6, 2 * count, width // (2 * count)).transpose(1, 0, 2)
    vec_sum = reduce(vec, orders[2], F32)[0]
    return (
        new_latents.reshape(latents.shape),
        patches_grad.reshape(patches.shape),
        latents_grad.reshape(latents.shape),
        query_sum,
        kv_sum[:, :INNER],
        kv_sum[:, INNER:],
        output_sum,
        up_sum,
        down_sum,
        vec_sum[0],
        vec_sum[1],
        vec_sum[2],
        vec_sum[3],
        vec_sum[4],
        vec_sum[5],
    )


def fits(mesh):
    return mesh.shape["img"] == 16 and mesh.shape["lat"] == 2


def quick(
    count,
    patches,
    latents,
    cotangent,
    doc_images,
    doc_device,
    query_weight,
    key_weight,
    value_weight,
    output_weight,
    up_weight,
    down_weight,
    media_gain,
    media_bias,
    latent_gain,
    latent_bias,
    ffn_gain,
    ffn_bias,
):
    slots, own_patches, width = patches.shape
    own_latents = latents.shape[1]
    hidden = up_weight.shape[1]
    np_, nl = slots * own_patches, slots * own_latents
    patch = patches.reshape(np_, width)
    latent = latents.reshape(nl, width)
    cot = cotangent.reshape(nl, width)
    mg, mb = media_gain.reshape(1, width), media_bias.reshape(1, width)
    lg, lb = latent_gain.reshape(1, width), latent_bias.reshape(1, width)
    fg, fb = ffn_gain.reshape(1, width), ffn_bias.reshape(1, width)
    sspec = pl.BlockSpec(memory_space=pltpu.SMEM)
    vmem = pl.BlockSpec(memory_space=pltpu.VMEM)
    hbm = pl.BlockSpec(memory_space=pl.ANY)
    names, scratch = main_scratch(nl, np_, width, hidden)
    given = (
        latent, query_weight, cot, output_weight, patch, key_weight, value_weight, up_weight,
        down_weight, doc_images, doc_device, fg, fb, mg, mb, lg, lb,
    )
    fin, vec, patches_low, latents_low, new_latents = pl.pallas_call(
        partial(main_body, names),
        in_specs=[hbm] * 9 + [sspec] * 2 + [vmem] * 6,
        out_specs=[vmem, vmem, hbm, hbm, hbm],
        out_shape=[
            struct((10,) + BLOCK, F32),
            struct((8, width), F32),
            struct((np_, width), BF),
            struct((nl, width), BF),
            struct((nl, width), BF),
        ],
        scratch_shapes=scratch,
        compiler_params=pltpu.CompilerParams(
            collective_id=0, has_side_effects=True, vmem_limit_bytes=60 * 1024 * 1024
        ),
    )(*given)
    d = 2 * count
    small = [
        (width // d, hidden),
        (hidden // d, width),
        (width // d, INNER),
        (width // d, INNER),
        (INNER // d, width),
        (width // d, INNER),
    ] + [(1, width // d)] * 6
    parts = 8
    patches_grad, fresh, latents_out, up_sum, down_sum, key_sum, value_sum, out_sum, query_sum, *thin = pl.pallas_call(
        last_body,
        in_specs=[hbm] * 4 + [vmem],
        out_specs=[hbm] * 9 + [vmem] * 6,
        out_shape=[struct((np_, width), F32), struct((nl, width), BF), struct((nl, width), F32)]
        + [struct(shape, F32) for shape in small],
        scratch_shapes=[
            pltpu.VMEM((parts, np_ // parts, width), BF),
            pltpu.VMEM((parts, np_ // parts, width), F32),
            pltpu.VMEM((nl, width), BF),
            pltpu.VMEM((nl, width), F32),
            pltpu.VMEM((nl, width), BF),
            pltpu.VMEM((10,) + BLOCK, F32),
            pltpu.SemaphoreType.DMA((2 * parts + 18,)),
        ],
        compiler_params=pltpu.CompilerParams(vmem_limit_bytes=VMEM_LIMIT),
    )(patches_low, latents_low, new_latents, fin, vec)
    return (
        fresh.reshape(latents.shape),
        patches_grad.reshape(patches.shape),
        latents_out.reshape(latents.shape),
        query_sum,
        key_sum,
        value_sum,
        out_sum,
        up_sum,
        down_sum,
    ) + tuple(v.reshape(-1) for v in thin)


def solution(mesh):
    split = P("img", "lat", None)
    both = P(("img", "lat"), None)
    line = P(("img", "lat"))
    return jax.shard_map(
        partial(quick if fits(mesh) else local, mesh.shape["img"]),
        mesh=mesh,
        in_specs=(split,) * 3 + (P(),) * 14,
        out_specs=(split,) * 3 + (both,) * 6 + (line,) * 6,
        check_vma=False,
    )
```

```python
from functools import partial
from types import SimpleNamespace

import jax
import jax.numpy as jnp
from jax import lax
from jax.experimental import pallas as pl
from jax.experimental.pallas import tpu as pltpu
from jax.sharding import PartitionSpec as P

HEADS = 8
HEAD_DIM = 64
INNER = HEADS * HEAD_DIM
LANES = 128
EPS = 1e-05
BF = jnp.bfloat16
F32 = jnp.float32
VMEM_LIMIT = 56 * 1024 * 1024


def dot(a, b):
    return lax.dot_general(a, b, (((1,), (0,)), ((), ())), preferred_element_type=F32)


def dot_t(a, b):
    return lax.dot_general(a, b, (((1,), (1,)), ((), ())), preferred_element_type=F32)


def t_dot(a, b):
    return lax.dot_general(a, b, (((0,), (0,)), ((), ())), preferred_element_type=F32)


def call(body, grid, ins, outs, args, flops, scratch=()):
    moved = sum(a.size * a.dtype.itemsize for a in args)
    moved += sum(o[0].size * o[0].dtype.itemsize for o in outs)
    return pl.pallas_call(
        body,
        grid=grid,
        in_specs=ins,
        out_specs=[o[1] for o in outs],
        out_shape=[o[0] for o in outs],
        scratch_shapes=list(scratch),
        compiler_params=pltpu.CompilerParams(
            dimension_semantics=("arbitrary",) * len(grid), vmem_limit_bytes=VMEM_LIMIT
        ),
        cost_estimate=pl.CostEstimate(flops=flops, bytes_accessed=moved, transcendentals=0),
    )(*args)


def whole(shape):
    return pl.BlockSpec(shape, lambda *_: (0,) * len(shape))


def rows(block, width):
    return pl.BlockSpec((block, width), lambda i: (i, 0))


def cols(height, block):
    return pl.BlockSpec((height, block), lambda i: (0, i))


def struct(shape, dtype):
    return jax.ShapeDtypeStruct(shape, dtype)


def centred(v):
    centre = v - jnp.mean(v, axis=-1, keepdims=True)
    scale = lax.rsqrt(jnp.mean(centre * centre, axis=-1, keepdims=True) + EPS)
    return centre * scale, scale


def norm_back(unit, scale, gain, grad):
    push = grad * gain
    mean_push = jnp.mean(push, axis=-1, keepdims=True)
    mean_both = jnp.mean(push * unit, axis=-1, keepdims=True)
    return scale * (push - mean_push - unit * mean_both)


def column_sum(v):
    return jnp.sum(v, axis=0, keepdims=True)


def latent_body(latent, gain, bias, wq, norm, query):
    unit, _ = centred(latent[...].astype(F32))
    low = (unit * gain[...] + bias[...]).astype(BF)
    norm[...] = low
    query[...] = (HEAD_DIM**-0.5 * dot(low, wq[...])).astype(BF)


def media_body(patch, gain, bias, wk, wv, latent_norm, norm, kp, vp, kl, vl):
    @pl.when(pl.program_id(0) == 0)
    def _():
        kl[...] = dot(latent_norm[...], wk[...]).astype(BF)
        vl[...] = dot(latent_norm[...], wv[...]).astype(BF)

    unit, _ = centred(patch[...].astype(F32))
    low = (unit * gain[...] + bias[...]).astype(BF)
    norm[...] = low
    kp[...] = dot(low, wk[...]).astype(BF)
    vp[...] = dot(low, wv[...]).astype(BF)


def head_of(shape):
    return lax.broadcasted_iota(jnp.int32, shape, 1) // HEAD_DIM


def spread_rows(v):
    head = head_of(v.shape)
    zero = jnp.zeros_like(v)
    count = v.shape[1] // HEAD_DIM
    return jnp.concatenate([jnp.where(head == h, v, zero) for h in range(count)], axis=0)


def gather_rows(v):
    heads = v.shape[1] // HEAD_DIM
    count = v.shape[0] // heads
    head = head_of((count, v.shape[1]))
    total = v[:count]
    for h in range(1, heads):
        total = jnp.where(head == h, v[h * count : (h + 1) * count], total)
    return total


def head_groups():
    half = INNER // 2
    return [(g, slice(g * half, (g + 1) * half)) for g in range(2)]


def pack_lanes(columns, first=0):
    count = columns[0].shape[0]
    lane = lax.broadcasted_iota(jnp.int32, (count, LANES), 1)
    total = jnp.zeros((count, LANES), F32)
    for h, column in enumerate(columns):
        total = jnp.where(lane == first + h, column, total)
    return total


def widen(packed):
    head = head_of((packed.shape[0], INNER))
    total = jnp.zeros((packed.shape[0], INNER), F32)
    for h in range(HEADS):
        total = jnp.where(head == h, packed[:, h : h + 1], total)
    return total


def stack_heads(packed, offset, group):
    first = offset + group * HEADS // 2
    return jnp.concatenate([packed[:, c : c + 1] for c in range(first, first + HEADS // 2)], axis=0)


def attend_slots(slots):
    work = []
    for qo, qp, kp, vp, kl, vl, *_ in slots:
        queries = jnp.concatenate([qo[...], qp[...]], axis=0)
        for _, at in head_groups():
            big = spread_rows(queries[:, at])
            keys = jnp.concatenate([kp[:, at], kl[:, at]], axis=0)
            values = jnp.concatenate([vp[:, at], vl[:, at]], axis=0)
            work.append((big, keys, values))
    scores = [dot_t(big, keys) for big, keys, _ in work]
    tops = [jnp.max(v, axis=-1, keepdims=True) for v in scores]
    expos = [jnp.exp(v - top) for v, top in zip(scores, tops)]
    totals = [jnp.sum(v, axis=-1, keepdims=True) for v in expos]
    probs = [(v * (1.0 / total)).astype(BF) for v, total in zip(expos, totals)]
    outs = [gather_rows(dot(v, w[2])) for v, w in zip(probs, work)]
    logs = [top + jnp.log(total) for top, total in zip(tops, totals)]
    for k, (qo, _, _, _, _, _, oo, op, so, sp) in enumerate(slots):
        own = qo.shape[0]
        count = 2 * own
        columns = []
        for g, at in head_groups():
            out, log_total = outs[2 * k + g], logs[2 * k + g]
            columns += [log_total[h * count : (h + 1) * count] for h in range(HEADS // 2)]
            oo[:, at] = out[:own]
            op[:, at] = out[own:].astype(BF)
        packed = pack_lanes(columns)
        so[...] = packed[:own]
        sp[...] = packed[own:]


def attend_body(*refs):
    attend_slots([refs])


def forward_body(
    slot_rows,
    holding,
    oo,
    orecv,
    so,
    srecv,
    latent,
    cot,
    wo,
    wup,
    wdown,
    gain,
    bias,
    new_latents,
    act_out,
    pre_out,
    ffn_t,
    og_out,
    residual_grad,
    attended_grad,
    stats,
    output_grad,
    vectors,
    residual,
    ffn_in,
    acc,
    gacc,
    attended,
    packed,
):
    step = pl.program_id(0)
    count = latent.shape[0]
    slot = lax.broadcasted_iota(jnp.int32, (count, 1), 0) // slot_rows
    live = jnp.where(slot < holding[0, 0], 1.0, 0.0).astype(F32)

    @pl.when(step == 0)
    def _():
        a, b = so[...], srecv[...]
        top = jnp.maximum(a, b)
        both = top + jnp.log(jnp.exp(a - top) + jnp.exp(b - top))
        packed[...] = both
        mix = widen(jnp.exp(a - both)) * oo[...]
        mix += widen(jnp.exp(b - both)) * orecv[...].astype(F32)
        attended[...] = mix
        res = latent[...].astype(F32) + dot(mix.astype(BF), wo[...])
        residual[...] = res
        unit, _ = centred(res)
        low = (unit * gain[...] + bias[...]).astype(BF)
        ffn_in[...] = low
        ffn_t[...] = low.T
        og_out[...] = (cot[...].astype(F32) * live).astype(BF)
        acc[...] = jnp.zeros_like(acc)
        gacc[...] = jnp.zeros_like(gacc)

    pre = dot(ffn_in[...], wup[...])
    cdf = 0.5 * (1.0 + lax.erf(pre * (0.5**0.5)))
    act = (pre * cdf).astype(BF)
    act_out[...] = act
    acc[...] += dot(act, wdown[...])
    act_grad = dot_t(og_out[...], wdown[...])
    pdf = jnp.exp(-0.5 * pre * pre) * 0.3989422804014327
    pre_grad = (act_grad * (cdf + pre * pdf)).astype(BF)
    pre_out[...] = pre_grad
    gacc[...] += dot_t(pre_grad, wup[...])

    @pl.when(step == pl.num_programs(0) - 1)
    def _():
        res = residual[...]
        new_latents[...] = ((res + acc[...]) * live).astype(BF)
        unit, scale = centred(res)
        grad = gacc[...]
        vectors[0:1, :] = column_sum(grad * unit)
        vectors[1:2, :] = column_sum(grad)
        res_grad = og_out[...].astype(F32) + norm_back(unit, scale, gain[...], grad)
        residual_grad[...] = res_grad
        branch = res_grad.astype(BF)
        back = dot_t(branch, wo[...]).astype(BF)
        attended_grad[...] = back
        mix = attended[...]
        product = back.astype(F32) * mix
        head = head_of(product.shape)
        sums = [
            jnp.sum(jnp.where(head == h, product, 0.0), axis=-1, keepdims=True)
            for h in range(HEADS)
        ]
        delta = pack_lanes(sums, HEADS)
        lane = lax.broadcasted_iota(jnp.int32, delta.shape, 1)
        stats[...] = jnp.where(lane < HEADS, packed[...], delta)
        output_grad[...] = t_dot(mix.astype(BF), branch).astype(BF)


def attend_back_slots(slots):
    work = []
    for qo, qp, kp, vp, kl, vl, do, dp, so, sp, *_ in slots:
        queries = jnp.concatenate([qo[...], qp[...]], axis=0)
        grads = jnp.concatenate([do[...], dp[...]], axis=0)
        stats = jnp.concatenate([so[...], sp[...]], axis=0)
        for g, at in head_groups():
            big = spread_rows(queries[:, at])
            back = spread_rows(grads[:, at])
            keys = jnp.concatenate([kp[:, at], kl[:, at]], axis=0)
            values = jnp.concatenate([vp[:, at], vl[:, at]], axis=0)
            work.append(
                (big, back, keys, values, stack_heads(stats, 0, g), stack_heads(stats, HEADS, g))
            )
    scores = [dot_t(w[0], w[2]) for w in work]
    prob_grads = [dot_t(w[1], w[3]) for w in work]
    probs = [jnp.exp(v - w[4]) for v, w in zip(scores, work)]
    score_grads = [(v * (d - w[5])).astype(BF) for v, d, w in zip(probs, prob_grads, work)]
    values_grads = [t_dot(v.astype(BF), w[1]).astype(BF) for v, w in zip(probs, work)]
    keys_grads = [t_dot(v, w[0]).astype(BF) for v, w in zip(score_grads, work)]
    dqs = [gather_rows(dot(v, w[2])) for v, w in zip(score_grads, work)]
    for k, refs in enumerate(slots):
        own, patches = refs[0].shape[0], refs[2].shape[0]
        dkvp, dkvl, dqo, dqp = refs[10:]
        for g, at in head_groups():
            late = slice(INNER + at.start, INNER + at.stop)
            u = 2 * k + g
            dkvp[:, at] = keys_grads[u][:patches]
            dkvp[:, late] = values_grads[u][:patches]
            dkvl[:, at] = keys_grads[u][patches:]
            dkvl[:, late] = values_grads[u][patches:]
            dqo[:, at] = dqs[u][:own]
            dqp[:, at] = dqs[u][own:].astype(BF)


def attend_back_body(*refs):
    attend_back_slots([refs])


def up_grad_body(left, right, out):
    out[...] = dot(left[...], right[...]).astype(BF)


def down_grad_body(left, right, out):
    out[...] = t_dot(left[...], right[...]).astype(BF)


def kv_grad_body(media, latent, dkvp, dkvl, out):
    out[...] = (t_dot(media[...], dkvp[...]) + t_dot(latent[...], dkvl[...])).astype(BF)


def patch_back_body(patch, dkvp, wk, wv, gain, out, vectors):
    @pl.when(pl.program_id(0) == 0)
    def _():
        vectors[...] = jnp.zeros_like(vectors)

    grad = dot_t(dkvp[:, :INNER], wk[...]) + dot_t(dkvp[:, INNER:], wv[...])
    unit, scale = centred(patch[...].astype(F32))
    vectors[0:1, :] += column_sum(grad * unit)
    vectors[1:2, :] += column_sum(grad)
    out[...] = norm_back(unit, scale, gain[...], grad)


def latent_back_body(
    latent, norm, dkvl, dqo, drecv, residual_grad, wq, wk, wv, gain, out, query_grad, vectors
):
    dq = (dqo[...] + drecv[...].astype(F32)).astype(BF)
    product = (HEAD_DIM**-0.5 * t_dot(norm[...], dq)).astype(BF)
    if query_grad.shape == product.shape:
        query_grad[...] = product
    else:
        product = product.reshape(-1, 32, INNER)
        shape = query_grad.shape[:-1] + (INNER,)
        query_grad[..., :INNER] = product[:, :16].reshape(shape)
        query_grad[..., INNER:] = product[:, 16:].reshape(shape)
    grad = dot_t(dkvl[:, :INNER], wk[...]) + dot_t(dkvl[:, INNER:], wv[...])
    grad += HEAD_DIM**-0.5 * dot_t(dq, wq[...])
    unit, scale = centred(latent[...].astype(F32))
    vectors[0:1, :] = column_sum(grad * unit)
    vectors[1:2, :] = column_sum(grad)
    out[...] = residual_grad[...] + norm_back(unit, scale, gain[...], grad)


def ffn_back_body(
    residual, gacc, og, mix_ref, packed, wo, gain, residual_grad, attended_grad, stats, out, vectors
):
    unit, scale = centred(residual[...])
    grad = gacc[...]
    vectors[0:1, :] = column_sum(grad * unit)
    vectors[1:2, :] = column_sum(grad)
    res_grad = og[...].astype(F32) + norm_back(unit, scale, gain[...], grad)
    residual_grad[...] = res_grad
    branch = res_grad.astype(BF)
    back = dot_t(branch, wo[...]).astype(BF)
    attended_grad[...] = back
    mix = mix_ref[...]
    product = back.astype(F32) * mix
    head = head_of(product.shape)
    sums = [
        jnp.sum(jnp.where(head == h, product, 0.0), axis=-1, keepdims=True) for h in range(HEADS)
    ]
    delta = pack_lanes(sums, HEADS)
    lane = lax.broadcasted_iota(jnp.int32, delta.shape, 1)
    stats[...] = jnp.where(lane < HEADS, packed[...], delta)
    if out is not None:
        out[...] = t_dot(mix.astype(BF), branch).astype(BF).reshape(out.shape)


def plus(a, b):
    return a.astype(F32) + b.astype(F32)


class Names:
    def __getattr__(self, name):
        return name


n = Names()
STREAMS = ("d0", "d1", "d2", "d3", "u0", "u1", "u2", "u3", "K", "W", "Q")
ORDERS = {
    "d0": "zyxw", "d1": "zxyw", "d2": "yzxw", "d3": "zyxw", "u0": "xywz", "u1": "yxzw",
    "u2": "wyzx", "u3": "yxzw", "K": "ywxz", "W": "xywz", "Q": "zxyw",
}
PLAN = (
    "fi", "md", "af0:4", "af4:6", "af6:8", "cb0", "cb1", "j0", "j1", "j2", "j3", "u0", "j4",
    "u1", "j5", "j6", "j7", "fb", "u2", "u3", "+u0", "+u1", "at0:8", "d1", "+u1", "d3", "kv0",
    "d2", "kv1", "+u3", "ow", "+u1", "lat", "+K", "+u2", "+u0", "kv2", "+d2", "+Q", "+d1",
    "+u1", "kv3", "+d3", "pt0", "+u3", "pt1", "d0", "+W", "+K", "+u0", "+d2", "pt2", "pt3",
    "+d3", "+V", "+u2", "+Q", "+K", "+W", "+d1", "+V", "+u3", "+d2", "+d3", "+d0", "+u0", "+Q",
    "+d1", "+W", "+K", "+V", "+u3", "+d0", "+u2", "+Q", "+W", "+u2", "+K", "+d0", "+V", "+Q",
    "+W", "+V",
)
DIMS = "wzyx"
DOWN_AXES = {ORDERS[s][0] for s in STREAMS if s[0] == "d"}
DIMS_ALL = "wzycx"
BLOCK = (32, 1024)
LOADED = (n.latent, n.wq, n.og, n.wo)
GIVEN = LOADED + (
    n.patch,
    n.wk, n.wv, n.wup, n.wdown, n.images, n.device, n.fg, n.fb, n.mg, n.mb, n.lg, n.lb,
)


def is_late(s):
    return s in "KWQ"


def main_scratch(nl, np_, width, hidden):
    def bf(*shape):
        return pltpu.VMEM(shape, BF)

    def f4(*shape):
        return pltpu.VMEM(shape, F32)

    step = hidden // 8
    turned = (2, 2, 2, 2, step // 4, nl)
    turned_in = (2, 2, 2, 2, 32, nl)
    items = [
        (n.latent, bf(nl, width)),
        (n.wq, bf(width, INNER)),
        (n.og, bf(nl, width)),
        (n.patch, bf(2, np_ // 4, width)),
        (n.wo, bf(INNER, width)),
        (n.oo, f4(nl, INNER)),
        (n.op, bf(nl, INNER)),
        (n.so, f4(nl, LANES)),
        (n.sp, f4(nl, LANES)),
        (n.sp_t, f4(HEADS, nl)),
        (n.orecv, bf(nl, INNER)),
        (n.srecv_t, f4(HEADS, nl)),
        (n.stats_t, f4(2 * HEADS, nl)),
        (n.stats_peer_t, f4(2 * HEADS, nl)),
        (n.q, bf(nl, INNER)),
        (n.q_peer, bf(nl, INNER)),
        (n.kp, bf(np_, INNER)),
        (n.vp, bf(np_, INNER)),
        (n.kl, bf(nl, INNER)),
        (n.vl, bf(nl, INNER)),
        (n.norm_l, bf(nl, width)),
        (n.norm_m, bf(np_, width)),
        (n.wu, bf(2, width, step)),
        (n.wd, bf(2, step, width)),
        (n.og_sib, bf(nl, width)),
        (n.act_own, bf(*turned)),
        (n.act_send, bf(*turned)),
        (n.act_sib, bf(*turned)),
        (n.ffn_own, bf(*turned_in)),
        (n.ffn_send, bf(*turned_in)),
        (n.ffn_sib, bf(*turned_in)),
        (n.residual, f4(nl, width)),
        (n.gacc, f4(nl, width)),
        (n.acc, f4(nl, width)),
        (n.ffn_in, bf(nl, width)),
        (n.attended, f4(nl, INNER)),
        (n.grad, bf(nl, INNER)),
        (n.stats, f4(nl, LANES)),
        (n.grad_peer, bf(nl, INNER)),
        (n.stats_peer, f4(nl, LANES)),
        (n.dkvp, bf(np_, 2 * INNER)),
        (n.dkvl, bf(nl, 2 * INNER)),
        (n.dq_peer, bf(nl, INNER)),
        (n.vs, f4(5, 8, width)),
        (n.vr, f4(5, 8, width)),
        (n.sums, f4(2, width)),
        (n.pre, bf(2, 2, 2, 2, 2, *BLOCK)),
        (n.pre_sib, bf(2, 2, 2, 2, 2, *BLOCK)),
    ]
    for s in STREAMS:
        if s[0] == "u":
            items.append((s, bf(2, 2, 2, 2, *BLOCK)))
        if s[0] == "d":
            items.append((s, bf(2, 2, 2, *BLOCK)))
            items += [(s + "_p", bf(2, 2, 2, 32, nl)), (s + "_q", bf(2, 2, 2, 32, nl))]
    for axis in sorted(DOWN_AXES):
        items += [("og_p" + axis, bf(nl, width)), ("og_q" + axis, bf(nl, width))]
    for s in STREAMS:
        wide = BLOCK[1] // 2 if s in "KW" else BLOCK[1]
        for k in range({"u": 3, "d": 2}.get(s[0], 4), -1, -1):
            items.append((s + "_%d" % k, bf(*((2,) * k), BLOCK[0], wide)))
    dma = pltpu.SemaphoreType.DMA
    items += [
        (n.load_sem, dma((len(LOADED) + 4,))),
        (n.weight_sem, dma((2, 2))),
        (n.store_sem, dma((6,))),
        (n.patch_sem, dma((2,))),
        (n.send_sem, dma((96,))),
        (n.recv_sem, dma((96,))),
    ]
    return [k for k, _ in items], [v for _, v in items]


def main_body(names, *refs):
    src = SimpleNamespace(**dict(zip(GIVEN, refs)))
    outs = len(GIVEN)
    fin, vec, patches_low, latents_grad, new_latents = refs[outs : outs + 5]
    t = SimpleNamespace(**dict(zip(names, refs[outs + 5 :])))
    load_sem, weight_sem, store_sem = t.load_sem, t.weight_sem, t.store_sem
    mine = lax.axis_index("img")
    xb = lax.axis_index("lat")
    bit = {"x": xb, "c": mine % 2, "y": (mine // 2) % 2, "z": (mine // 4) % 2, "w": (mine // 8) % 2}

    def to(axis, weight):
        return (mine + weight - 2 * weight * bit[axis], xb)

    peer = {"c": to("c", 1), "y": to("y", 2), "z": to("z", 4), "w": to("w", 8), "x": (mine, 1 - xb)}
    for axis in sorted(DOWN_AXES):
        beside = peer[axis][0] + 1 - 2 * bit["c"]
        peer["c" + axis] = (beside, peer[axis][1])
    barrier = pltpu.get_barrier_semaphore()
    for axis in peer:
        pl.semaphore_signal(
            barrier, inc=1, device_id=peer[axis], device_id_type=pl.DeviceIdType.MESH
        )

    step = t.wd.shape[1]
    count = t.og.shape[0]
    weights = {}

    def load_weights(j):
        slot = j % 2
        col = pl.ds(j * step, step)
        pair = (
            pltpu.make_async_copy(src.wup.at[:, col], t.wu.at[slot], weight_sem.at[0, slot]),
            pltpu.make_async_copy(src.wdown.at[col], t.wd.at[slot], weight_sem.at[1, slot]),
        )
        for copy in pair:
            copy.start()
        weights[j] = pair

    loads = {}

    def load(names):
        for name in names:
            i = LOADED.index(name)
            loads[name] = pltpu.make_async_copy(getattr(src, name), getattr(t, name), load_sem.at[i])
            loads[name].start()

    def load_kv(first):
        for i, name in enumerate((n.wk, n.wv)):
            loads[name] = pltpu.make_async_copy(
                getattr(src, name), t.wu.at[i], load_sem.at[len(LOADED) + first + i]
            )
            loads[name].start()

    size = src.patch.shape[0] // 4
    patch_loads = []

    def load_patch():
        i = len(patch_loads)
        copy = pltpu.make_async_copy(
            src.patch.at[pl.ds(i % 4 * size, size)], t.patch.at[i % 2], t.patch_sem.at[i % 2]
        )
        copy.start()
        patch_loads.append(copy)

    load(LOADED[:3])
    load_kv(0)
    load_patch()
    load_patch()
    load(LOADED[3:])

    def need(*names):
        for name in names:
            if name in loads:
                loads.pop(name).wait()

    used = []

    def send(source, target, axis):
        slot = len(used)
        copy = pltpu.make_async_remote_copy(
            src_ref=source,
            dst_ref=target,
            send_sem=t.send_sem.at[slot],
            recv_sem=t.recv_sem.at[slot],
            device_id=peer[axis],
            device_id_type=pl.DeviceIdType.MESH,
        )
        copy.start()
        used.append(copy)
        return copy

    arriving = {}

    def arrive(*names):
        for name in names:
            if name in arriving:
                arriving.pop(name).wait_recv()

    order = {s: ("c" if is_late(s) else "") + ORDERS[s] for s in STREAMS}
    place = {s: 1 if s[0] == "d" else 0 for s in STREAMS}
    half = BLOCK[1] // 2
    buffer = {s: getattr(t, s) for s in STREAMS if not is_late(s)}
    buffer["K"] = buffer["W"] = t.pre
    buffer["Q"] = t.pre_sib
    column = {"K": pl.ds(0, half), "W": pl.ds(half, half)}

    def where(s, axis, value):
        done = order[s][: place[s]]
        index = []
        for d in DIMS_ALL if is_late(s) else DIMS:
            if s[0] == "d" and d == order[s][0]:
                continue
            if d == axis:
                index.append(value)
            else:
                index.append(bit[d] if d in done else slice(None))
        if s in column:
            index += [slice(None), column[s]]
        return tuple(index)

    def got(s):
        return getattr(t, s + "_%d" % (len(order[s]) - 1 - place[s]))

    def start(s):
        axis = order[s][place[s]]
        arriving[s] = send(buffer[s].at[where(s, axis, 1 - bit[axis])], got(s), axis)

    def take(s):
        axis = order[s][place[s]]
        arrive(s)
        if s == "Q" and place[s] == 0:
            arrive(n.O)
        at = where(s, axis, bit[axis])
        total = plus(buffer[s][at], got(s)[...])
        place[s] += 1
        if place[s] < len(order[s]):
            buffer[s][at] = total.astype(BF)
            start(s)
        elif s in column:
            fin[8, :, column[s]] = total
        else:
            fin[9 if s == "Q" else STREAMS.index(s)] = total

    vs, vr = t.vs, t.vr
    vec_order = "cxyzw"
    vec_place = [0]

    def take_vector():
        i = vec_place[0]
        arrive(n.V)
        if i < 4:
            vs[i + 1] = vs[i] + vr[i]
            arriving["V"] = send(vs.at[i + 1], vr.at[i + 1], vec_order[i + 1])
        else:
            vec[...] = vs[i] + vr[i]
        vec_place[0] += 1

    stores = []

    def store(source, target):
        slot = len(stores)
        stores.append(pltpu.make_async_copy(source, target, store_sem.at[slot]))
        stores[slot].start()

    core = bit["c"]
    def live_rows():
        total = jnp.int32(0)
        for i in range(src.images.shape[0]):
            total += jnp.where(src.device[i] == mine, src.images[i], 0)
        slot = lax.broadcasted_iota(jnp.int32, (count, 1), 0) // (count // 8)
        return jnp.where(slot < total, 1.0, 0.0).astype(F32)

    def share_og(axes):
        for axis in sorted(DOWN_AXES.intersection(axes)):
            arriving["og_p" + axis] = send(t.og, getattr(t, "og_p" + axis), axis)

    def pass_og(axes):
        for axis in sorted(DOWN_AXES.intersection(axes)):
            name = "og_p" + axis
            arrive(name)
            arriving["og_q" + axis] = send(getattr(t, name), getattr(t, "og_q" + axis), "c")

    def first():
        need(n.latent, n.wq)
        part = count // 2
        for i in range(2):
            at = pl.ds(i * part, part)
            unit, _ = centred(t.latent[at].astype(F32))
            low = (unit * src.lg[...] + src.lb[...]).astype(BF)
            t.norm_l[at] = low
            t.q[at] = (HEAD_DIM**-0.5 * dot(low, t.wq[...])).astype(BF)
            if i == 0:
                pl.semaphore_wait(barrier, len(peer))
            arriving["q%d" % i] = send(t.q.at[at], t.q_peer.at[at], "x")
        low = t.norm_l[...]
        need(n.og, n.wk, n.wv)
        t.og[...] = (t.og[...].astype(F32) * live_rows()).astype(BF)
        arriving[n.og_sib] = send(t.og, t.og_sib, "c")
        share_og("yz")
        t.kl[...] = dot(low, t.wu[0]).astype(BF)
        t.vl[...] = dot(low, t.wu[1]).astype(BF)

    def media():
        def norm(i):
            patch_loads[i].wait()
            unit, _ = centred(t.patch[i % 2].astype(F32))
            low = (unit * src.mg[...] + src.mb[...]).astype(BF)
            t.norm_m[pl.ds(i * size, size)] = low

        norm(0)
        for i in range(4):
            at = pl.ds(i * size, size)
            if i < 3:
                norm(i + 1)
            t.kp[at] = dot(t.norm_m[at], t.wu[0]).astype(BF)
            t.vp[at] = dot(t.norm_m[at], t.wu[1]).astype(BF)
            load_patch()
        load_weights(0)
        load_weights(1)

    def slot_rows(i):
        lat, med = count // 8, t.kp.shape[0] // 8
        return (
            pl.ds(pl.multiple_of(i * lat, lat), lat),
            pl.ds(pl.multiple_of(i * med, med), med),
        )

    def attend(first, last):
        arrive("q0")
        if last > 4:
            arrive("q1")

        def refs(i):
            a, b = slot_rows(i)
            return (
                t.q.at[a], t.q_peer.at[a], t.kp.at[b], t.vp.at[b], t.kl.at[a], t.vl.at[a],
                t.oo.at[a], t.op.at[a], t.so.at[a], t.sp.at[a],
            )

        @pl.loop(first // 2, last // 2)
        def _(i):
            attend_slots([refs(2 * i), refs(2 * i + 1)])

        at = pl.ds(first * (count // 8), (last - first) * (count // 8))
        arriving["o%d" % first] = send(t.op.at[at], t.orecv.at[at], "x")
        if last % 4 == 0:
            at = pl.ds((last - 4) * (count // 8), count // 2)
            t.sp_t[:, at] = t.sp[at].T[:HEADS]
            arriving["s%d" % first] = send(t.sp_t.at[:, at], t.srecv_t.at[:, at], "x")
        if last == 8:
            share_og("x")

    def combine(h):
        if h == 0:
            need(n.wo)
        part = count // 2
        at = pl.ds(h * part, part)
        for first in (0, 1, 2, 3) if h == 0 else (4, 5, 6, 7):
            arrive("o%d" % first, "s%d" % first)
        a, b = t.so[at, :HEADS], t.srecv_t[:, at].T
        top = jnp.maximum(a, b)
        both = top + jnp.log(jnp.exp(a - top) + jnp.exp(b - top))
        t.so[at, :HEADS] = both
        mix = widen(jnp.exp(a - both)) * t.oo[at]
        mix += widen(jnp.exp(b - both)) * t.orecv[at].astype(F32)
        t.attended[at] = mix
        res = t.latent[at].astype(F32) + dot(mix.astype(BF), t.wo[...])
        t.residual[at] = res
        unit, _ = centred(res)
        low = (unit * src.fg[...] + src.fb[...]).astype(BF)
        t.ffn_in[at] = low
        turned = low.T.reshape(8, 2, -1, part)
        even, odd = turned[:, 0], turned[:, 1]
        shape = t.ffn_own.shape[:-1] + (part,)
        t.ffn_own[..., at] = jnp.where(core == 0, even, odd).reshape(shape)
        t.ffn_send[..., at] = jnp.where(core == 0, odd, even).reshape(shape)
        if h == 1:
            arriving[n.ffn_sib] = send(t.ffn_send, t.ffn_sib, "c")
            pass_og("yz")

    def ffn(j):
        for copy in weights.pop(j):
            copy.wait()
        wup, wdown = t.wu[j % 2], t.wd[j % 2]
        pre = dot(t.ffn_in[...], wup)
        cdf = 0.5 * (1.0 + lax.erf(pre * (0.5**0.5)))
        pdf = jnp.exp(-0.5 * pre * pre) * 0.3989422804014327
        act = (pre * cdf).astype(BF)
        turned = act.T
        even, odd = turned[: step // 2], turned[step // 2 :]
        at = (j // 4, (j // 2) % 2, j % 2)
        shape = t.act_own.shape[3:]
        t.act_own[at] = jnp.where(core == 0, even, odd).reshape(shape)
        t.act_send[at] = jnp.where(core == 0, odd, even).reshape(shape)
        arriving["act%d" % j] = send(t.act_send.at[at], t.act_sib.at[at], "c")
        down = dot(act, wdown)
        act_grad = dot_t(t.og[...], wdown)
        pre_grad = (act_grad * (cdf + pre * pdf)).astype(BF)
        group = (j // 4, (j // 2) % 2)
        t.pre[group + (slice(None),) * 4 + (pl.ds((j % 2) * step, step),)] = pre_grad.reshape(
            2, 2, 2, 32, step
        )
        if j % 2 == 1:
            name = "pre%d" % (j // 2)
            arriving[name] = send(t.pre.at[group], t.pre_sib.at[group], "c")
            pre_sent.append(len(used) - 1)
        back = dot_t(pre_grad, wup)
        if j == 0:
            t.acc[...] = down
            t.gacc[...] = back
        else:
            t.acc[...] += down
            t.gacc[...] += back
        if j in (3, 7):
            for g in range(4):
                s = "d%d" % g
                axis = order[s][0]
                at = tuple(1 - bit[d] if d == axis else slice(None) for d in DIMS[1:])
                at = (j // 4,) + at + (pl.ds(g * 32, 32),)
                p, q = getattr(t, s + "_p").at[j // 4], getattr(t, s + "_q").at[j // 4]
                arriving[s + "_p%d" % j] = send(t.act_own.at[at], p, axis)
                arriving[s + "_q%d" % j] = send(t.act_send.at[at], q, "c" + axis)
        if j < 6:
            load_weights(j + 2)
        if j == 7:
            pass_og("x")
            load_kv(2)
            t.ffn_in[...] = ((t.residual[...] + t.acc[...]) * live_rows()).astype(BF)
            store(t.ffn_in, new_latents)

    pre_sent = []

    def ffn_back():
        ffn_back_body(
            t.residual, t.gacc, t.og, t.attended, t.so, t.wo, src.fg,
            t.residual, t.grad, t.stats, None, vs.at[0, pl.ds(4, 2)],
        )
        arriving[n.grad_peer] = send(t.grad, t.grad_peer, "x")
        t.stats_t[...] = t.stats[...].T[: 2 * HEADS]
        arriving[n.stats_peer] = send(t.stats_t, t.stats_peer_t, "x")

    def send_late(rows, name):
        o, r = buffer["Q"], t.Q_4
        arriving[name] = send(
            o.at[:, :, :, 1 - core, :, rows], r.at[:, :, :, :, rows], "c"
        )

    def output_group():
        product = t_dot(t.attended[...].astype(BF), t.residual[...].astype(BF)).astype(BF)
        buffer["Q"][..., pl.ds(0, 16), :] = product.reshape(2, 2, 2, 2, 2, 16, BLOCK[1])
        send_late(pl.ds(0, 16), "O")

    def rows_of(ref, at):
        v = ref[at]
        return v.reshape(-1, v.shape[-1])

    def down_group(g):
        s = "d%d" % g
        axis = order[s][0]
        arrive(n.og_sib, "og_q" + axis, *("act%d" % j for j in range(8)))
        arrive(*(s + end for end in ("_p3", "_q3", "_p7", "_q7")))
        at = tuple(bit[d] if d == axis else slice(None) for d in DIMS) + (pl.ds(g * 32, 32),)
        v = dot(rows_of(t.act_own, at), t.og[...])
        v += dot(rows_of(t.act_sib, at), t.og_sib[...])
        every = (slice(None),)
        v += dot(rows_of(getattr(t, s + "_p"), every), getattr(t, "og_p" + axis)[...])
        v += dot(rows_of(getattr(t, s + "_q"), every), getattr(t, "og_q" + axis)[...])
        buffer[s][...] = v.astype(BF).reshape((2, 2, 2) + BLOCK)
        start(s)

    def up_group(g):
        s = "u%d" % g
        arrive(n.ffn_sib, "pre%d" % g)
        axis = order[s][0]
        group = (g // 2, g % 2)
        for value in (1 - bit[axis], bit[axis]):
            at = where(s, axis, value)
            v = dot(rows_of(t.ffn_own, at), rows_of(t.pre, group))
            v += dot(rows_of(t.ffn_sib, at), rows_of(t.pre_sib, group))
            buffer[s][at] = v.astype(BF).reshape((2, 2, 2) + BLOCK)
            if s not in arriving:
                start(s)

    def attend_back(first, last):
        if n.stats_peer in arriving:
            arrive(n.grad_peer, n.stats_peer)
            t.stats_peer[:, : 2 * HEADS] = t.stats_peer_t[...].T

        def refs(i):
            a, b = slot_rows(i)
            return (
                t.q.at[a], t.q_peer.at[a], t.kp.at[b], t.vp.at[b], t.kl.at[a], t.vl.at[a],
                t.grad.at[a], t.grad_peer.at[a], t.stats.at[a], t.stats_peer.at[a],
                t.dkvp.at[b], t.dkvl.at[a], t.oo.at[a], t.dq_peer.at[a],
            )

        @pl.loop(first // 2, last // 2)
        def _(i):
            attend_back_slots([refs(2 * i), refs(2 * i + 1)])

        if last == 8:
            arriving[n.dq_recv] = send(t.dq_peer, t.orecv, "x")

    def kv_group(g):
        while pre_sent:
            slot = pre_sent.pop()
            used[slot].wait_send()
            used[slot] = None
        col = pl.ds(g * 256, 256)
        v = t_dot(t.norm_m[...], t.dkvp[:, col])
        v += t_dot(t.norm_l[...], t.dkvl[:, col])
        buffer["K"][..., col] = v.astype(BF).reshape(2, 2, 2, 2, 2, 32, 256)
        if g == 1:
            start("K")
        if g == 3:
            start("W")

    def latent_back():
        need(n.wk, n.wv)
        arrive(n.dq_recv)
        latent_back_body(
            t.latent, t.norm_l, t.dkvl, t.oo, t.orecv, t.residual,
            t.wq, t.wu.at[0], t.wu.at[1], src.lg, t.residual,
            buffer["Q"].at[..., pl.ds(16, 16), :], vs.at[0, pl.ds(2, 2)],
        )
        send_late(pl.ds(16, 16), "Q")
        stores[0].wait()
        stores[0] = None
        t.ffn_in[...] = t.residual[...].astype(BF)
        store(t.ffn_in, latents_grad)

    def patch_back(i):
        need(n.wk, n.wv)
        at = pl.ds(i * size, size)
        dkv = t.dkvp
        grad = dot_t(dkv[at, :INNER], t.wu[0]) + dot_t(dkv[at, INNER:], t.wu[1])
        patch_loads[4 + i].wait()
        unit, scale = centred(t.patch[i % 2].astype(F32))
        sums = t.sums
        a, b = column_sum(grad * unit), column_sum(grad)
        if i > 0:
            a, b = a + sums[0:1, :], b + sums[1:2, :]
        sums[0:1, :] = a
        sums[1:2, :] = b
        dkv[at] = norm_back(unit, scale, src.mg[...], grad).astype(BF)
        store(dkv.at[at], patches_low.at[at])
        if i < 2:
            load_patch()
        if i == 3:
            vs[0, 0:2, :] = sums[...]
            vs[0, 6:8, :] = jnp.zeros((2, vs.shape[2]), F32)
            arriving["V"] = send(vs.at[0], vr.at[0], vec_order[0])

    simple = {"fi": first, "md": media,  "fb": ffn_back, "ow": output_group, "lat": latent_back}
    simple["+V"] = take_vector
    for item in PLAN:
        if item in simple:
            simple[item]()
        elif item[0] == "+":
            take(item[1:])
        elif item[:2] == "at":
            a, b = item[2:].split(":")
            attend_back(int(a), int(b))
        elif item[:2] == "cb":
            combine(int(item[2:]))
        elif item[:2] == "af":
            a, b = item[2:].split(":")
            attend(int(a), int(b))
        elif item[:2] == "kv":
            kv_group(int(item[2:]))
        elif item[:2] == "pt":
            patch_back(int(item[2:]))
        else:
            {"j": ffn, "d": down_group, "u": up_group}[item[0]](int(item[1:]))
    for copy in stores:
        if copy is not None:
            copy.wait()
    for copy in used:
        if copy is not None:
            copy.wait_send()


def last_body(
    patches_in, latents_in, fresh, fin, vec,
    patches_grad, new_latents, latents_grad, up, down, key, value, out, query, *rest,
):
    thin, (pin, pout, lin, lout, nin, held, sem) = rest[:6], rest[6:]
    copies = []

    def move(source, target):
        copies.append(pltpu.make_async_copy(source, target, sem.at[len(copies)]))
        copies[-1].start()
        return copies[-1]

    parts = pin.shape[0]
    size = pin.shape[1]
    waits = [move(patches_in.at[pl.ds(i * size, size)], pin.at[i]) for i in range(parts)]
    waits += [move(fin, held), move(latents_in, lin), move(fresh, nin)]
    for i in range(parts):
        waits[i].wait()
        pout[i] = pin[i].astype(F32)
        move(pout.at[i], patches_grad.at[pl.ds(i * size, size)])
    waits[parts].wait()
    for g in range(4):
        move(held.at[4 + g], up.at[:, pl.ds(g * 1024, 1024)])
        move(held.at[g], down.at[pl.ds(g * 32, 32)])
    move(held.at[8, :, pl.ds(0, INNER)], key)
    move(held.at[8, :, pl.ds(INNER, INNER)], value)
    move(held.at[9, pl.ds(0, 16)], out)
    for k in range(2):
        move(held.at[9, pl.ds(16, 16), pl.ds(k * INNER, INNER)], query.at[pl.ds(k * 16, 16)])
    waits[parts + 1].wait()
    lout[...] = lin[...].astype(F32)
    move(lout, latents_grad)
    waits[parts + 2].wait()
    move(nin, new_latents)
    place = lax.axis_index("img") * 2 + lax.axis_index("lat")
    width = vec.shape[1]
    turned = pltpu.roll(vec[...], width - place * 32, 1)
    for i, ref in enumerate(thin):
        ref[...] = turned[i : i + 1, :32]
    for copy in copies[len(waits) :]:
        copy.wait()


def swap_lat(v):
    return lax.ppermute(v, "lat", [(0, 1), (1, 0)])


def halving_sum(v, order, bits, count, keep):
    left = list(range(bits - 1, -1, -1)) + [-1]
    mine = lax.axis_index("img")
    for place, axis in enumerate(order):
        dim = left.index(axis)
        if axis < 0:
            bit = lax.axis_index("lat")
            pairs, name = [(0, 1), (1, 0)], "lat"
        else:
            bit = (mine // 2**axis) % 2
            pairs, name = [(i, i ^ 2**axis) for i in range(count)], "img"
        out = lax.dynamic_index_in_dim(v, 1 - bit, dim, keepdims=False)
        stay = lax.dynamic_index_in_dim(v, bit, dim, keepdims=False)
        got = lax.ppermute(out, name, pairs)
        v = stay.astype(F32) + got.astype(F32)
        if place < len(order) - 1 and keep == BF:
            v = v.astype(BF)
        left.pop(dim)
    return v


def local(
    count,
    patches,
    latents,
    cotangent,
    doc_images,
    doc_device,
    query_weight,
    key_weight,
    value_weight,
    output_weight,
    up_weight,
    down_weight,
    media_gain,
    media_bias,
    latent_gain,
    latent_bias,
    ffn_gain,
    ffn_bias,
):
    slots, own_patches, width = patches.shape
    own_latents = latents.shape[1]
    hidden = up_weight.shape[1]
    np_, nl = slots * own_patches, slots * own_latents
    mine = lax.axis_index("img")
    holding = jnp.sum(jnp.where(doc_device == mine, doc_images, 0)).reshape(1, 1)
    patch = patches.reshape(np_, width)
    latent = latents.reshape(nl, width)
    cot = cotangent.reshape(nl, width)
    mg, mb = media_gain.reshape(1, width), media_bias.reshape(1, width)
    lg, lb = latent_gain.reshape(1, width), latent_bias.reshape(1, width)
    fg, fb = ffn_gain.reshape(1, width), ffn_bias.reshape(1, width)
    wspec = whole((width, INNER))
    vspec = whole((1, width))
    lspec = whole((nl, width))

    norm_l, query = call(
        latent_body,
        (1,),
        [lspec, vspec, vspec, wspec],
        [(struct((nl, width), BF), lspec), (struct((nl, INNER), BF), whole((nl, INNER)))],
        (latent, lg, lb, query_weight),
        2 * nl * width * INNER,
    )
    query_peer = swap_lat(query)
    blk = min(np_, 256)
    norm_m, kp, vp, kl, vl = call(
        media_body,
        (np_ // blk,),
        [rows(blk, width), vspec, vspec, wspec, wspec, lspec],
        [
            (struct((np_, width), BF), rows(blk, width)),
            (struct((np_, INNER), BF), rows(blk, INNER)),
            (struct((np_, INNER), BF), rows(blk, INNER)),
            (struct((nl, INNER), BF), whole((nl, INNER))),
            (struct((nl, INNER), BF), whole((nl, INNER))),
        ],
        (patch, mg, mb, key_weight, value_weight, norm_l),
        4 * (np_ + nl) * width * INNER,
    )
    q_s, p_s, s_s = rows(own_latents, INNER), rows(own_patches, INNER), rows(own_latents, LANES)
    att_flops = 4 * slots * (own_patches + own_latents) * INNER * INNER
    o_own, o_peer, s_own, s_peer = call(
        attend_body,
        (slots,),
        [q_s, q_s, p_s, p_s, q_s, q_s],
        [
            (struct((nl, INNER), F32), q_s),
            (struct((nl, INNER), BF), q_s),
            (struct((nl, LANES), F32), s_s),
            (struct((nl, LANES), F32), s_s),
        ],
        (query, query_peer, kp, vp, kl, vl),
        att_flops,
    )
    o_recv, s_recv = swap_lat(o_peer), swap_lat(s_peer)
    fblk = min(hidden, 512)
    nspec = whole((nl, INNER))
    (
        new_latents,
        act,
        pre_grad,
        ffn_t,
        out_grad,
        residual_grad,
        attended_grad,
        stats,
        output_grad,
        ffn_vec,
    ) = call(
        partial(forward_body, own_latents),
        (hidden // fblk,),
        [
            pl.BlockSpec(memory_space=pltpu.SMEM),
            nspec,
            nspec,
            whole((nl, LANES)),
            whole((nl, LANES)),
            lspec,
            lspec,
            whole((INNER, width)),
            cols(width, fblk),
            rows(fblk, width),
            vspec,
            vspec,
        ],
        [
            (struct((nl, width), BF), lspec),
            (struct((nl, hidden), BF), cols(nl, fblk)),
            (struct((nl, hidden), BF), cols(nl, fblk)),
            (struct((width, nl), BF), whole((width, nl))),
            (struct((nl, width), BF), lspec),
            (struct((nl, width), F32), lspec),
            (struct((nl, INNER), BF), nspec),
            (struct((nl, LANES), F32), whole((nl, LANES))),
            (struct((INNER, width), BF), whole((INNER, width))),
            (struct((2, width), F32), whole((2, width))),
        ],
        (
            holding,
            o_own,
            o_recv,
            s_own,
            s_recv,
            latent,
            cot,
            output_weight,
            up_weight,
            down_weight,
            fg,
            fb,
        ),
        8 * nl * width * hidden,
        scratch=[
            pltpu.VMEM((nl, width), F32),
            pltpu.VMEM((nl, width), BF),
            pltpu.VMEM((nl, width), F32),
            pltpu.VMEM((nl, width), F32),
            pltpu.VMEM((nl, INNER), F32),
            pltpu.VMEM((nl, LANES), F32),
        ],
    )
    grad_peer, stats_peer = swap_lat(attended_grad), swap_lat(stats)
    (down_grad,) = call(
        down_grad_body,
        (hidden // fblk,),
        [cols(nl, fblk), lspec],
        [(struct((hidden, width), BF), rows(fblk, width))],
        (act, out_grad),
        2 * nl * width * hidden,
    )
    (up_grad,) = call(
        up_grad_body,
        (hidden // fblk,),
        [whole((width, nl)), cols(nl, fblk)],
        [(struct((width, hidden), BF), cols(width, fblk))],
        (ffn_t, pre_grad),
        2 * nl * width * hidden,
    )
    dkvp, dkvl, dq_own, dq_peer = call(
        attend_back_body,
        (slots,),
        [q_s, q_s, p_s, p_s, q_s, q_s, q_s, q_s, s_s, s_s],
        [
            (struct((np_, 2 * INNER), BF), rows(own_patches, 2 * INNER)),
            (struct((nl, 2 * INNER), BF), rows(own_latents, 2 * INNER)),
            (struct((nl, INNER), F32), q_s),
            (struct((nl, INNER), BF), q_s),
        ],
        (query, query_peer, kp, vp, kl, vl, attended_grad, grad_peer, stats, stats_peer),
        att_flops * 5 // 2,
    )
    dq_recv = swap_lat(dq_peer)
    kblk = 256
    (kv_grad,) = call(
        kv_grad_body,
        (2 * INNER // kblk,),
        [whole((np_, width)), lspec, cols(np_, kblk), cols(nl, kblk)],
        [(struct((width, 2 * INNER), BF), cols(width, kblk))],
        (norm_m, norm_l, dkvp, dkvl),
        4 * (np_ + nl) * width * INNER,
    )
    patches_grad, media_vec = call(
        patch_back_body,
        (np_ // blk,),
        [rows(blk, width), rows(blk, 2 * INNER), wspec, wspec, vspec],
        [(struct((np_, width), F32), rows(blk, width)), (struct((2, width), F32), whole((2, width)))],
        (patch, dkvp, key_weight, value_weight, mg),
        4 * np_ * width * INNER,
    )
    latents_grad, query_grad, latent_vec = call(
        latent_back_body,
        (1,),
        [
            lspec,
            lspec,
            whole((nl, 2 * INNER)),
            nspec,
            nspec,
            lspec,
            wspec,
            wspec,
            wspec,
            vspec,
        ],
        [
            (struct((nl, width), F32), lspec),
            (struct((width, INNER), BF), wspec),
            (struct((2, width), F32), whole((2, width))),
        ],
        (
            latent,
            norm_l,
            dkvl,
            dq_own,
            dq_recv,
            residual_grad,
            query_weight,
            key_weight,
            value_weight,
            lg,
        ),
        8 * nl * width * INNER,
    )

    bits = count.bit_length() - 1
    first = list(range(1, bits))
    orders = (
        [0, -1] + first,
        [0] + first + [-1],
        [0] + first[1:] + [-1] + first[:1],
    )

    def reduce(v, order, keep=BF):
        shape = (2,) * (bits + 1) + (v.shape[0] // (2 * count),) + v.shape[1:]
        return halving_sum(v.reshape(shape), order, bits, count, keep)

    def reduce_parts(v):
        unit = v.shape[1] // 8
        cuts = (0, 3 * unit, 6 * unit, 8 * unit)
        return jnp.concatenate(
            [reduce(v[:, a:b], order) for a, b, order in zip(cuts, cuts[1:], orders)], axis=1
        )

    down_sum = reduce_parts(down_grad)
    up_sum = reduce_parts(up_grad)
    output_sum = reduce(output_grad, orders[1])
    kv_sum = reduce_parts(kv_grad)
    query_sum = reduce(query_grad, orders[0])
    vec = jnp.concatenate([media_vec, latent_vec, ffn_vec], axis=0)
    vec = vec.reshape(6, 2 * count, width // (2 * count)).transpose(1, 0, 2)
    vec_sum = reduce(vec, orders[2], F32)[0]
    return (
        new_latents.reshape(latents.shape),
        patches_grad.reshape(patches.shape),
        latents_grad.reshape(latents.shape),
        query_sum,
        kv_sum[:, :INNER],
        kv_sum[:, INNER:],
        output_sum,
        up_sum,
        down_sum,
        vec_sum[0],
        vec_sum[1],
        vec_sum[2],
        vec_sum[3],
        vec_sum[4],
        vec_sum[5],
    )


def fits(mesh):
    return mesh.shape["img"] == 16 and mesh.shape["lat"] == 2


def quick(
    count,
    patches,
    latents,
    cotangent,
    doc_images,
    doc_device,
    query_weight,
    key_weight,
    value_weight,
    output_weight,
    up_weight,
    down_weight,
    media_gain,
    media_bias,
    latent_gain,
    latent_bias,
    ffn_gain,
    ffn_bias,
):
    slots, own_patches, width = patches.shape
    own_latents = latents.shape[1]
    hidden = up_weight.shape[1]
    np_, nl = slots * own_patches, slots * own_latents
    patch = patches.reshape(np_, width)
    latent = latents.reshape(nl, width)
    cot = cotangent.reshape(nl, width)
    mg, mb = media_gain.reshape(1, width), media_bias.reshape(1, width)
    lg, lb = latent_gain.reshape(1, width), latent_bias.reshape(1, width)
    fg, fb = ffn_gain.reshape(1, width), ffn_bias.reshape(1, width)
    sspec = pl.BlockSpec(memory_space=pltpu.SMEM)
    vmem = pl.BlockSpec(memory_space=pltpu.VMEM)
    hbm = pl.BlockSpec(memory_space=pl.ANY)
    names, scratch = main_scratch(nl, np_, width, hidden)
    given = (
        latent, query_weight, cot, output_weight, patch, key_weight, value_weight, up_weight,
        down_weight, doc_images, doc_device, fg, fb, mg, mb, lg, lb,
    )
    fin, vec, patches_low, latents_low, new_latents = pl.pallas_call(
        partial(main_body, names),
        in_specs=[hbm] * 9 + [sspec] * 2 + [vmem] * 6,
        out_specs=[vmem, vmem, hbm, hbm, hbm],
        out_shape=[
            struct((10,) + BLOCK, F32),
            struct((8, width), F32),
            struct((np_, width), BF),
            struct((nl, width), BF),
            struct((nl, width), BF),
        ],
        scratch_shapes=scratch,
        compiler_params=pltpu.CompilerParams(
            collective_id=0, has_side_effects=True, vmem_limit_bytes=60 * 1024 * 1024
        ),
    )(*given)
    d = 2 * count
    small = [
        (width // d, hidden),
        (hidden // d, width),
        (width // d, INNER),
        (width // d, INNER),
        (INNER // d, width),
        (width // d, INNER),
    ] + [(1, width // d)] * 6
    parts = 8
    patches_grad, fresh, latents_out, up_sum, down_sum, key_sum, value_sum, out_sum, query_sum, *thin = pl.pallas_call(
        last_body,
        in_specs=[hbm] * 4 + [vmem],
        out_specs=[hbm] * 9 + [vmem] * 6,
        out_shape=[struct((np_, width), F32), struct((nl, width), BF), struct((nl, width), F32)]
        + [struct(shape, F32) for shape in small],
        scratch_shapes=[
            pltpu.VMEM((parts, np_ // parts, width), BF),
            pltpu.VMEM((parts, np_ // parts, width), F32),
            pltpu.VMEM((nl, width), BF),
            pltpu.VMEM((nl, width), F32),
            pltpu.VMEM((nl, width), BF),
            pltpu.VMEM((10,) + BLOCK, F32),
            pltpu.SemaphoreType.DMA((2 * parts + 18,)),
        ],
        compiler_params=pltpu.CompilerParams(vmem_limit_bytes=VMEM_LIMIT),
    )(patches_low, latents_low, new_latents, fin, vec)
    return (
        fresh.reshape(latents.shape),
        patches_grad.reshape(patches.shape),
        latents_out.reshape(latents.shape),
        query_sum,
        key_sum,
        value_sum,
        out_sum,
        up_sum,
        down_sum,
    ) + tuple(v.reshape(-1) for v in thin)


def solution(mesh):
    split = P("img", "lat", None)
    both = P(("img", "lat"), None)
    line = P(("img", "lat"))
    return jax.shard_map(
        partial(quick if fits(mesh) else local, mesh.shape["img"]),
        mesh=mesh,
        in_specs=(split,) * 3 + (P(),) * 14,
        out_specs=(split,) * 3 + (both,) * 6 + (line,) * 6,
        check_vma=False,
    )
```
